512 devices in a mesh: tm: 8 (over x, core), tile: 64 (over y, z).
Axes of the slice: x: 4, y: 8, z: 8, core: 2. Of those that a mesh axis runs over, the one named last changes fastest.
Arguments:
- features: bfloat16 [2, 32, 128, 16, 512], P(None, 'tm', 'tile')
- lengths: int32 [2], replicated, may hold values from 1 to 32, as said below
- gain_in: float32 [512], replicated, may hold values from 0.5 to 1.5
- bias_in: float32 [512], replicated, may hold values from -3 to 3
- conv_in: bfloat16 [512, 27, 256], P('tile'), may hold values from -0.0546875 to 0.0546875
- skip_weight: bfloat16 [512, 256], P('tile'), may hold values from -0.25 to 0.25
Outputs:
- decoded: bfloat16 [2, 32, 128, 16, 256], P(None, 'tm', 'tile')
The draws below stay inside these ranges and needn't reach their ends.
Inputs may be any that keep to these rules, and one draw needn't show every extreme that they name: `lengths`: every video has one or more valid frames, the first ones of its buffer; in every draw one video fills all 32 frames.
All inputs are finite; a program needn't handle non-finite values.
Results may differ from the reference program's by a relative error of at most 0.0021.
Values may be sent and summed in bfloat16 or wider, within the bound.
No kernel may reach another device: no remote copies, remote signals or barrier semaphores. Data moves between devices by JAX's collectives and lax.ppermute only.
A program may use at most 64 MiB of HBM per device.

```python
import math
import jax
import jax.numpy as jnp
from jax import lax

C1 = 512
C2 = 256
GROUPS = 32
NV = 2
TF = 4
COLS = 16
NT = 32
H = 128
N_TM = 8


def draw_features(key, part):
    key = jax.random.fold_in(key, 3)
    base_key, spot_key, chan_key = jax.random.split(key, 3)
    shape = (NV, NT, H, COLS, C1)
    spots = jnp.exp(jax.random.uniform(spot_key, (NV, NT, H, 1, 1), jnp.float32, 0.0, math.log(10.0)))
    frame_ramp = 1.0 + 2.0 * jnp.arange(NT, dtype=jnp.float32) / max(NT - 1, 1)
    row_ramp = 1.0 + 2.0 * jnp.arange(H, dtype=jnp.float32) / max(H - 1, 1)
    ramps = frame_ramp[None, :, None, None, None] * row_ramp[None, None, :, None, None]
    channel = jnp.exp(jax.random.uniform(chan_key, (C1,), jnp.float32, -math.log(2.0), math.log(2.0)))
    base = jax.random.normal(base_key, shape, jnp.float32)
    return (0.12 * base * spots * ramps * channel).astype(jnp.bfloat16)


def draw_lengths(key, part):
    key = jax.random.fold_in(key, 5)
    first_key, second_key = jax.random.split(key)
    drawn = jax.random.randint(first_key, (NV,), 1, NT + 1)
    longest = jax.random.randint(second_key, (), 0, NV)
    return jnp.where(jnp.arange(NV) == longest, NT, drawn).astype(jnp.int32)


def shard_levels(stream_key, dims, cuts, smallest, largest):
    loudness, own = 1.0, jax.random.fold_in(stream_key, 6)
    for axis_at, parts in cuts:
        steps = jnp.exp(jax.random.uniform(jax.random.fold_in(own, axis_at), (parts,), jnp.float32, smallest / len(cuts), largest / len(cuts)))
        loudness = loudness * jnp.repeat(steps, dims[axis_at] // parts).reshape([-1 if axis == axis_at else 1 for axis in range(len(dims))])
    return loudness


def scatter_about(stream_key, dims, deviation, limit, shards=(), kind=jnp.bfloat16):
    values = jax.random.normal(stream_key, dims, jnp.float32) * deviation
    if len(shards) > 0:
        values = shard_levels(stream_key, dims, shards, -0.22, 0.18) * values
    return jnp.clip(values, min=-limit, max=limit).astype(kind)


def setup_inputs(seed: int = 0) -> dict:
    key_list = jax.random.split(jax.random.key(seed), 7)
    return {
        "features": draw_features(jax.random.fold_in(key_list[6], 71), 0),
        "lengths": draw_lengths(jax.random.fold_in(key_list[6], 71), 0),
        "gain_in": jnp.clip(1.0 + 0.1 * jax.random.normal(key_list[2], (C1,), jnp.float32), 0.5, 1.5),
        "bias_in": scatter_about(key_list[3], (C1,), 0.5, 3.0, (), jnp.float32),
        "conv_in": scatter_about(key_list[4], (C1, 27, C2), (27 * C1) ** -0.5, 0.0546875, ((0, 64),)),
        "skip_weight": scatter_about(key_list[5], (C1, C2), C1 ** -0.5, 0.25, ((0, 64),)),
    }


EPS = 1e-06

def causal_norm(signal, present, lengths, norm_gain, norm_bias):
    videos, frames_all, rows_all, col_count, channels = signal.shape
    per_group = channels // GROUPS
    grouped = signal.reshape(videos, frames_all, rows_all * col_count, GROUPS, per_group)
    masked = grouped * present[:, :, None, None, None]
    linear = lax.optimization_barrier(jnp.sum(masked, axis=(2, 4))).reshape(videos, N_TM, TF, GROUPS).sum(axis=2)
    square = lax.optimization_barrier(jnp.sum(masked * masked, axis=(2, 4))).reshape(videos, N_TM, TF, GROUPS).sum(axis=2)
    linear = jnp.cumsum(linear, axis=1)
    square = jnp.cumsum(square, axis=1)
    span_ends = (jnp.arange(N_TM, dtype=jnp.int32) + 1) * TF
    frames_seen = jnp.minimum(lengths[:, None], span_ends[None, :]).astype(jnp.float32)
    cell_count = frames_seen * float(rows_all * col_count * per_group)
    centre = linear / cell_count[:, :, None]
    inverse = lax.rsqrt(square / cell_count[:, :, None] - centre * centre + EPS)
    centre = jnp.repeat(centre, TF, axis=1)
    inverse = jnp.repeat(inverse, TF, axis=1)
    normed = (grouped - centre[:, :, None, :, None]) * inverse[:, :, None, :, None]
    normed = normed.reshape(signal.shape) * norm_gain + norm_bias
    return (jax.nn.silu(normed) * present[:, :, None, None, None]).astype(jnp.bfloat16)

def causal_conv(active, weight):
    padded = jnp.pad(active.astype(jnp.float32), ((0, 0), (2, 0), (1, 1), (1, 1), (0, 0)), mode='edge')
    kernel = weight.astype(jnp.float32).reshape(weight.shape[0], 3, 3, 3, weight.shape[2]).transpose(1, 2, 3, 0, 4)
    return lax.conv_general_dilated(padded, kernel, (1, 1, 1), 'VALID', dimension_numbers=('NDHWC', 'DHWIO', 'NDHWC'), precision=lax.Precision.HIGHEST)

def reference(features, lengths, gain_in, bias_in, conv_in, skip_weight):
    stamps = jnp.arange(NT, dtype=jnp.int32)
    present = (stamps[None, :] < lengths[:, None]).astype(jnp.float32)
    signal = features.astype(jnp.float32)
    active = causal_norm(signal, present, lengths, gain_in, bias_in)
    output = causal_conv(active, conv_in)
    skipped = jnp.dot(features.reshape(-1, C1), skip_weight, preferred_element_type=jnp.float32).reshape(output.shape)
    return ((output + skipped) * present[:, :, None, None, None]).astype(jnp.bfloat16)
```

```python
import jax
import jax.numpy as jnp
from jax import lax
from jax.sharding import Mesh
from jax.sharding import PartitionSpec as P

GROUPS = 32
EPS = 1e-06
TM = ("xh", "xl", "core")
TILE = ("y", "z")
TEAM = ("xl", "core")
TEAM_SIZE = 4


def three_parts(value):
    high = lax.reduce_precision(value, 8, 7)
    rest = value - high
    middle = lax.reduce_precision(rest, 8, 7)
    low = rest - middle
    return jnp.stack([high, middle, low]).astype(jnp.bfloat16)


def to_all(block, axis):
    count = lax.axis_size(axis)
    copies = jnp.broadcast_to(block[None], (count,) + block.shape)
    return lax.all_to_all(copies, axis, 0, 0, tiled=True)


def local_sums(features, present):
    videos, frames, row_count, col_count, channels = features.shape
    masked = features.astype(jnp.float32) * present[:, :, None, None, None]
    linear = jnp.sum(masked, axis=(1, 2, 3)).reshape(videos, GROUPS, channels // GROUPS)
    square = jnp.sum(masked * masked, axis=(1, 2, 3)).reshape(videos, GROUPS, channels // GROUPS)
    return jnp.stack([jnp.sum(linear, axis=2), jnp.sum(square, axis=2)])


def with_rows(features):
    place, count = lax.axis_index(TILE), lax.axis_size(TILE)
    forward = [(i, i + 1) for i in range(count - 1)]
    backward = [(i + 1, i) for i in range(count - 1)]
    first, last = features[:, :, :1], features[:, :, -1:]
    low = lax.ppermute(last, TILE, forward)
    high = lax.ppermute(first, TILE, backward)
    low = jnp.where(place == 0, first, low)
    high = jnp.where(place == count - 1, last, high)
    return jnp.concatenate([low, features, high], axis=2)


def by_member(block):
    channels = block.shape[-1]
    share = channels // TEAM_SIZE
    column = jnp.arange(channels, dtype=jnp.int32)
    member, rest = column // share, column % share
    source = (rest // 2) * 8 + member * 2 + rest % 2
    chosen = (jnp.arange(channels, dtype=jnp.int32)[:, None] == source[None, :]).astype(jnp.bfloat16)
    flat = jnp.dot(block.reshape(-1, channels), chosen, preferred_element_type=jnp.float32)
    flat = flat.astype(jnp.bfloat16).reshape(-1, TEAM_SIZE, share).transpose(1, 0, 2)
    return flat.reshape((TEAM_SIZE,) + block.shape[:-1] + (share,))


def spans_of_team(shares):
    me = lax.axis_index(TEAM)
    arrived = [lax.dynamic_index_in_dim(shares, me, 0, False)]
    for step in range(1, TEAM_SIZE):
        pairs = [(i, i ^ step) for i in range(TEAM_SIZE)]
        outgoing = lax.dynamic_index_in_dim(shares, me ^ step, 0, False)
        arrived.append(lax.ppermute(outgoing, TEAM, pairs))
    arrived = jnp.stack(arrived)
    return [lax.dynamic_index_in_dim(arrived, me ^ span, 0, False) for span in range(TEAM_SIZE)]


def per_device(features, lengths, gain_in, bias_in, conv_in, skip_weight):
    videos, frames, row_count, col_count, wide_in = features.shape
    wide_out = conv_in.shape[2]
    share = wide_in // TEAM_SIZE
    taps = conv_in.shape[1]
    me = lax.axis_index(TEAM)
    team_first = lax.axis_index("xh") * TEAM_SIZE
    span = team_first + me

    stamps = span * frames + jnp.arange(frames, dtype=jnp.int32)
    present = (stamps[None, :] < lengths[:, None]).astype(jnp.float32)
    sums = local_sums(features, present)

    weights = jnp.concatenate([conv_in, skip_weight[:, None, :]], axis=1)
    mine = conv_in.shape[0] // TEAM_SIZE
    weights = lax.dynamic_slice_in_dim(weights, me * mine, mine, axis=0)
    weights = weights.transpose(1, 0, 2).reshape((taps + 1) * mine, wide_out)
    parts = three_parts(sums.reshape(-1)).reshape(-1)
    parts = jnp.pad(parts, (0, 8 * wide_out - parts.shape[0])).reshape(8, wide_out)
    around_z = to_all(jnp.concatenate([weights, parts], axis=0), "z")
    rows = (taps + 1) * mine
    z_count = lax.axis_size("z")
    weights = around_z[:, :rows].reshape(z_count, taps + 1, mine, wide_out).transpose(1, 0, 2, 3)
    weights = lax.all_gather(
        weights.reshape(taps + 1, z_count * mine, wide_out), "y", axis=1, tiled=True
    )
    parts = around_z[:, rows:].astype(jnp.float32).reshape(z_count, -1)[:, : 3 * sums.size]
    sums = jnp.sum(parts.reshape(z_count, 3, sums.size), axis=(0, 1)).reshape(1, -1)
    sums = jnp.sum(to_all(sums, "y"), axis=0)
    sums = to_all(sums, TM).reshape(-1, 2, videos, GROUPS)
    sums = jnp.cumsum(sums, axis=0)

    spans = spans_of_team(by_member(with_rows(features)))
    cached = lax.ppermute(spans[-1][:, frames - 2 :], "xh", [(0, 1)])
    first = jnp.broadcast_to(spans[0][:, :1], cached.shape)
    cached = jnp.where(team_first == 0, first, cached)
    signal = jnp.concatenate([cached] + spans, axis=1)

    span_count = sums.shape[0]
    ends = (jnp.arange(span_count, dtype=jnp.int32) + 1) * frames
    seen = jnp.minimum(lengths[None, :], ends[:, None]).astype(jnp.float32)
    cells = seen * float(row_count * lax.axis_size(TILE) * col_count * (wide_in // GROUPS))
    centre = sums[:, 0] / cells[:, :, None]
    inverse = lax.rsqrt(sums[:, 1] / cells[:, :, None] - centre * centre + EPS)
    gain = lax.dynamic_index_in_dim(gain_in.reshape(-1, TEAM_SIZE, mine), me, 1, False).reshape(-1)
    bias = lax.dynamic_index_in_dim(bias_in.reshape(-1, TEAM_SIZE, mine), me, 1, False).reshape(-1)
    centre = jnp.repeat(centre, share // GROUPS, axis=2)
    scale = jnp.repeat(inverse, share // GROUPS, axis=2) * gain
    stamps = team_first * frames - 2 + jnp.arange(signal.shape[1], dtype=jnp.int32)
    stamps = jnp.maximum(stamps, 0)
    centre = jnp.take(centre, stamps // frames, axis=0).transpose(1, 0, 2)
    scale = jnp.take(scale, stamps // frames, axis=0).transpose(1, 0, 2)
    shown = (stamps[None, :] < lengths[:, None]).astype(jnp.float32)
    normed = (signal.astype(jnp.float32) - centre[:, :, None, None, :]) * scale[:, :, None, None, :] + bias
    active = (jax.nn.silu(normed) * shown[:, :, None, None, None]).astype(jnp.bfloat16)
    active = jnp.pad(active, ((0, 0), (0, 0), (0, 0), (1, 1), (0, 0)), mode="edge")

    length = TEAM_SIZE * frames
    windows = []
    for a in range(3):
        for b in range(3):
            for e in range(3):
                windows.append(active[:, a : a + length, b : b + row_count, e : e + col_count])
    windows.append(signal[:, 2:, 1 : 1 + row_count])
    patches = jnp.concatenate(windows, axis=4).reshape(-1, (taps + 1) * share)
    total = jnp.dot(patches, weights.reshape(-1, wide_out), preferred_element_type=jnp.float32)
    total = total.reshape(videos, 2, 2, frames, row_count, col_count, wide_out)

    core, xl = lax.axis_index("core"), lax.axis_index("xl")
    swap = [(0, 1), (1, 0)]
    other = lax.ppermute(lax.dynamic_index_in_dim(total, 1 - core, 2, False), "core", swap)
    total = lax.dynamic_index_in_dim(total, core, 2, False) + other
    other = lax.ppermute(lax.dynamic_index_in_dim(total, 1 - xl, 1, False), "xl", swap)
    total = lax.dynamic_index_in_dim(total, xl, 1, False) + other
    return (total * present[:, :, None, None, None]).astype(jnp.bfloat16)


def solution(mesh):
    spans, tiles = mesh.devices.shape
    fine = Mesh(
        mesh.devices.reshape(spans // TEAM_SIZE, 2, 2, 8, tiles // 8), TM + TILE
    )
    placed = (
        P(None, TM, TILE, None, None),
        P(),
        P(),
        P(),
        P(TILE, None, None),
        P(TILE, None),
    )
    return jax.shard_map(
        per_device,
        mesh=fine,
        in_specs=placed,
        out_specs=P(None, TM, TILE, None, None),
        check_vma=False,
    )
```

```python
import functools

import jax
import jax.numpy as jnp
from jax import lax
from jax.experimental import pallas as pl
from jax.experimental.pallas import tpu as pltpu
from jax.sharding import Mesh
from jax.sharding import PartitionSpec as P

GROUPS = 32
EPS = 1e-06
TM = ("x", "core")
TILE = ("y", "z")
SPANS = 8
VIDEOS = 2
FRAMES = 4
COLS = 16
SHARE = 64
ROWS = 4
WIDE = ROWS * SHARE
OUT = 256


def three_parts(value):
    high = lax.reduce_precision(value, 8, 7)
    rest = value - high
    middle = lax.reduce_precision(rest, 8, 7)
    low = rest - middle
    return jnp.stack([high, middle, low]).astype(jnp.bfloat16)


def to_all(block, axis):
    count = lax.axis_size(axis)
    copies = jnp.broadcast_to(block[None], (count,) + block.shape)
    return lax.all_to_all(copies, axis, 0, 0, tiled=True)


def local_sums(features, present):
    videos, channels = features.shape[0], features.shape[-1]
    masked = features.astype(jnp.float32) * present[:, :, None, None, None]
    linear = jnp.sum(masked, axis=(1, 2, 3)).reshape(videos, GROUPS, channels // GROUPS)
    square = jnp.sum(masked * masked, axis=(1, 2, 3)).reshape(videos, GROUPS, channels // GROUPS)
    return jnp.stack([jnp.sum(linear, axis=2), jnp.sum(square, axis=2)])


def with_rows(features):
    place, count = lax.axis_index(TILE), lax.axis_size(TILE)
    forward = [(i, i + 1) for i in range(count - 1)]
    backward = [(i + 1, i) for i in range(count - 1)]
    first, last = features[:, :, 0], features[:, :, 1]
    low = lax.ppermute(last, TILE, forward)
    high = lax.ppermute(first, TILE, backward)
    low = jnp.where(place == 0, first, low)
    high = jnp.where(place == count - 1, last, high)
    return low, first, last, high


def by_member(low, first, last, high):
    channels = low.shape[-1]
    pairs = jnp.stack(
        [jnp.concatenate([low, first], axis=-1), jnp.concatenate([last, high], axis=-1)]
    )
    pairs = pairs.reshape(-1, 2 * channels)
    column = jnp.arange(2 * channels, dtype=jnp.int32)
    member, row, tile = column // (2 * SHARE), column // SHARE % 2, column % SHARE
    source = row * channels + tile * SPANS + member
    chosen = (column[:, None] == source[None, :]).astype(jnp.bfloat16)
    flat = jnp.dot(pairs, chosen, preferred_element_type=jnp.float32).astype(jnp.bfloat16)
    flat = flat.reshape(2, -1, SPANS, 2 * SHARE).transpose(2, 1, 0, 3)
    return flat.reshape(SPANS, -1, WIDE)


def conv_kernel(
    lengths, core, totals, gain, bias, signal, weights, send, keep, shifted, *, cells
):
    summed = [totals[0:1, :]]
    for span in range(1, SPANS):
        summed.append(summed[-1] + totals[span : span + 1, :])
    summed = jnp.concatenate(summed, axis=0)
    entry = lax.broadcasted_iota(jnp.int32, (128, WIDE), 0)
    group = lax.broadcasted_iota(jnp.int32, (128, WIDE), 1) % SHARE // 2
    ends = (lax.broadcasted_iota(jnp.int32, (SPANS, WIDE), 0) + 1) * FRAMES

    def spread(which):
        chosen = (entry == group + which * GROUPS).astype(jnp.float32)
        return jnp.dot(
            summed, chosen, precision=lax.Precision.HIGHEST, preferred_element_type=jnp.float32
        )

    offset = bias[...].reshape(1, 1, WIDE)
    for video in range(VIDEOS):
        seen = jnp.minimum(ends, lengths[video]).astype(jnp.float32) * cells
        centre = spread(video) / seen
        scale = lax.rsqrt(spread(VIDEOS + video) / seen - centre * centre + EPS) * gain[...]
        for span in range(SPANS):
            block = signal[span, video * FRAMES : (video + 1) * FRAMES].astype(jnp.float32)
            block = (block - centre[span : span + 1].reshape(1, 1, WIDE)) * scale[
                span : span + 1
            ].reshape(1, 1, WIDE) + offset
            block = block / (1.0 + jnp.exp(-block))
            frame = lax.broadcasted_iota(jnp.int32, block.shape, 0) + span * FRAMES
            block = jnp.where(frame < lengths[video], block, 0.0)
            left = jnp.concatenate([block[:, :1], block[:, :-1]], axis=1).astype(jnp.bfloat16)
            right = jnp.concatenate([block[:, 1:], block[:, -1:]], axis=1).astype(jnp.bfloat16)
            place = slice(2 + span * FRAMES, 2 + (span + 1) * FRAMES)
            for side, value in enumerate((left, block.astype(jnp.bfloat16), right)):
                shifted[side, video, place] = value
                if span == 0:
                    shifted[side, video, 0] = value[0]
                    shifted[side, video, 1] = value[0]

    pieces = SPANS // 2
    for target, parity in ((send, 1 - core[0]), (keep, core[0])):
        for half in range(2):
            rows = slice(SHARE, SHARE + WIDE) if half == 0 else slice(0, WIDE)
            total = None
            for tap in range(10):
                blocks = []
                for piece in range(pieces):
                    span = 2 * piece + parity
                    for video in range(VIDEOS):
                        if tap < 9:
                            blocks.append(
                                shifted[tap % 3, video, pl.ds(span * FRAMES + tap // 3, FRAMES)]
                            )
                        else:
                            blocks.append(signal[span, video * FRAMES : (video + 1) * FRAMES])
                left = jnp.concatenate(blocks, axis=0).reshape(-1, WIDE)
                term = jnp.dot(left, weights[tap, rows, :], preferred_element_type=jnp.float32)
                total = term if total is None else total + term
            target[:, :, half * OUT : (half + 1) * OUT] = total.reshape(pieces, -1, OUT)


def per_device(features, lengths, gain_in, bias_in, conv_in, skip_weight):
    videos, frames, row_count, col_count, wide_in = features.shape
    span, core = lax.axis_index(TM), lax.axis_index("core")
    tiles = lax.axis_size(TILE)
    taps = conv_in.shape[1]

    stamps = span * frames + jnp.arange(frames, dtype=jnp.int32)
    present = (stamps[None, :] < lengths[:, None]).astype(jnp.float32)
    sums = local_sums(features, present)

    weights = jnp.concatenate([conv_in, skip_weight[:, None, :]], axis=1)
    weights = lax.dynamic_index_in_dim(weights, span, 0, False)
    parts = three_parts(sums.reshape(-1)).reshape(-1)
    parts = jnp.pad(parts, (0, 4 * OUT - parts.shape[0])).reshape(4, OUT)
    arrived = to_all(jnp.concatenate([weights, parts], axis=0), TILE)

    signal = lax.all_to_all(by_member(*with_rows(features)), TM, 0, 0, tiled=True)
    signal = signal.reshape(SPANS, videos * frames, col_count, WIDE)

    parts = arrived[:, taps + 1 :].astype(jnp.float32).reshape(tiles, -1)[:, : 3 * sums.size]
    sums = jnp.sum(parts.reshape(tiles, 3, sums.size), axis=(0, 1)).reshape(1, -1)
    totals = to_all(sums, TM).reshape(SPANS, -1)

    conv = arrived[:, :taps].reshape(tiles, 3, 3, 3, OUT).transpose(1, 3, 2, 0, 4)
    conv = jnp.pad(conv.reshape(9, 3 * SHARE, OUT), ((0, 0), (SHARE, SHARE), (0, 0)))
    skip = jnp.pad(arrived[:, taps][None], ((0, 0), (2 * SHARE, 2 * SHARE), (0, 0)))
    weights = jnp.concatenate([conv, skip], axis=0)

    def lanes(vector):
        own = lax.dynamic_index_in_dim(vector.reshape(SHARE, SPANS), span, 1, False)
        return jnp.tile(own, ROWS).reshape(1, WIDE)

    cells = float(row_count * tiles * col_count * (wide_in // GROUPS))
    shape = jax.ShapeDtypeStruct((SPANS // 2, videos * frames * col_count, 2 * OUT), jnp.float32)
    on_chip = pl.BlockSpec(memory_space=pltpu.VMEM)
    scalar = pl.BlockSpec(memory_space=pltpu.SMEM)
    send, keep = pl.pallas_call(
        functools.partial(conv_kernel, cells=cells),
        out_shape=(shape, shape),
        in_specs=[scalar, scalar] + [on_chip] * 5,
        out_specs=(on_chip, on_chip),
        scratch_shapes=[
            pltpu.VMEM((3, videos, SPANS * frames + 2, col_count, WIDE), jnp.bfloat16)
        ],
        compiler_params=pltpu.CompilerParams(vmem_limit_bytes=40 * 1024 * 1024),
        cost_estimate=pl.CostEstimate(
            flops=2 * 10 * 1024 * 256 * 512, bytes_accessed=6 << 20, transcendentals=1 << 19
        ),
        name="norm_conv",
    )(lengths, core.reshape(1), totals, lanes(gain_in), lanes(bias_in), signal, weights)

    total = keep + lax.ppermute(send, "core", [(0, 1), (1, 0)])
    total = jnp.sum(lax.all_to_all(total, "x", 0, 0, tiled=True), axis=0)
    total = total.reshape(videos, frames, col_count, row_count, OUT).transpose(0, 1, 3, 2, 4)
    return (total * present[:, :, None, None, None]).astype(jnp.bfloat16)


def solution(mesh):
    spans, tiles = mesh.devices.shape
    fine = Mesh(mesh.devices.reshape(spans // 2, 2, 8, tiles // 8), TM + TILE)
    placed = (
        P(None, TM, TILE, None, None),
        P(),
        P(),
        P(),
        P(TILE, None, None),
        P(TILE, None),
    )
    return jax.shard_map(
        per_device,
        mesh=fine,
        in_specs=placed,
        out_specs=P(None, TM, TILE, None, None),
        check_vma=False,
    )
```

```python
import functools

import jax
import jax.numpy as jnp
from jax import lax
from jax.experimental import pallas as pl
from jax.experimental.pallas import tpu as pltpu
from jax.sharding import Mesh
from jax.sharding import PartitionSpec as P

GROUPS = 32
EPS = 1e-06
TM = ("x", "core")
TILE = ("y", "z")
SPANS = 8
VIDEOS = 2
FRAMES = 4
COLS = 16
SHARE = 64
ROWS = 4
WIDE = ROWS * SHARE
OUT = 256


def to_all(block, axis):
    count = lax.axis_size(axis)
    copies = jnp.broadcast_to(block[None], (count,) + block.shape)
    return lax.all_to_all(copies, axis, 0, 0, tiled=True)


def payload_kernel(features, conv, skip, lengths, copies, planes, taps, skips, valid, rows, done):
    moves = [
        pltpu.make_async_copy(source, target, done.at[index])
        for index, (source, target) in enumerate(
            ((features, planes), (conv, taps), (skip, skips), (lengths, valid))
        )
    ]
    for move in moves:
        move.start()
    for move in moves:
        move.wait()
    count, channels = taps.shape[0], planes.shape[-1]
    span = lax.axis_index(TM)
    pick = lax.broadcasted_iota(jnp.int32, (count, SPANS, OUT), 1) == span
    rows[...] = jnp.zeros_like(rows)
    rows[0:count, :] = jnp.sum(jnp.where(pick, taps[...].astype(jnp.float32), 0.0), axis=1)
    pick = lax.broadcasted_iota(jnp.int32, (SPANS, OUT), 0) == span
    rows[count : count + 1, :] = jnp.sum(
        jnp.where(pick, skips[...].astype(jnp.float32), 0.0), axis=0, keepdims=True
    )
    group = lax.broadcasted_iota(jnp.int32, (channels, 128), 0) // (channels // GROUPS)
    lane = lax.broadcasted_iota(jnp.int32, (channels, 128), 1)
    sums = jnp.zeros((1, 128), jnp.float32)
    for video in range(VIDEOS):
        linear = jnp.zeros((1, channels), jnp.float32)
        square = jnp.zeros((1, channels), jnp.float32)
        for frame in range(FRAMES):
            block = planes[video * FRAMES + frame].astype(jnp.float32)
            shown = (span * FRAMES + frame < valid[video]).astype(jnp.float32)
            linear += jnp.sum(block, axis=0, keepdims=True) * shown
            square += jnp.sum(block * block, axis=0, keepdims=True) * shown
        for which, value in ((video, linear), (VIDEOS + video, square)):
            chosen = (lane == group + which * GROUPS).astype(jnp.float32)
            sums += jnp.dot(
                value, chosen, precision=lax.Precision.HIGHEST, preferred_element_type=jnp.float32
            )
    high = sums.astype(jnp.bfloat16).astype(jnp.float32)
    middle = (sums - high).astype(jnp.bfloat16).astype(jnp.float32)
    rows[count + 1 : count + 2, 0:128] = high
    rows[count + 1 : count + 2, 128:256] = middle
    rows[count + 2 : count + 3, 0:128] = sums - high - middle
    value = rows[...].astype(jnp.bfloat16)
    for index in range(copies.shape[0]):
        copies[index] = value


def member_kernel(features, kept, sent):
    voxels, channels = features.shape[0] * COLS, features.shape[-1]
    column = lax.broadcasted_iota(jnp.int32, (channels, 2 * channels), 1)
    source = column % SHARE * SPANS + column // (2 * SHARE)
    match = lax.broadcasted_iota(jnp.int32, (channels, 2 * channels), 0) == source
    second = column // SHARE % 2 == 1
    left = jnp.where(match & ~second, 1.0, 0.0).astype(jnp.bfloat16)
    right = jnp.where(match & second, 1.0, 0.0).astype(jnp.bfloat16)
    first = features[:, :COLS].reshape(voxels, channels)
    last = features[:, COLS:].reshape(voxels, channels)
    flat = jnp.dot(first, left, preferred_element_type=jnp.float32)
    flat = flat + jnp.dot(last, right, preferred_element_type=jnp.float32)
    flat = flat.astype(jnp.bfloat16)
    even = lax.axis_index("core") == 0
    for chip in range(SPANS // 2):
        zero = flat[:, chip * 256 : chip * 256 + 128]
        one = flat[:, chip * 256 + 128 : chip * 256 + 256]
        kept[chip] = jnp.where(even, zero, one)
        sent[chip] = jnp.where(even, one, zero)


def conv_kernel(
    lengths, totals, gain, bias, own, above, below, weights,
    send, keep, factor, shifted, raw, moments, *, cells, tiles, tap_bound, skip_bound
):
    half = 2 * SHARE
    chips = SPANS // 2
    chip, core = lax.axis_index("x"), lax.axis_index("core")
    tile = lax.axis_index(TILE)
    summed = [totals[0:1, :]]
    for span in range(1, SPANS):
        summed.append(summed[-1] + totals[span : span + 1, :])
    summed = jnp.concatenate(summed, axis=0)
    entry = lax.broadcasted_iota(jnp.int32, (128, half), 0)
    group = lax.broadcasted_iota(jnp.int32, (128, half), 1) % SHARE // 2
    ends = (lax.broadcasted_iota(jnp.int32, (SPANS, half), 0) + 1) * FRAMES

    def spread(which):
        chosen = (entry == group + which * GROUPS).astype(jnp.float32)
        return jnp.dot(
            summed, chosen, precision=lax.Precision.HIGHEST, preferred_element_type=jnp.float32
        )

    ratio = jnp.zeros((SPANS, half), jnp.float32)
    largest = jnp.zeros((SPANS, half), jnp.float32)
    for video in range(VIDEOS):
        seen = jnp.minimum(ends, lengths[video]).astype(jnp.float32) * cells
        square = spread(VIDEOS + video)
        centre = spread(video) / seen
        inverse = lax.rsqrt(square / seen - centre * centre + EPS)
        moments[2 * video] = centre
        moments[2 * video + 1] = inverse * gain[...]
        size = jnp.sqrt(square)
        ratio = jnp.maximum(ratio, size * inverse)
        largest = jnp.maximum(largest, size)
    bound = tap_bound * (3.0 * jnp.max(ratio, keepdims=True) + 3.0)
    bound = bound + skip_bound * jnp.max(largest, keepdims=True)
    factor[...] = jnp.broadcast_to(jnp.exp2(14.0 - jnp.floor(jnp.log2(bound))), factor.shape)

    offset = bias[...].reshape(1, 1, half)
    lane = lax.broadcasted_iota(jnp.int32, (FRAMES, COLS, half), 2)
    for step in range(chips):
        for parity in range(2):
            span = lax.rem(chip - step + chips, chips) * 2 + parity
            start = span * FRAMES
            for video in range(VIDEOS):
                place = slice(video * FRAMES, (video + 1) * FRAMES)
                block = own[2 * step + parity, place]
                raw[video, pl.ds(start, FRAMES)] = block
                block = block.astype(jnp.float32)
                turned = pltpu.roll(block, SHARE, 2)
                upper = jnp.where(tile == 0, turned, above[2 * step + parity, place].astype(jnp.float32))
                lower = jnp.where(
                    tile == tiles - 1, turned, below[2 * step + parity, place].astype(jnp.float32)
                )
                edges = jnp.where(lane < SHARE, lower, upper)
                centre = moments[2 * video, pl.ds(span, 1)].reshape(1, 1, half)
                scale = moments[2 * video + 1, pl.ds(span, 1)].reshape(1, 1, half)
                shown = lax.broadcasted_iota(jnp.int32, block.shape, 0) + start < lengths[video]
                for at, value in enumerate((block, edges)):
                    value = (value - centre) * scale + offset
                    value = value / (1.0 + jnp.exp(-value))
                    value = jnp.where(shown, value, 0.0)
                    left = jnp.concatenate([value[:, :1], value[:, :-1]], axis=1)
                    right = jnp.concatenate([value[:, 1:], value[:, -1:]], axis=1)
                    lanes = slice(at * half, (at + 1) * half)
                    for side, part in enumerate((left, value, right)):
                        shifted[side, video, pl.ds(2 + start, FRAMES), :, lanes] = part.astype(jnp.bfloat16)
    for side in range(3):
        for video in range(VIDEOS):
            shifted[side, video, 0] = shifted[side, video, 2]
            shifted[side, video, 1] = shifted[side, video, 2]

    for target, parity in ((send, 1 - core), (keep, core)):
        for row in range(2):
            place = slice(0, WIDE) if row == 1 else slice(SHARE, SHARE + WIDE)
            total = None
            for tap in range(10):
                blocks = []
                for piece in range(chips):
                    start = (2 * piece + parity) * FRAMES
                    for video in range(VIDEOS):
                        if tap < 9:
                            blocks.append(shifted[tap % 3, video, pl.ds(start + tap // 3, FRAMES)])
                        else:
                            blocks.append(raw[video, pl.ds(start, FRAMES)])
                left = jnp.concatenate(blocks, axis=0)
                if tap < 9:
                    term = jnp.dot(
                        left.reshape(-1, WIDE), weights[tap, place, :], preferred_element_type=jnp.float32
                    )
                else:
                    place = slice(place.start, place.start + half)
                    term = jnp.dot(
                        left.reshape(-1, half), weights[tap, place, :], preferred_element_type=jnp.float32
                    )
                total = term if total is None else total + term
            target[:, :, row * COLS : (row + 1) * COLS, :] = total.reshape(chips, -1, COLS, OUT)


def per_device(features, lengths, gain_in, bias_in, conv_in, skip_weight):
    videos, frames, row_count, col_count, wide_in = features.shape
    span, core, chip = lax.axis_index(TM), lax.axis_index("core"), lax.axis_index("x")
    tiles, chips = lax.axis_size(TILE), lax.axis_size("x")
    taps = conv_in.shape[1]
    on_chip = pl.BlockSpec(memory_space=pltpu.VMEM)
    anywhere = pl.BlockSpec(memory_space=pl.ANY)
    scalar = pl.BlockSpec(memory_space=pltpu.SMEM)
    params = pltpu.CompilerParams(vmem_limit_bytes=40 * 1024 * 1024)
    voxels = videos * frames * col_count

    planes = features.reshape(videos * frames, row_count * col_count, wide_in)
    copies = pl.pallas_call(
        payload_kernel,
        out_shape=jax.ShapeDtypeStruct((tiles, 32, OUT), jnp.bfloat16),
        in_specs=[anywhere] * 4,
        out_specs=on_chip,
        scratch_shapes=[
            pltpu.VMEM(planes.shape, jnp.bfloat16),
            pltpu.VMEM((taps, SPANS, OUT), jnp.bfloat16),
            pltpu.VMEM((SPANS, OUT), jnp.bfloat16),
            pltpu.SMEM((videos,), jnp.int32),
            pltpu.VMEM((32, OUT), jnp.float32),
            pltpu.SemaphoreType.DMA((4,)),
        ],
        compiler_params=params,
        name="payload",
    )(planes, conv_in.transpose(1, 0, 2), skip_weight, lengths)
    arrived = lax.all_to_all(copies, TILE, 0, 0, tiled=True)

    share = jax.ShapeDtypeStruct((chips, voxels, 2 * SHARE), jnp.bfloat16)
    kept, sent = pl.pallas_call(
        member_kernel,
        out_shape=(share, share),
        in_specs=[on_chip],
        out_specs=(on_chip, on_chip),
        compiler_params=params,
        name="member_shares",
    )(planes)
    other = lax.ppermute(sent, "core", [(0, 1), (1, 0)])
    both = jnp.stack([jnp.where(core == 0, kept, other), jnp.where(core == 0, other, kept)], axis=1)
    signal = []
    for step in range(chips):
        block = lax.dynamic_index_in_dim(both, lax.rem(chip + step, chips), 0, False)
        if step:
            block = lax.ppermute(block, "x", [(i, (i + step) % chips) for i in range(chips)])
        signal.append(block)
    signal = jnp.concatenate(signal, axis=0).reshape(SPANS, videos * frames, col_count, 2 * SHARE)
    above = lax.ppermute(signal, TILE, [(i, i + 1) for i in range(tiles - 1)])
    below = lax.ppermute(signal, TILE, [(i + 1, i) for i in range(tiles - 1)])

    parts = jnp.sum(arrived[:, taps + 1 : taps + 3].astype(jnp.float32), axis=0)
    sums = parts[:1, :128] + parts[:1, 128:] + parts[1:, :128]
    totals = to_all(sums, TM).reshape(SPANS, -1)

    conv = arrived[:, :taps].reshape(tiles, 3, 3, 3, OUT).transpose(1, 3, 2, 0, 4)
    conv = conv.reshape(9, 3 * SHARE, OUT)
    conv = jnp.concatenate([jnp.pad(conv, ((0, 0), (0, SHARE), (0, 0))), conv[:, :SHARE]], axis=1)
    skip = jnp.pad(arrived[:, taps][None], ((0, 0), (SHARE, 3 * SHARE), (0, 0)))
    weights = jnp.concatenate([conv, skip], axis=0)

    def lanes(vector):
        own = lax.dynamic_index_in_dim(vector.reshape(SHARE, SPANS), span, 1, False)
        return jnp.tile(own, 2).reshape(1, 2 * SHARE)

    shape = jax.ShapeDtypeStruct((chips, videos * frames, row_count * col_count, OUT), jnp.float32)
    send, keep, factor = pl.pallas_call(
        functools.partial(
            conv_kernel,
            cells=float(row_count * tiles * col_count * (wide_in // GROUPS)),
            tiles=tiles,
            tap_bound=float(taps * SHARE) * 0.0546875,
            skip_bound=float(SHARE) * 0.25,
        ),
        out_shape=(shape, shape, jax.ShapeDtypeStruct((1, OUT), jnp.float32)),
        in_specs=[scalar] + [on_chip] * 7,
        out_specs=(on_chip, on_chip, on_chip),
        scratch_shapes=[
            pltpu.VMEM((3, videos, SPANS * frames + 2, col_count, WIDE), jnp.bfloat16),
            pltpu.VMEM((videos, SPANS * frames, col_count, 2 * SHARE), jnp.bfloat16),
            pltpu.VMEM((2 * videos, SPANS, 2 * SHARE), jnp.float32),
        ],
        compiler_params=params,
        cost_estimate=pl.CostEstimate(
            flops=2 * 10 * 1024 * 256 * 512, bytes_accessed=6 << 20, transcendentals=1 << 19
        ),
        name="norm_conv",
    )(lengths, totals, lanes(gain_in), lanes(bias_in), signal, above, below, weights)

    total = keep + lax.ppermute(send, "core", [(0, 1), (1, 0)])
    total = (total * factor).astype(jnp.float16)
    total = lax.all_to_all(total, "x", 0, 0, tiled=True)
    total = jnp.sum(total.astype(jnp.float32), axis=0) / factor
    total = total.reshape(videos, frames, row_count, col_count, OUT)
    stamps = span * frames + jnp.arange(frames, dtype=jnp.int32)
    present = stamps[None, :] < lengths[:, None]
    return jnp.where(present[:, :, None, None, None], total, 0.0).astype(jnp.bfloat16)


def solution(mesh):
    spans, tiles = mesh.devices.shape
    fine = Mesh(mesh.devices.reshape(spans // 2, 2, 8, tiles // 8), TM + TILE)
    placed = (
        P(None, TM, TILE, None, None),
        P(),
        P(),
        P(),
        P(TILE, None, None),
        P(TILE, None),
    )
    return jax.shard_map(
        per_device,
        mesh=fine,
        in_specs=placed,
        out_specs=P(None, TM, TILE, None, None),
        check_vma=False,
    )
```

```python
import functools

import jax
import jax.numpy as jnp
from jax import lax
from jax.experimental import pallas as pl
from jax.experimental.pallas import tpu as pltpu
from jax.sharding import Mesh
from jax.sharding import PartitionSpec as P

GROUPS = 32
EPS = 1e-06
TM = ("x", "core")
TILE = ("y", "z")
SPANS = 8
VIDEOS = 2
FRAMES = 4
COLS = 16
SHARE = 64
CHIPS = 4
PART = 2 * SHARE
ROWS = 4
OUT = 256


def to_all(block, axis):
    count = lax.axis_size(axis)
    copies = jnp.broadcast_to(block[None], (count,) + block.shape)
    return lax.all_to_all(copies, axis, 0, 0, tiled=True)


def payload_kernel(features, conv, skip, lengths, copies, planes, taps, skips, valid, rows, done):
    moves = [
        pltpu.make_async_copy(source, target, done.at[index])
        for index, (source, target) in enumerate(
            ((features, planes), (conv, taps), (skip, skips), (lengths, valid))
        )
    ]
    for move in moves:
        move.start()
    for move in moves:
        move.wait()
    count, channels = taps.shape[0], planes.shape[-1]
    span = lax.axis_index(TM)
    pick = lax.broadcasted_iota(jnp.int32, (count, SPANS, OUT), 1) == span
    rows[...] = jnp.zeros_like(rows)
    rows[0:count, :] = jnp.sum(jnp.where(pick, taps[...].astype(jnp.float32), 0.0), axis=1)
    pick = lax.broadcasted_iota(jnp.int32, (SPANS, OUT), 0) == span
    rows[count : count + 1, :] = jnp.sum(
        jnp.where(pick, skips[...].astype(jnp.float32), 0.0), axis=0, keepdims=True
    )
    group = lax.broadcasted_iota(jnp.int32, (channels, 128), 0) // (channels // GROUPS)
    lane = lax.broadcasted_iota(jnp.int32, (channels, 128), 1)
    sums = jnp.zeros((1, 128), jnp.float32)
    for video in range(VIDEOS):
        linear = jnp.zeros((1, channels), jnp.float32)
        square = jnp.zeros((1, channels), jnp.float32)
        for frame in range(FRAMES):
            block = planes[video * FRAMES + frame].astype(jnp.float32)
            shown = (span * FRAMES + frame < valid[video]).astype(jnp.float32)
            linear += jnp.sum(block, axis=0, keepdims=True) * shown
            square += jnp.sum(block * block, axis=0, keepdims=True) * shown
        for which, value in ((video, linear), (VIDEOS + video, square)):
            chosen = (lane == group + which * GROUPS).astype(jnp.float32)
            sums += jnp.dot(
                value, chosen, precision=lax.Precision.HIGHEST, preferred_element_type=jnp.float32
            )
    high = sums.astype(jnp.bfloat16).astype(jnp.float32)
    middle = (sums - high).astype(jnp.bfloat16).astype(jnp.float32)
    rows[count + 1 : count + 2, 0:128] = high
    rows[count + 1 : count + 2, 128:256] = middle
    rows[count + 2 : count + 3, 0:128] = sums - high - middle
    value = rows[...].astype(jnp.bfloat16)
    for index in range(copies.shape[0]):
        copies[index] = value


def member_kernel(features, shares, tails):
    voxels, channels = features.shape[0] * COLS, features.shape[-1]
    column = lax.broadcasted_iota(jnp.int32, (channels, channels), 1)
    place = column % PART
    source = place % SHARE * SPANS + column // PART * 2 + place // SHARE
    match = lax.broadcasted_iota(jnp.int32, (channels, channels), 0) == source
    chosen = jnp.where(match, 1.0, 0.0).astype(jnp.bfloat16)
    for row in range(2):
        block = features[:, row * COLS : (row + 1) * COLS].reshape(voxels, channels)
        flat = jnp.dot(block, chosen, preferred_element_type=jnp.float32).astype(jnp.bfloat16)
        flat = flat.reshape(VIDEOS, FRAMES, COLS, channels)
        lanes = slice(row * PART, (row + 1) * PART)
        for chip in range(CHIPS):
            part = flat[..., chip * PART : (chip + 1) * PART]
            shares[chip, :, :, :, lanes] = part
            tails[chip, :, :, :, lanes] = part[:, FRAMES - 2 :]


def norm_kernel(
    lengths, totals, gain, bias, signal, above, below, shifted, raw, factor, moments,
    *, cells, tiles, tap_bound, skip_bound
):
    chip, core = lax.axis_index("x"), lax.axis_index("core")
    tile = lax.axis_index(TILE)
    summed = [totals[0:1, :]]
    for span in range(1, SPANS):
        summed.append(summed[-1] + totals[span : span + 1, :])
    summed = jnp.concatenate(summed, axis=0)
    entry = lax.broadcasted_iota(jnp.int32, (128, PART), 0)
    group = lax.broadcasted_iota(jnp.int32, (128, PART), 1) % SHARE // 2
    ends = (lax.broadcasted_iota(jnp.int32, (SPANS, PART), 0) + 1) * FRAMES

    def spread(which):
        chosen = (entry == group + which * GROUPS).astype(jnp.float32)
        return jnp.dot(
            summed, chosen, precision=lax.Precision.HIGHEST, preferred_element_type=jnp.float32
        )

    ratio = jnp.zeros((SPANS, PART), jnp.float32)
    largest = jnp.zeros((SPANS, PART), jnp.float32)
    for video in range(VIDEOS):
        seen = jnp.minimum(ends, lengths[video]).astype(jnp.float32) * cells
        square = spread(VIDEOS + video)
        centre = spread(video) / seen
        inverse = lax.rsqrt(square / seen - centre * centre + EPS)
        moments[2 * video] = centre
        moments[2 * video + 1] = inverse * gain[...]
        size = jnp.sqrt(square)
        ratio = jnp.maximum(ratio, size * inverse)
        largest = jnp.maximum(largest, size)
    bound = tap_bound * (3.0 * jnp.max(ratio, keepdims=True) + 3.0)
    bound = bound + skip_bound * jnp.max(largest, keepdims=True)
    factor[...] = jnp.broadcast_to(jnp.exp2(14.0 - jnp.floor(jnp.log2(bound))), factor.shape)

    offset = bias[...].reshape(1, 1, PART)

    def normed(value, video, span, first):
        centre = moments[2 * video, pl.ds(span, 1)].reshape(1, 1, PART)
        scale = moments[2 * video + 1, pl.ds(span, 1)].reshape(1, 1, PART)
        shown = lax.broadcasted_iota(jnp.int32, value.shape, 0) + first < lengths[video]
        value = (value.astype(jnp.float32) - centre) * scale + offset
        value = value / (1.0 + jnp.exp(-value))
        return jnp.where(shown, value, 0.0)

    for step in range(CHIPS):
        span = lax.rem(chip - step + CHIPS, CHIPS) * 2 + core
        before = jnp.maximum(span - 1, 0)
        behind = lax.rem(step + 1 - core, CHIPS)
        for video in range(VIDEOS):
            raw[step, video] = signal[step, video, :FRAMES]
            for row in range(ROWS):
                if row == 0:
                    now, past, lanes, edge = above, above, slice(0, PART), tile == 0
                elif row == ROWS - 1:
                    now, past, lanes, edge = below, below, slice(0, PART), tile == tiles - 1
                else:
                    now, past, lanes, edge = signal, signal, slice((row - 1) * PART, row * PART), None
                value = now[step, video, :FRAMES, :, lanes]
                old = past[behind, video, FRAMES:, :, lanes]
                if edge is not None:
                    same = slice(0, PART) if row == 0 else slice(PART, 2 * PART)
                    value = jnp.where(edge, signal[step, video, :FRAMES, :, same], value)
                    old = jnp.where(edge, signal[behind, video, FRAMES:, :, same], old)
                value = normed(value, video, span, span * FRAMES)
                old = normed(old, video, before, span * FRAMES - 2)
                old = jnp.where(span == 0, jnp.broadcast_to(value[:1], old.shape), old)
                value = jnp.concatenate([old, value], axis=0)
                left = jnp.concatenate([value[:, :1], value[:, :-1]], axis=1)
                right = jnp.concatenate([value[:, 1:], value[:, -1:]], axis=1)
                lanes = slice(row * PART, (row + 1) * PART)
                for side, part in enumerate((left, value, right)):
                    shifted[side, step, video, :, :, lanes] = part.astype(jnp.bfloat16)


def taps_kernel(shifted, raw, factor, mine, theirs, out, weights):
    chip, core = lax.axis_index("x"), lax.axis_index("core")
    count = mine.shape[0]
    for tap in range(count):
        weights[tap, pl.ds(pl.multiple_of(core * SHARE, SHARE), SHARE)] = mine[tap]
        weights[tap, pl.ds(pl.multiple_of((1 - core) * SHARE, SHARE), SHARE)] = theirs[tap]
    for row in range(2):
        total = None
        for pair in range(count // 2):
            blocks = []
            for tap in (2 * pair, 2 * pair + 1):
                if tap < count - 1:
                    at = (row + tap // 3 % 3) * PART
                    first = tap // 9
                    block = shifted[tap % 3, :, :, first : first + FRAMES, :, at : at + PART]
                else:
                    block = raw[..., row * PART : (row + 1) * PART]
                blocks.append(block.reshape(-1, PART))
            term = jnp.dot(
                jnp.concatenate(blocks, axis=1),
                weights[2 * pair : 2 * pair + 2].reshape(2 * PART, OUT),
                preferred_element_type=jnp.float32,
            )
            total = term if total is None else total + term
        total = (total * factor[...]).astype(out.dtype)
        total = total.reshape(CHIPS, -1, COLS, OUT)
        for step in range(CHIPS):
            owner = lax.rem(chip - step + CHIPS, CHIPS)
            out[owner, :, row * COLS : (row + 1) * COLS, :] = total[step]


def per_device(features, lengths, gain_in, bias_in, conv_in, skip_weight):
    videos, frames, row_count, col_count, wide_in = features.shape
    span, chip = lax.axis_index(TM), lax.axis_index("x")
    tiles, chips = lax.axis_size(TILE), lax.axis_size("x")
    taps = conv_in.shape[1]
    on_chip = pl.BlockSpec(memory_space=pltpu.VMEM)
    anywhere = pl.BlockSpec(memory_space=pl.ANY)
    scalar = pl.BlockSpec(memory_space=pltpu.SMEM)
    params = pltpu.CompilerParams(vmem_limit_bytes=20 * 1024 * 1024)

    planes = features.reshape(videos * frames, row_count * col_count, wide_in)
    copies = pl.pallas_call(
        payload_kernel,
        out_shape=jax.ShapeDtypeStruct((tiles, 32, OUT), jnp.bfloat16),
        in_specs=[anywhere] * 4,
        out_specs=on_chip,
        scratch_shapes=[
            pltpu.VMEM(planes.shape, jnp.bfloat16),
            pltpu.VMEM((taps, SPANS, OUT), jnp.bfloat16),
            pltpu.VMEM((SPANS, OUT), jnp.bfloat16),
            pltpu.SMEM((videos,), jnp.int32),
            pltpu.VMEM((32, OUT), jnp.float32),
            pltpu.SemaphoreType.DMA((4,)),
        ],
        compiler_params=pltpu.CompilerParams(vmem_limit_bytes=63 * 1024 * 1024),
        name="payload",
    )(planes, conv_in.transpose(1, 0, 2), skip_weight, lengths)
    arrived = lax.all_to_all(copies, TILE, 0, 0, tiled=True)

    shape = (chips, videos, frames, col_count, 2 * PART)
    shares, tails = pl.pallas_call(
        member_kernel,
        out_shape=(
            jax.ShapeDtypeStruct(shape, jnp.bfloat16),
            jax.ShapeDtypeStruct(shape[:2] + (2,) + shape[3:], jnp.bfloat16),
        ),
        in_specs=[on_chip],
        out_specs=(on_chip, on_chip),
        compiler_params=params,
        name="member_shares",
    )(planes)
    swap = [(0, 1), (1, 0)]
    shares = jnp.concatenate([shares, lax.ppermute(tails, "core", swap)], axis=2)
    signal = []
    for step in range(chips):
        block = lax.dynamic_index_in_dim(shares, lax.rem(chip + step, chips), 0, False)
        if step:
            block = lax.ppermute(block, "x", [(i, (i + step) % chips) for i in range(chips)])
        signal.append(block)
    signal = jnp.stack(signal)
    upper, lower = signal[..., PART:], signal[..., :PART]
    above = lax.ppermute(upper, TILE, [(i, i + 1) for i in range(tiles - 1)])
    below = lax.ppermute(lower, TILE, [(i + 1, i) for i in range(tiles - 1)])

    def lanes(vector):
        own = lax.dynamic_slice_in_dim(vector.reshape(SHARE, SPANS), 2 * chip, 2, axis=1)
        return own.T.reshape(1, PART)

    parts = jnp.sum(arrived[:, taps + 1 : taps + 3].astype(jnp.float32), axis=0)
    sums = parts[:1, :128] + parts[:1, 128:] + parts[1:, :128]
    gain, bias = lanes(gain_in), lanes(bias_in)
    sums, upper, lower, gain, bias = lax.optimization_barrier((sums, upper, lower, gain, bias))
    copies = jnp.broadcast_to(sums[None], (SPANS,) + sums.shape)
    totals = lax.all_to_all(copies, TM, 0, 0, tiled=True).reshape(SPANS, -1)
    mine = arrived[:, : taps + 1].transpose(1, 0, 2)
    theirs = lax.ppermute(mine, "core", swap)

    shifted, raw, factor = pl.pallas_call(
        functools.partial(
            norm_kernel,
            cells=float(row_count * tiles * col_count * (wide_in // GROUPS)),
            tiles=tiles,
            tap_bound=float(taps * PART) * 0.0546875,
            skip_bound=float(PART) * 0.25,
        ),
        out_shape=(
            jax.ShapeDtypeStruct(
                (3, chips, videos, frames + 2, col_count, ROWS * PART), jnp.bfloat16
            ),
            jax.ShapeDtypeStruct((chips, videos, frames, col_count, 2 * PART), jnp.bfloat16),
            jax.ShapeDtypeStruct((1, OUT), jnp.float32),
        ),
        in_specs=[scalar] + [on_chip] * 6,
        out_specs=(on_chip, on_chip, on_chip),
        scratch_shapes=[pltpu.VMEM((2 * videos, SPANS, PART), jnp.float32)],
        compiler_params=params,
        cost_estimate=pl.CostEstimate(flops=1 << 34, bytes_accessed=1 << 26, transcendentals=1 << 24),
        name="norm",
    )(lengths, totals, gain, bias, signal, above, below)
    total = pl.pallas_call(
        taps_kernel,
        out_shape=jax.ShapeDtypeStruct((chips, videos * frames, row_count * col_count, OUT), jnp.float32),
        in_specs=[on_chip] * 5,
        out_specs=on_chip,
        scratch_shapes=[pltpu.VMEM((taps + 1, PART, OUT), jnp.bfloat16)],
        compiler_params=params,
        cost_estimate=pl.CostEstimate(
            flops=2 * 28 * 1024 * 128 * 256, bytes_accessed=6 << 20, transcendentals=0
        ),
        name="taps",
    )(shifted, raw, factor, mine, theirs)

    total = total.astype(jnp.float16)
    total = lax.all_to_all(total, "x", 0, 0, tiled=True)
    total = jnp.sum(total.astype(jnp.float32), axis=0) / factor
    total = total.reshape(videos, frames, row_count, col_count, OUT)
    stamps = span * frames + jnp.arange(frames, dtype=jnp.int32)
    present = stamps[None, :] < lengths[:, None]
    return jnp.where(present[:, :, None, None, None], total, 0.0).astype(jnp.bfloat16)


def solution(mesh):
    spans, tiles = mesh.devices.shape
    fine = Mesh(mesh.devices.reshape(spans // 2, 2, 8, tiles // 8), TM + TILE)
    placed = (
        P(None, TM, TILE, None, None),
        P(),
        P(),
        P(),
        P(TILE, None, None),
        P(TILE, None),
    )
    return jax.shard_map(
        per_device,
        mesh=fine,
        in_specs=placed,
        out_specs=P(None, TM, TILE, None, None),
        check_vma=False,
    )
```

```python
import functools

import jax
import jax.numpy as jnp
from jax import lax
from jax.experimental import pallas as pl
from jax.experimental.pallas import tpu as pltpu
from jax.sharding import Mesh
from jax.sharding import PartitionSpec as P

GROUPS = 32
EPS = 1e-06
TM = ("x", "core")
TILE = ("y", "z")
SPANS = 8
VIDEOS = 2
FRAMES = 4
COLS = 16
SHARE = 64
CHIPS = 4
PART = 2 * SHARE
ROWS = 4
OUT = 256


def to_all(block, axis):
    count = lax.axis_size(axis)
    copies = jnp.broadcast_to(block[None], (count,) + block.shape)
    return lax.all_to_all(copies, axis, 0, 0, tiled=True)


def exact_dot(value, chosen):
    high = value.astype(jnp.bfloat16)
    rest = value - high.astype(jnp.float32)
    middle = rest.astype(jnp.bfloat16)
    low = (rest - middle.astype(jnp.float32)).astype(jnp.bfloat16)
    total = jnp.dot(low, chosen, preferred_element_type=jnp.float32)
    total = total + jnp.dot(middle, chosen, preferred_element_type=jnp.float32)
    return total + jnp.dot(high, chosen, preferred_element_type=jnp.float32)


def payload_kernel(features, conv, skip, lengths, copies, planes, taps, skips, valid, rows, done):
    moves = [
        pltpu.make_async_copy(source, target, done.at[index])
        for index, (source, target) in enumerate(
            ((features, planes), (conv, taps), (skip, skips), (lengths, valid))
        )
    ]
    for move in moves:
        move.start()
    for move in moves:
        move.wait()
    count, channels = taps.shape[0], planes.shape[-1]
    span = lax.axis_index(TM)
    pick = lax.broadcasted_iota(jnp.int32, (count, SPANS, OUT), 1) == span
    rows[...] = jnp.zeros_like(rows)
    rows[0:count, :] = jnp.sum(jnp.where(pick, taps[...].astype(jnp.float32), 0.0), axis=1)
    pick = lax.broadcasted_iota(jnp.int32, (SPANS, OUT), 0) == span
    rows[count : count + 1, :] = jnp.sum(
        jnp.where(pick, skips[...].astype(jnp.float32), 0.0), axis=0, keepdims=True
    )
    lines = []
    for video in range(VIDEOS):
        linear = jnp.zeros((1, channels), jnp.float32)
        square = jnp.zeros((1, channels), jnp.float32)
        for frame in range(FRAMES):
            block = planes[video * FRAMES + frame].astype(jnp.float32)
            shown = (span * FRAMES + frame < valid[video]).astype(jnp.float32)
            linear += jnp.sum(block, axis=0, keepdims=True) * shown
            square += jnp.sum(block * block, axis=0, keepdims=True) * shown
        lines += [(video, linear), (VIDEOS + video, square)]
    lines = jnp.concatenate([line for _, line in sorted(lines, key=lambda pair: pair[0])], axis=0)
    group = lax.broadcasted_iota(jnp.int32, (channels, 128), 0) // (channels // GROUPS)
    lane = lax.broadcasted_iota(jnp.int32, (channels, 128), 1)
    spots = exact_dot(lines, (lane % GROUPS == group).astype(jnp.bfloat16))
    line = lax.broadcasted_iota(jnp.int32, spots.shape, 0)
    lane = lax.broadcasted_iota(jnp.int32, spots.shape, 1)
    sums = jnp.sum(jnp.where(lane // GROUPS == line, spots, 0.0), axis=0, keepdims=True)
    high = sums.astype(jnp.bfloat16).astype(jnp.float32)
    middle = (sums - high).astype(jnp.bfloat16).astype(jnp.float32)
    rows[count + 1 : count + 2, 0:128] = high
    rows[count + 1 : count + 2, 128:256] = middle
    rows[count + 2 : count + 3, 0:128] = sums - high - middle
    value = rows[...].astype(jnp.bfloat16)
    for index in range(copies.shape[0]):
        copies[index] = value


def sums_kernel(arrived, copies, *, first):
    at = first // 16 * 16
    rows = jnp.sum(arrived[:, at : at + 16, :].astype(jnp.float32), axis=0)
    rows = rows[first - at : first - at + 2]
    total = rows[1:2, 0:128] + rows[0:1, 128:256] + rows[0:1, 0:128]
    copies[...] = jnp.broadcast_to(total[None], copies.shape)


def member_kernel(features, shares, tails):
    voxels, channels = features.shape[0] * COLS, features.shape[-1]
    column = lax.broadcasted_iota(jnp.int32, (channels, channels), 1)
    place = column % PART
    source = place % SHARE * SPANS + column // PART * 2 + place // SHARE
    match = lax.broadcasted_iota(jnp.int32, (channels, channels), 0) == source
    chosen = jnp.where(match, 1.0, 0.0).astype(jnp.bfloat16)
    for row in range(2):
        block = features[:, row * COLS : (row + 1) * COLS].reshape(voxels, channels)
        flat = jnp.dot(block, chosen, preferred_element_type=jnp.float32).astype(jnp.bfloat16)
        flat = flat.reshape(VIDEOS, FRAMES, COLS, channels)
        lanes = slice(row * PART, (row + 1) * PART)
        for chip in range(CHIPS):
            part = flat[..., chip * PART : (chip + 1) * PART]
            shares[chip, :, :, :, lanes] = part
            tails[chip, :, :, :, lanes] = part[:, FRAMES - 2 :]


def norm_kernel(
    lengths, totals, gain, bias, signal, above, below, shifted, raw, factor, moments,
    *, cells, tiles, tap_bound, skip_bound
):
    chip, core = lax.axis_index("x"), lax.axis_index("core")
    tile = lax.axis_index(TILE)
    summed = [totals[0:1, :]]
    for span in range(1, SPANS):
        summed.append(summed[-1] + totals[span : span + 1, :])
    summed = jnp.concatenate(summed, axis=0)
    entry = lax.broadcasted_iota(jnp.int32, (128, 4 * PART), 0)
    lane = lax.broadcasted_iota(jnp.int32, (128, 4 * PART), 1)
    wanted = lane // PART * GROUPS + lane % SHARE // 2
    spread = exact_dot(summed, (entry == wanted).astype(jnp.bfloat16))
    ends = (lax.broadcasted_iota(jnp.int32, (SPANS, PART), 0) + 1) * FRAMES

    ratio = jnp.zeros((SPANS, PART), jnp.float32)
    largest = jnp.zeros((SPANS, PART), jnp.float32)
    for video in range(VIDEOS):
        seen = jnp.minimum(ends, lengths[video]).astype(jnp.float32) * cells
        square = spread[:, (VIDEOS + video) * PART : (VIDEOS + video + 1) * PART]
        centre = spread[:, video * PART : (video + 1) * PART] / seen
        inverse = lax.rsqrt(square / seen - centre * centre + EPS)
        moments[2 * video] = centre
        moments[2 * video + 1] = 0.5 * inverse * gain[...]
        size = jnp.sqrt(square)
        ratio = jnp.maximum(ratio, size * inverse)
        largest = jnp.maximum(largest, size)
    bound = tap_bound * (3.0 * jnp.max(ratio, keepdims=True) + 3.0)
    bound = bound + skip_bound * jnp.max(largest, keepdims=True)
    factor[...] = jnp.broadcast_to(jnp.exp2(14.0 - jnp.floor(jnp.log2(bound))), factor.shape)

    def normed(value, video, span, first):
        frame = lax.broadcasted_iota(jnp.int32, (value.shape[0], 1, PART), 0) + first
        shown = frame < lengths[video]
        centre = moments[2 * video, pl.ds(span, 1)].reshape(1, 1, PART)
        scale = jnp.where(shown, moments[2 * video + 1, pl.ds(span, 1)].reshape(1, 1, PART), 0.0)
        offset = jnp.where(shown, 0.5 * bias[...].reshape(1, 1, PART), 0.0)
        value = (value.astype(jnp.float32) - centre) * scale + offset
        return value + value * jnp.tanh(value)

    for step in range(CHIPS):
        span = lax.rem(chip - step + CHIPS, CHIPS) * 2 + core
        before = jnp.maximum(span - 1, 0)
        behind = lax.rem(step + 1 - core, CHIPS)
        for video in range(VIDEOS):
            raw[step, video] = signal[step, video, :FRAMES]
            for row in range(ROWS):
                if row == 0:
                    now, past, lanes, edge = above, above, slice(0, PART), tile == 0
                elif row == ROWS - 1:
                    now, past, lanes, edge = below, below, slice(0, PART), tile == tiles - 1
                else:
                    now, past, lanes, edge = signal, signal, slice((row - 1) * PART, row * PART), None
                value = now[step, video, :FRAMES, :, lanes]
                old = past[behind, video, FRAMES:, :, lanes]
                if edge is not None:
                    same = slice(0, PART) if row == 0 else slice(PART, 2 * PART)
                    value = jnp.where(edge, signal[step, video, :FRAMES, :, same], value)
                    old = jnp.where(edge, signal[behind, video, FRAMES:, :, same], old)
                value = normed(value, video, span, span * FRAMES)
                old = normed(old, video, before, span * FRAMES - 2)
                old = jnp.where(span == 0, jnp.broadcast_to(value[:1], old.shape), old)
                value = jnp.concatenate([old, value], axis=0)
                left = jnp.concatenate([value[:, :1], value[:, :-1]], axis=1)
                right = jnp.concatenate([value[:, 1:], value[:, -1:]], axis=1)
                lanes = slice(row * PART, (row + 1) * PART)
                for side, part in enumerate((left, value, right)):
                    shifted[side, step, video, :, :, lanes] = part.astype(jnp.bfloat16)


def taps_kernel(shifted, raw, factor, mine, theirs, out, weights):
    chip, core = lax.axis_index("x"), lax.axis_index("core")
    count = mine.shape[0]
    for tap in range(count):
        weights[tap, pl.ds(pl.multiple_of(core * SHARE, SHARE), SHARE)] = mine[tap]
        weights[tap, pl.ds(pl.multiple_of((1 - core) * SHARE, SHARE), SHARE)] = theirs[tap]
    for row in range(2):
        total = None
        for pair in range(count // 2):
            blocks = []
            for tap in (2 * pair, 2 * pair + 1):
                if tap < count - 1:
                    at = (row + tap // 3 % 3) * PART
                    first = tap // 9
                    block = shifted[tap % 3, :, :, first : first + FRAMES, :, at : at + PART]
                else:
                    block = raw[..., row * PART : (row + 1) * PART]
                blocks.append(block.reshape(-1, PART))
            term = jnp.dot(
                jnp.concatenate(blocks, axis=1),
                weights[2 * pair : 2 * pair + 2].reshape(2 * PART, OUT),
                preferred_element_type=jnp.float32,
            )
            total = term if total is None else total + term
        total = (total * factor[...]).astype(out.dtype)
        total = total.reshape(CHIPS, -1, COLS, OUT)
        for step in range(CHIPS):
            owner = lax.rem(chip - step + CHIPS, CHIPS)
            out[owner, :, row * COLS : (row + 1) * COLS, :] = total[step]


def per_device(features, lengths, gain_in, bias_in, conv_in, skip_weight):
    videos, frames, row_count, col_count, wide_in = features.shape
    span, chip = lax.axis_index(TM), lax.axis_index("x")
    tiles, chips = lax.axis_size(TILE), lax.axis_size("x")
    taps = conv_in.shape[1]
    on_chip = pl.BlockSpec(memory_space=pltpu.VMEM)
    outside = pl.BlockSpec(memory_space=pl.ANY)
    scalar = pl.BlockSpec(memory_space=pltpu.SMEM)
    params = pltpu.CompilerParams(vmem_limit_bytes=20 * 1024 * 1024)

    planes = features.reshape(videos * frames, row_count * col_count, wide_in)
    copies = pl.pallas_call(
        payload_kernel,
        out_shape=jax.ShapeDtypeStruct((tiles, 32, OUT), jnp.bfloat16),
        in_specs=[outside] * 4,
        out_specs=on_chip,
        scratch_shapes=[
            pltpu.VMEM(planes.shape, jnp.bfloat16),
            pltpu.VMEM((taps, SPANS, OUT), jnp.bfloat16),
            pltpu.VMEM((SPANS, OUT), jnp.bfloat16),
            pltpu.SMEM((videos,), jnp.int32),
            pltpu.VMEM((32, OUT), jnp.float32),
            pltpu.SemaphoreType.DMA((4,)),
        ],
        compiler_params=params,
        name="payload",
    )(
        *[
            pltpu.with_memory_space_constraint(value, pltpu.HBM)
            for value in (planes, conv_in.transpose(1, 0, 2), skip_weight, lengths)
        ]
    )
    arrived = lax.all_to_all(copies, TILE, 0, 0, tiled=True)

    shape = (chips, videos, frames, col_count, 2 * PART)
    shares, tails = pl.pallas_call(
        member_kernel,
        out_shape=(
            jax.ShapeDtypeStruct(shape, jnp.bfloat16),
            jax.ShapeDtypeStruct(shape[:2] + (2,) + shape[3:], jnp.bfloat16),
        ),
        in_specs=[on_chip],
        out_specs=(on_chip, on_chip),
        compiler_params=params,
        name="member_shares",
    )(planes)
    swap = [(0, 1), (1, 0)]
    shares = jnp.concatenate([shares, lax.ppermute(tails, "core", swap)], axis=2)
    signal = []
    for step in range(chips):
        block = lax.dynamic_index_in_dim(shares, lax.rem(chip + step, chips), 0, False)
        if step:
            block = lax.ppermute(block, "x", [(i, (i + step) % chips) for i in range(chips)])
        signal.append(block)
    signal = jnp.stack(signal)
    upper, lower = signal[..., PART:], signal[..., :PART]
    above = lax.ppermute(upper, TILE, [(i, i + 1) for i in range(tiles - 1)])
    below = lax.ppermute(lower, TILE, [(i + 1, i) for i in range(tiles - 1)])

    def lanes(vector):
        own = lax.dynamic_slice_in_dim(vector.reshape(SHARE, SPANS), 2 * chip, 2, axis=1)
        return own.T.reshape(1, PART)

    gain, bias = lanes(gain_in), lanes(bias_in)
    held, upper, lower, gain, bias = lax.optimization_barrier((arrived, upper, lower, gain, bias))
    copies = pl.pallas_call(
        functools.partial(sums_kernel, first=taps + 1),
        out_shape=jax.ShapeDtypeStruct((SPANS, 1, 128), jnp.float32),
        in_specs=[on_chip],
        out_specs=on_chip,
        compiler_params=params,
        name="sums",
    )(pltpu.with_memory_space_constraint(held, pltpu.VMEM))
    totals = lax.all_to_all(copies, TM, 0, 0, tiled=True).reshape(SPANS, -1)
    mine = arrived[:, : taps + 1].transpose(1, 0, 2)
    theirs = lax.ppermute(mine, "core", swap)

    shifted, raw, factor = pl.pallas_call(
        functools.partial(
            norm_kernel,
            cells=float(row_count * tiles * col_count * (wide_in // GROUPS)),
            tiles=tiles,
            tap_bound=float(taps * PART) * 0.0546875,
            skip_bound=float(PART) * 0.25,
        ),
        out_shape=(
            jax.ShapeDtypeStruct(
                (3, chips, videos, frames + 2, col_count, ROWS * PART), jnp.bfloat16
            ),
            jax.ShapeDtypeStruct((chips, videos, frames, col_count, 2 * PART), jnp.bfloat16),
            jax.ShapeDtypeStruct((1, OUT), jnp.float32),
        ),
        in_specs=[scalar] + [on_chip] * 6,
        out_specs=(on_chip, on_chip, on_chip),
        scratch_shapes=[pltpu.VMEM((2 * videos, SPANS, PART), jnp.float32)],
        compiler_params=params,
        cost_estimate=pl.CostEstimate(flops=1 << 34, bytes_accessed=1 << 26, transcendentals=1 << 24),
        name="norm",
    )(lengths, totals, gain, bias, signal, above, below)
    total = pl.pallas_call(
        taps_kernel,
        out_shape=jax.ShapeDtypeStruct((chips, videos * frames, row_count * col_count, OUT), jnp.float32),
        in_specs=[on_chip] * 5,
        out_specs=on_chip,
        scratch_shapes=[pltpu.VMEM((taps + 1, PART, OUT), jnp.bfloat16)],
        compiler_params=params,
        cost_estimate=pl.CostEstimate(
            flops=2 * 28 * 1024 * 128 * 256, bytes_accessed=6 << 20, transcendentals=0
        ),
        name="taps",
    )(shifted, raw, factor, mine, theirs)

    total = total.astype(jnp.float16)
    total = lax.all_to_all(total, "x", 0, 0, tiled=True)
    total = jnp.sum(total.astype(jnp.float32), axis=0) / factor
    total = total.reshape(videos, frames, row_count, col_count, OUT)
    stamps = span * frames + jnp.arange(frames, dtype=jnp.int32)
    present = stamps[None, :] < lengths[:, None]
    return jnp.where(present[:, :, None, None, None], total, 0.0).astype(jnp.bfloat16)


def solution(mesh):
    spans, tiles = mesh.devices.shape
    fine = Mesh(mesh.devices.reshape(spans // 2, 2, 8, tiles // 8), TM + TILE)
    placed = (
        P(None, TM, TILE, None, None),
        P(),
        P(),
        P(),
        P(TILE, None, None),
        P(TILE, None),
    )
    return jax.shard_map(
        per_device,
        mesh=fine,
        in_specs=placed,
        out_specs=P(None, TM, TILE, None, None),
        check_vma=False,
    )
```

```python
import functools

import jax
import jax.numpy as jnp
from jax import lax
from jax.experimental import pallas as pl
from jax.experimental.pallas import tpu as pltpu
from jax.sharding import Mesh
from jax.sharding import PartitionSpec as P

GROUPS = 32
EPS = 1e-06
TM = ("x", "core")
TILE = ("y", "z")
SPANS = 8
VIDEOS = 2
FRAMES = 4
COLS = 16
SHARE = 64
CHIPS = 4
PART = 2 * SHARE
ROWS = 4
LINE = 15
OUT = 256


def to_all(block, axis):
    count = lax.axis_size(axis)
    copies = jnp.broadcast_to(block[None], (count,) + block.shape)
    return lax.all_to_all(copies, axis, 0, 0, tiled=True)


def exact_dot(value, chosen):
    high = value.astype(jnp.bfloat16)
    rest = value - high.astype(jnp.float32)
    middle = rest.astype(jnp.bfloat16)
    low = (rest - middle.astype(jnp.float32)).astype(jnp.bfloat16)
    total = jnp.dot(low, chosen, preferred_element_type=jnp.float32)
    total = total + jnp.dot(middle, chosen, preferred_element_type=jnp.float32)
    return total + jnp.dot(high, chosen, preferred_element_type=jnp.float32)


def payload_kernel(features, conv, skip, lengths, copies, planes, taps, skips, valid, rows, packed, few, done, left):
    moves = [
        pltpu.make_async_copy(source, target, done.at[index])
        for index, (source, target) in enumerate(
            ((features, planes), (conv, taps), (skip, skips), (lengths, valid))
        )
    ]
    for move in moves:
        move.start()
    for move in moves:
        move.wait()
    count, channels = taps.shape[0], planes.shape[-1]
    span = lax.axis_index(TM)
    pick = lax.broadcasted_iota(jnp.int32, (count, SPANS, OUT), 1) == span
    rows[...] = jnp.zeros_like(rows)
    rows[0:count, :] = jnp.sum(jnp.where(pick, taps[...].astype(jnp.float32), 0.0), axis=1)
    pick = lax.broadcasted_iota(jnp.int32, (SPANS, OUT), 0) == span
    rows[count : count + 1, :] = jnp.sum(
        jnp.where(pick, skips[...].astype(jnp.float32), 0.0), axis=0, keepdims=True
    )
    lines = []
    for video in range(VIDEOS):
        linear = jnp.zeros((1, channels), jnp.float32)
        square = jnp.zeros((1, channels), jnp.float32)
        for frame in range(FRAMES):
            block = planes[video * FRAMES + frame].astype(jnp.float32)
            shown = (span * FRAMES + frame < valid[video]).astype(jnp.float32)
            linear += jnp.sum(block, axis=0, keepdims=True) * shown
            square += jnp.sum(block * block, axis=0, keepdims=True) * shown
        lines += [(video, linear), (VIDEOS + video, square)]
    lines = jnp.concatenate([line for _, line in sorted(lines, key=lambda pair: pair[0])], axis=0)
    group = lax.broadcasted_iota(jnp.int32, (channels, 128), 0) // (channels // GROUPS)
    lane = lax.broadcasted_iota(jnp.int32, (channels, 128), 1)
    spots = exact_dot(lines, (lane % GROUPS == group).astype(jnp.bfloat16))
    line = lax.broadcasted_iota(jnp.int32, spots.shape, 0)
    lane = lax.broadcasted_iota(jnp.int32, spots.shape, 1)
    sums = jnp.sum(jnp.where(lane // GROUPS == line, spots, 0.0), axis=0, keepdims=True)
    high = sums.astype(jnp.bfloat16).astype(jnp.float32)
    middle = (sums - high).astype(jnp.bfloat16).astype(jnp.float32)
    rows[count + 1 : count + 2, 0:128] = high
    rows[count + 1 : count + 2, 128:256] = middle
    rows[count + 2 : count + 3, 0:128] = sums - high - middle
    for row in range(2 * LINE):
        at = row % LINE * OUT
        packed[row // LINE : row // LINE + 1, at : at + OUT] = rows[row : row + 1, :]
    value = packed[...].astype(jnp.bfloat16)
    some = few.shape[0]
    for index in range(some):
        few[index] = value
    moves = [
        pltpu.make_async_copy(few, copies.at[pl.ds(index * some, some)], left.at[index])
        for index in range(copies.shape[0] // some)
    ]
    for move in moves:
        move.start()
    for move in moves:
        move.wait()


def sums_kernel(arrived, copies, *, first):
    at = (first - LINE) * OUT
    line = jnp.sum(arrived[:, :, at : at + 2 * OUT].astype(jnp.float32), axis=0)[1:2]
    total = line[:, 256:384] + line[:, 128:256] + line[:, 0:128]
    copies[...] = jnp.broadcast_to(total[None], copies.shape)


def member_kernel(features, gain, bias, kept, sent, lanes):
    voxels, channels = features.shape[0] * COLS, features.shape[-1]
    column = lax.broadcasted_iota(jnp.int32, (channels, channels), 1)
    place = column % PART
    source = place % SHARE * SPANS + column // PART * 2 + place // SHARE
    match = lax.broadcasted_iota(jnp.int32, (channels, channels), 0) == source
    chosen = jnp.where(match, 1.0, 0.0).astype(jnp.bfloat16)
    even = lax.axis_index("core") == 0
    for row in range(2):
        block = features[:, row * COLS : (row + 1) * COLS].reshape(voxels, channels)
        flat = jnp.dot(block, chosen, preferred_element_type=jnp.float32).astype(jnp.bfloat16)
        flat = flat.reshape(VIDEOS, FRAMES, COLS, channels)
        mine, other = jnp.where(even, flat[0], flat[1]), jnp.where(even, flat[1], flat[0])
        at = slice(row * PART, (row + 1) * PART)
        for chip in range(CHIPS):
            kept[chip, :, :, at] = mine[..., chip * PART : (chip + 1) * PART]
            sent[chip, :, :, at] = other[..., chip * PART : (chip + 1) * PART]
    place = lax.broadcasted_iota(jnp.int32, (channels, PART), 1)
    source = place % SHARE * SPANS + lax.axis_index("x") * 2 + place // SHARE
    match = lax.broadcasted_iota(jnp.int32, (channels, PART), 0) == source
    pair = jnp.concatenate([gain[...], bias[...]], axis=0)
    lanes[...] = exact_dot(pair, jnp.where(match, 1.0, 0.0).astype(jnp.bfloat16))


def norm_kernel(
    lengths, totals, lanes, signal, above, below, shifted, raw, factor, moments,
    *, cells, tiles, tap_bound, skip_bound
):
    chip, core = lax.axis_index("x"), lax.axis_index("core")
    tile = lax.axis_index(TILE)
    summed = [totals[0:1, :]]
    for span in range(1, SPANS):
        summed.append(summed[-1] + totals[span : span + 1, :])
    summed = jnp.concatenate(summed, axis=0)
    entry = lax.broadcasted_iota(jnp.int32, (128, 4 * PART), 0)
    lane = lax.broadcasted_iota(jnp.int32, (128, 4 * PART), 1)
    wanted = lane // PART * GROUPS + lane % SHARE // 2
    spread = exact_dot(summed, jnp.where(entry == wanted, 1.0, 0.0).astype(jnp.bfloat16))
    ends = (lax.broadcasted_iota(jnp.int32, (SPANS, PART), 0) + 1) * FRAMES
    for video in range(VIDEOS):
        seen = jnp.minimum(ends, lengths[video]).astype(jnp.float32) * cells
        square = spread[:, (VIDEOS + video) * PART : (VIDEOS + video + 1) * PART]
        centre = spread[:, video * PART : (video + 1) * PART] / seen
        inverse = lax.rsqrt(square / seen - centre * centre + EPS)
        moments[2 * video] = centre
        moments[2 * video + 1] = 0.5 * inverse * lanes[0:1, :]
        size = jnp.sqrt(square)
        bound = tap_bound * (3.0 * jnp.max(size * inverse, keepdims=True) + 3.0)
        bound = bound + skip_bound * jnp.max(size, keepdims=True)
        bound = jnp.exp2(14.0 - jnp.floor(jnp.log2(bound)))
        factor[video : video + 1, :] = jnp.broadcast_to(bound, (1, OUT))
    half_bias = 0.5 * lanes[1:2, :]

    def normed(value, span):
        frame = lax.broadcasted_iota(jnp.int32, (FRAMES, 1, PART), 0) + span * FRAMES
        shown = frame < lengths[core]
        centre = moments[2 * core, pl.ds(span, 1)].reshape(1, 1, PART)
        scale = jnp.where(shown, moments[2 * core + 1, pl.ds(span, 1)].reshape(1, 1, PART), 0.0)
        offset = jnp.where(shown, half_bias.reshape(1, 1, PART), 0.0)
        value = (value.astype(jnp.float32) - centre) * scale + offset
        return value + value * jnp.tanh(value)

    for step in range(CHIPS):
        for other in range(2):
            span = lax.rem(chip - step + CHIPS, CHIPS) * 2 + lax.rem(core + other, 2)
            raw[pl.ds(span * FRAMES, FRAMES)] = signal[step, other]
            for row in range(ROWS):
                if row == 0:
                    value = jnp.where(tile == 0, signal[step, other, :, :, :PART], above[step, other])
                elif row == ROWS - 1:
                    value = jnp.where(
                        tile == tiles - 1, signal[step, other, :, :, PART:], below[step, other]
                    )
                else:
                    value = signal[step, other, :, :, (row - 1) * PART : row * PART]
                value = normed(value, span)
                left = jnp.concatenate([value[:, :1], value[:, :-1]], axis=1)
                right = jnp.concatenate([value[:, 1:], value[:, -1:]], axis=1)
                for side, part in enumerate((left, value, right)):
                    shifted[
                        side, pl.ds(2 + span * FRAMES, FRAMES), :, row * PART : (row + 1) * PART
                    ] = part.astype(jnp.bfloat16)
    for side in range(3):
        shifted[side, 0] = shifted[side, 2]
        shifted[side, 1] = shifted[side, 2]


def taps_kernel(shifted, raw, mine, theirs, factor, out, weights):
    core = lax.axis_index("core")
    count = mine.shape[0]
    for tap in range(count):
        weights[tap, pl.ds(pl.multiple_of(core * SHARE, SHARE), SHARE)] = mine[tap]
        weights[tap, pl.ds(pl.multiple_of((1 - core) * SHARE, SHARE), SHARE)] = theirs[tap]
    length = SPANS * FRAMES
    scale = jnp.where(core == 0, factor[0:1, :], factor[1:2, :])
    for row in range(2):
        total = None
        for pair in range(count // 2):
            blocks = []
            for tap in (2 * pair, 2 * pair + 1):
                if tap < count - 1:
                    at = (row + tap // 3 % 3) * PART
                    block = shifted[tap % 3, tap // 9 : tap // 9 + length, :, at : at + PART]
                else:
                    block = raw[..., row * PART : (row + 1) * PART]
                blocks.append(block.reshape(-1, PART))
            term = jnp.dot(
                jnp.concatenate(blocks, axis=1),
                weights[2 * pair : 2 * pair + 2].reshape(2 * PART, OUT),
                preferred_element_type=jnp.float32,
            )
            total = term if total is None else total + term
        total = (total * scale).reshape(SPANS, FRAMES, COLS, OUT)
        out[:, :, row * COLS : (row + 1) * COLS, :] = total


def per_device(features, lengths, gain_in, bias_in, conv_in, skip_weight):
    videos, frames, row_count, col_count, wide_in = features.shape
    span, chip = lax.axis_index(TM), lax.axis_index("x")
    tiles, chips = lax.axis_size(TILE), lax.axis_size("x")
    taps = conv_in.shape[1]
    on_chip = pl.BlockSpec(memory_space=pltpu.VMEM)
    outside = pl.BlockSpec(memory_space=pl.ANY)
    scalar = pl.BlockSpec(memory_space=pltpu.SMEM)
    params = pltpu.CompilerParams(vmem_limit_bytes=20 * 1024 * 1024)

    planes = features.reshape(videos * frames, row_count * col_count, wide_in)
    copies = pl.pallas_call(
        payload_kernel,
        out_shape=jax.ShapeDtypeStruct((tiles, 2, LINE * OUT), jnp.bfloat16),
        in_specs=[outside] * 4,
        out_specs=outside,
        scratch_shapes=[
            pltpu.VMEM(planes.shape, jnp.bfloat16),
            pltpu.VMEM((taps, SPANS, OUT), jnp.bfloat16),
            pltpu.VMEM((SPANS, OUT), jnp.bfloat16),
            pltpu.SMEM((videos,), jnp.int32),
            pltpu.VMEM((32, OUT), jnp.float32),
            pltpu.VMEM((2, LINE * OUT), jnp.float32),
            pltpu.VMEM((8, 2, LINE * OUT), jnp.bfloat16),
            pltpu.SemaphoreType.DMA((4,)),
            pltpu.SemaphoreType.DMA((tiles // 8,)),
        ],
        compiler_params=params,
        name="payload",
    )(
        *[
            pltpu.with_memory_space_constraint(value, pltpu.HBM)
            for value in (planes, conv_in.transpose(1, 0, 2), skip_weight, lengths)
        ]
    )
    arrived = lax.all_to_all(copies, TILE, 0, 0, tiled=True)

    shape = (chips, frames, col_count, 2 * PART)
    kept, sent, lanes = pl.pallas_call(
        member_kernel,
        out_shape=(
            jax.ShapeDtypeStruct(shape, jnp.bfloat16),
            jax.ShapeDtypeStruct(shape, jnp.bfloat16),
            jax.ShapeDtypeStruct((2, PART), jnp.float32),
        ),
        in_specs=[on_chip] * 3,
        out_specs=(on_chip, on_chip, on_chip),
        compiler_params=params,
        name="member_shares",
    )(planes, gain_in.reshape(1, -1), bias_in.reshape(1, -1))
    swap = [(0, 1), (1, 0)]
    shares = jnp.stack([kept, lax.ppermute(sent, "core", swap)], axis=1)
    signal = []
    for step in range(chips):
        block = lax.dynamic_index_in_dim(shares, lax.rem(chip + step, chips), 0, False)
        if step:
            block = lax.ppermute(block, "x", [(i, (i + step) % chips) for i in range(chips)])
        signal.append(block)
    signal = jnp.stack(signal)
    upper, lower = signal[..., PART:], signal[..., :PART]
    above = lax.ppermute(upper, TILE, [(i, i + 1) for i in range(tiles - 1)])
    below = lax.ppermute(lower, TILE, [(i + 1, i) for i in range(tiles - 1)])

    held, upper, lower = lax.optimization_barrier((arrived, upper, lower))
    copies = pl.pallas_call(
        functools.partial(sums_kernel, first=taps + 1),
        out_shape=jax.ShapeDtypeStruct((SPANS, 1, 128), jnp.float32),
        in_specs=[on_chip],
        out_specs=on_chip,
        compiler_params=params,
        name="sums",
    )(pltpu.with_memory_space_constraint(held, pltpu.VMEM))
    totals = lax.all_to_all(copies, TM, 0, 0, tiled=True).reshape(SPANS, -1)
    mine = arrived.reshape(tiles, 2 * LINE, OUT)[:, : taps + 1].transpose(1, 0, 2)
    theirs = lax.ppermute(mine, "core", swap)

    shifted, raw, factor = pl.pallas_call(
        functools.partial(
            norm_kernel,
            cells=float(row_count * tiles * col_count * (wide_in // GROUPS)),
            tiles=tiles,
            tap_bound=float(taps * PART) * 0.0546875,
            skip_bound=float(PART) * 0.25,
        ),
        out_shape=(
            jax.ShapeDtypeStruct((3, SPANS * frames + 2, col_count, ROWS * PART), jnp.bfloat16),
            jax.ShapeDtypeStruct((SPANS * frames, col_count, 2 * PART), jnp.bfloat16),
            jax.ShapeDtypeStruct((videos, OUT), jnp.float32),
        ),
        in_specs=[scalar] + [on_chip] * 5,
        out_specs=(on_chip, on_chip, on_chip),
        scratch_shapes=[pltpu.VMEM((2 * videos, SPANS, PART), jnp.float32)],
        compiler_params=params,
        cost_estimate=pl.CostEstimate(flops=1 << 34, bytes_accessed=1 << 26, transcendentals=1 << 24),
        name="norm",
    )(lengths, totals, lanes, signal, above, below)
    total = pl.pallas_call(
        taps_kernel,
        out_shape=jax.ShapeDtypeStruct((SPANS, frames, row_count * col_count, OUT), jnp.float32),
        in_specs=[on_chip] * 5,
        out_specs=on_chip,
        scratch_shapes=[pltpu.VMEM((taps + 1, PART, OUT), jnp.bfloat16)],
        compiler_params=params,
        cost_estimate=pl.CostEstimate(
            flops=2 * 28 * 1024 * 128 * 256, bytes_accessed=6 << 20, transcendentals=0
        ),
        name="taps",
    )(shifted, raw, mine, theirs, factor)

    total = total.astype(jnp.float16)
    total = lax.all_to_all(total, TM, 0, 0, tiled=True).astype(jnp.float32)
    total = jnp.sum(total.reshape((chips, videos) + total.shape[1:]), axis=0)
    total = total / factor[:, None, None, :]
    total = total.reshape(videos, frames, row_count, col_count, OUT)
    stamps = span * frames + jnp.arange(frames, dtype=jnp.int32)
    present = stamps[None, :] < lengths[:, None]
    return jnp.where(present[:, :, None, None, None], total, 0.0).astype(jnp.bfloat16)


def solution(mesh):
    spans, tiles = mesh.devices.shape
    fine = Mesh(mesh.devices.reshape(spans // 2, 2, 8, tiles // 8), TM + TILE)
    placed = (
        P(None, TM, TILE, None, None),
        P(),
        P(),
        P(),
        P(TILE, None, None),
        P(TILE, None),
    )
    return jax.shard_map(
        per_device,
        mesh=fine,
        in_specs=placed,
        out_specs=P(None, TM, TILE, None, None),
        check_vma=False,
    )
```

```python
import functools

import jax
import jax.numpy as jnp
from jax import lax
from jax.experimental import pallas as pl
from jax.experimental.pallas import tpu as pltpu
from jax.sharding import Mesh
from jax.sharding import PartitionSpec as P

GROUPS = 32
EPS = 1e-06
TM = ("x", "core")
TILE = ("y", "z")
SPANS = 8
VIDEOS = 2
FRAMES = 4
COLS = 16
SHARE = 64
CHIPS = 4
PART = 2 * SHARE
ROWS = 4
LINE = 15
OUT = 256


def to_all(block, axis):
    count = lax.axis_size(axis)
    copies = jnp.broadcast_to(block[None], (count,) + block.shape)
    return lax.all_to_all(copies, axis, 0, 0, tiled=True)


def exact_dot(value, chosen):
    high = value.astype(jnp.bfloat16)
    rest = value - high.astype(jnp.float32)
    middle = rest.astype(jnp.bfloat16)
    low = (rest - middle.astype(jnp.float32)).astype(jnp.bfloat16)
    total = jnp.dot(low, chosen, preferred_element_type=jnp.float32)
    total = total + jnp.dot(middle, chosen, preferred_element_type=jnp.float32)
    return total + jnp.dot(high, chosen, preferred_element_type=jnp.float32)


def payload_kernel(features, conv, skip, lengths, copies, planes, taps, skips, valid, rows, packed, few, done, left):
    moves = [
        pltpu.make_async_copy(source, target, done.at[index])
        for index, (source, target) in enumerate(
            ((features, planes), (conv, taps), (skip, skips), (lengths, valid))
        )
    ]
    for move in moves:
        move.start()
    for move in moves:
        move.wait()
    count, channels = taps.shape[0], planes.shape[-1]
    span = lax.axis_index(TM)
    pick = lax.broadcasted_iota(jnp.int32, (count, SPANS, OUT), 1) == span
    rows[...] = jnp.zeros_like(rows)
    rows[0:count, :] = jnp.sum(jnp.where(pick, taps[...].astype(jnp.float32), 0.0), axis=1)
    pick = lax.broadcasted_iota(jnp.int32, (SPANS, OUT), 0) == span
    rows[count : count + 1, :] = jnp.sum(
        jnp.where(pick, skips[...].astype(jnp.float32), 0.0), axis=0, keepdims=True
    )
    lines = []
    for video in range(VIDEOS):
        linear = jnp.zeros((1, channels), jnp.float32)
        square = jnp.zeros((1, channels), jnp.float32)
        for frame in range(FRAMES):
            block = planes[video * FRAMES + frame].astype(jnp.float32)
            shown = (span * FRAMES + frame < valid[video]).astype(jnp.float32)
            linear += jnp.sum(block, axis=0, keepdims=True) * shown
            square += jnp.sum(block * block, axis=0, keepdims=True) * shown
        lines += [(video, linear), (VIDEOS + video, square)]
    lines = jnp.concatenate([line for _, line in sorted(lines, key=lambda pair: pair[0])], axis=0)
    group = lax.broadcasted_iota(jnp.int32, (channels, 128), 0) // (channels // GROUPS)
    lane = lax.broadcasted_iota(jnp.int32, (channels, 128), 1)
    spots = exact_dot(lines, (lane % GROUPS == group).astype(jnp.bfloat16))
    line = lax.broadcasted_iota(jnp.int32, spots.shape, 0)
    lane = lax.broadcasted_iota(jnp.int32, spots.shape, 1)
    sums = jnp.sum(jnp.where(lane // GROUPS == line, spots, 0.0), axis=0, keepdims=True)
    high = sums.astype(jnp.bfloat16).astype(jnp.float32)
    middle = (sums - high).astype(jnp.bfloat16).astype(jnp.float32)
    rows[count + 1 : count + 2, 0:128] = high
    rows[count + 1 : count + 2, 128:256] = middle
    rows[count + 2 : count + 3, 0:128] = sums - high - middle
    for row in range(2 * LINE):
        at = row % LINE * OUT
        packed[row // LINE : row // LINE + 1, at : at + OUT] = rows[row : row + 1, :]
    value = packed[...].astype(jnp.bfloat16)
    some = few.shape[0]
    for index in range(some):
        few[index] = value
    moves = [
        pltpu.make_async_copy(few, copies.at[pl.ds(index * some, some)], left.at[index])
        for index in range(copies.shape[0] // some)
    ]
    for move in moves:
        move.start()
    for move in moves:
        move.wait()


def sums_kernel(arrived, copies, *, first):
    at = (first - LINE) * OUT
    line = jnp.sum(arrived[:, :, at : at + 2 * OUT].astype(jnp.float32), axis=0)[1:2]
    total = line[:, 256:384] + line[:, 128:256] + line[:, 0:128]
    copies[...] = jnp.broadcast_to(total[None], copies.shape)


def member_kernel(features, gain, bias, kept, sent, lanes):
    voxels, channels = features.shape[0] * COLS, features.shape[-1]
    column = lax.broadcasted_iota(jnp.int32, (channels, channels), 1)
    place = column % PART
    source = place % SHARE * SPANS + column // PART * 2 + place // SHARE
    match = lax.broadcasted_iota(jnp.int32, (channels, channels), 0) == source
    chosen = jnp.where(match, 1.0, 0.0).astype(jnp.bfloat16)
    even = lax.axis_index("core") == 0
    for row in range(2):
        block = features[:, row * COLS : (row + 1) * COLS].reshape(voxels, channels)
        flat = jnp.dot(block, chosen, preferred_element_type=jnp.float32).astype(jnp.bfloat16)
        flat = flat.reshape(VIDEOS, FRAMES, COLS, channels)
        mine, other = jnp.where(even, flat[0], flat[1]), jnp.where(even, flat[1], flat[0])
        at = slice(row * PART, (row + 1) * PART)
        for chip in range(CHIPS):
            kept[chip, :, :, at] = mine[..., chip * PART : (chip + 1) * PART]
            sent[chip, :, :, at] = other[..., chip * PART : (chip + 1) * PART]
    place = lax.broadcasted_iota(jnp.int32, (channels, PART), 1)
    source = place % SHARE * SPANS + lax.axis_index("x") * 2 + place // SHARE
    match = lax.broadcasted_iota(jnp.int32, (channels, PART), 0) == source
    pair = jnp.concatenate([gain[...], bias[...]], axis=0)
    lanes[...] = exact_dot(pair, jnp.where(match, 1.0, 0.0).astype(jnp.bfloat16))


def edges_kernel(*refs):
    signal, upper, lower = refs[-3:]
    for step, block in enumerate(refs[:-3]):
        value = block[...]
        signal[step] = value
        upper[step] = value[..., PART:]
        lower[step] = value[..., :PART]


def norm_kernel(
    lengths, totals, lanes, signal, above, below, shifted, raw, factor, moments,
    *, cells, tiles, tap_bound, skip_bound
):
    chip, core = lax.axis_index("x"), lax.axis_index("core")
    tile = lax.axis_index(TILE)
    summed = [totals[0:1, :]]
    for span in range(1, SPANS):
        summed.append(summed[-1] + totals[span : span + 1, :])
    summed = jnp.concatenate(summed, axis=0)
    entry = lax.broadcasted_iota(jnp.int32, (128, 4 * PART), 0)
    lane = lax.broadcasted_iota(jnp.int32, (128, 4 * PART), 1)
    wanted = lane // PART * GROUPS + lane % SHARE // 2
    spread = exact_dot(summed, jnp.where(entry == wanted, 1.0, 0.0).astype(jnp.bfloat16))
    ends = (lax.broadcasted_iota(jnp.int32, (SPANS, PART), 0) + 1) * FRAMES
    for video in range(VIDEOS):
        seen = jnp.minimum(ends, lengths[video]).astype(jnp.float32) * cells
        square = spread[:, (VIDEOS + video) * PART : (VIDEOS + video + 1) * PART]
        centre = spread[:, video * PART : (video + 1) * PART] / seen
        inverse = lax.rsqrt(square / seen - centre * centre + EPS)
        moments[2 * video] = centre
        moments[2 * video + 1] = 0.5 * inverse * lanes[0:1, :]
        size = jnp.sqrt(square)
        bound = tap_bound * (3.0 * jnp.max(size * inverse, keepdims=True) + 3.0)
        bound = bound + skip_bound * jnp.max(size, keepdims=True)
        bound = jnp.exp2(14.0 - jnp.floor(jnp.log2(bound)))
        factor[video : video + 1, :] = jnp.broadcast_to(bound, (1, OUT))
    half_bias = 0.5 * lanes[1:2, :]

    def normed(value, span):
        frame = lax.broadcasted_iota(jnp.int32, (FRAMES, 1, PART), 0) + span * FRAMES
        shown = frame < lengths[core]
        centre = moments[2 * core, pl.ds(span, 1)].reshape(1, 1, PART)
        scale = jnp.where(shown, moments[2 * core + 1, pl.ds(span, 1)].reshape(1, 1, PART), 0.0)
        offset = jnp.where(shown, half_bias.reshape(1, 1, PART), 0.0)
        value = (value.astype(jnp.float32) - centre) * scale + offset
        return value + value * jnp.tanh(value)

    for step in range(CHIPS):
        for other in range(2):
            span = lax.rem(chip - step + CHIPS, CHIPS) * 2 + lax.rem(core + other, 2)
            raw[pl.ds(span * FRAMES, FRAMES)] = signal[step, other]
            for row in range(ROWS):
                if row == 0:
                    value = jnp.where(tile == 0, signal[step, other, :, :, :PART], above[step, other])
                elif row == ROWS - 1:
                    value = jnp.where(
                        tile == tiles - 1, signal[step, other, :, :, PART:], below[step, other]
                    )
                else:
                    value = signal[step, other, :, :, (row - 1) * PART : row * PART]
                value = normed(value, span)
                left = jnp.concatenate([value[:, :1], value[:, :-1]], axis=1)
                right = jnp.concatenate([value[:, 1:], value[:, -1:]], axis=1)
                for side, part in enumerate((left, value, right)):
                    shifted[
                        side, pl.ds(2 + span * FRAMES, FRAMES), :, row * PART : (row + 1) * PART
                    ] = part.astype(jnp.bfloat16)
    for side in range(3):
        shifted[side, 0] = shifted[side, 2]
        shifted[side, 1] = shifted[side, 2]


def taps_kernel(shifted, raw, mine, theirs, factor, out, weights):
    core = lax.axis_index("core")
    count = weights.shape[0]
    for tap in range(count):
        line, at = tap // LINE, tap % LINE * OUT
        for place, half in ((core, mine), (1 - core, theirs)):
            rows = pl.ds(pl.multiple_of(place * SHARE, SHARE), SHARE)
            weights[tap, rows] = half[line, :, at : at + OUT]
    length = SPANS * FRAMES
    scale = jnp.where(core == 0, factor[0:1, :], factor[1:2, :])
    for row in range(2):
        total = None
        for pair in range(count // 2):
            blocks = []
            for tap in (2 * pair, 2 * pair + 1):
                if tap < count - 1:
                    at = (row + tap // 3 % 3) * PART
                    block = shifted[tap % 3, tap // 9 : tap // 9 + length, :, at : at + PART]
                else:
                    block = raw[..., row * PART : (row + 1) * PART]
                blocks.append(block.reshape(-1, PART))
            term = jnp.dot(
                jnp.concatenate(blocks, axis=1),
                weights[2 * pair : 2 * pair + 2].reshape(2 * PART, OUT),
                preferred_element_type=jnp.float32,
            )
            total = term if total is None else total + term
        total = (total * scale).reshape(SPANS, FRAMES, COLS, OUT)
        out[:, :, row * COLS : (row + 1) * COLS, :] = total


def per_device(features, lengths, gain_in, bias_in, conv_in, skip_weight):
    videos, frames, row_count, col_count, wide_in = features.shape
    span, chip = lax.axis_index(TM), lax.axis_index("x")
    tiles, chips = lax.axis_size(TILE), lax.axis_size("x")
    taps = conv_in.shape[1]
    on_chip = pl.BlockSpec(memory_space=pltpu.VMEM)
    outside = pl.BlockSpec(memory_space=pl.ANY)
    scalar = pl.BlockSpec(memory_space=pltpu.SMEM)
    params = pltpu.CompilerParams(vmem_limit_bytes=20 * 1024 * 1024)

    planes = features.reshape(videos * frames, row_count * col_count, wide_in)
    copies = pl.pallas_call(
        payload_kernel,
        out_shape=jax.ShapeDtypeStruct((tiles, 2, LINE * OUT), jnp.bfloat16),
        in_specs=[outside] * 4,
        out_specs=outside,
        scratch_shapes=[
            pltpu.VMEM(planes.shape, jnp.bfloat16),
            pltpu.VMEM((taps, SPANS, OUT), jnp.bfloat16),
            pltpu.VMEM((SPANS, OUT), jnp.bfloat16),
            pltpu.SMEM((videos,), jnp.int32),
            pltpu.VMEM((32, OUT), jnp.float32),
            pltpu.VMEM((2, LINE * OUT), jnp.float32),
            pltpu.VMEM((8, 2, LINE * OUT), jnp.bfloat16),
            pltpu.SemaphoreType.DMA((4,)),
            pltpu.SemaphoreType.DMA((tiles // 8,)),
        ],
        compiler_params=params,
        name="payload",
    )(
        *[
            pltpu.with_memory_space_constraint(value, pltpu.HBM)
            for value in (planes, conv_in.transpose(1, 0, 2), skip_weight, lengths)
        ]
    )
    arrived = lax.all_to_all(copies, TILE, 0, 0, tiled=True)

    shape = (chips, frames, col_count, 2 * PART)
    kept, sent, lanes = pl.pallas_call(
        member_kernel,
        out_shape=(
            jax.ShapeDtypeStruct(shape, jnp.bfloat16),
            jax.ShapeDtypeStruct(shape, jnp.bfloat16),
            jax.ShapeDtypeStruct((2, PART), jnp.float32),
        ),
        in_specs=[on_chip] * 3,
        out_specs=(on_chip, on_chip, on_chip),
        compiler_params=params,
        name="member_shares",
    )(planes, gain_in.reshape(1, -1), bias_in.reshape(1, -1))
    swap = [(0, 1), (1, 0)]
    shares = jnp.stack([kept, lax.ppermute(sent, "core", swap)], axis=1)
    signal = []
    for step in range(chips):
        block = lax.dynamic_index_in_dim(shares, lax.rem(chip + step, chips), 0, False)
        if step:
            block = lax.ppermute(block, "x", [(i, (i + step) % chips) for i in range(chips)])
        signal.append(block)
    whole = (chips,) + signal[0].shape
    edge = whole[:-1] + (PART,)
    signal, upper, lower = pl.pallas_call(
        edges_kernel,
        out_shape=tuple(pltpu.VMEM(shape, jnp.bfloat16) for shape in (whole, edge, edge)),
        in_specs=[on_chip] * chips,
        out_specs=(on_chip, on_chip, on_chip),
        compiler_params=params,
        name="edges",
    )(*signal)
    above = lax.ppermute(upper, TILE, [(i, i + 1) for i in range(tiles - 1)])
    below = lax.ppermute(lower, TILE, [(i + 1, i) for i in range(tiles - 1)])

    held, upper, lower = lax.optimization_barrier((arrived, upper, lower))
    copies = pl.pallas_call(
        functools.partial(sums_kernel, first=taps + 1),
        out_shape=jax.ShapeDtypeStruct((SPANS, 1, 128), jnp.float32),
        in_specs=[on_chip],
        out_specs=on_chip,
        compiler_params=params,
        name="sums",
    )(pltpu.with_memory_space_constraint(held, pltpu.VMEM))
    totals = lax.all_to_all(copies, TM, 0, 0, tiled=True).reshape(SPANS, -1)
    mine = arrived.transpose(1, 0, 2)
    theirs = lax.ppermute(mine, "core", swap)

    shifted, raw, factor = pl.pallas_call(
        functools.partial(
            norm_kernel,
            cells=float(row_count * tiles * col_count * (wide_in // GROUPS)),
            tiles=tiles,
            tap_bound=float(taps * PART) * 0.0546875,
            skip_bound=float(PART) * 0.25,
        ),
        out_shape=(
            jax.ShapeDtypeStruct((3, SPANS * frames + 2, col_count, ROWS * PART), jnp.bfloat16),
            jax.ShapeDtypeStruct((SPANS * frames, col_count, 2 * PART), jnp.bfloat16),
            jax.ShapeDtypeStruct((videos, OUT), jnp.float32),
        ),
        in_specs=[scalar] + [on_chip] * 5,
        out_specs=(on_chip, on_chip, on_chip),
        scratch_shapes=[pltpu.VMEM((2 * videos, SPANS, PART), jnp.float32)],
        compiler_params=params,
        cost_estimate=pl.CostEstimate(flops=1 << 34, bytes_accessed=1 << 26, transcendentals=1 << 24),
        name="norm",
    )(lengths, totals, lanes, signal, above, below)
    total = pl.pallas_call(
        taps_kernel,
        out_shape=jax.ShapeDtypeStruct((SPANS, frames, row_count * col_count, OUT), jnp.float32),
        in_specs=[on_chip] * 5,
        out_specs=on_chip,
        scratch_shapes=[pltpu.VMEM((taps + 1, PART, OUT), jnp.bfloat16)],
        compiler_params=params,
        cost_estimate=pl.CostEstimate(
            flops=2 * 28 * 1024 * 128 * 256, bytes_accessed=6 << 20, transcendentals=0
        ),
        name="taps",
    )(shifted, raw, mine, theirs, factor)

    total = total.astype(jnp.float16)
    total = lax.all_to_all(total, TM, 0, 0, tiled=True).astype(jnp.float32)
    total = jnp.sum(total.reshape((chips, videos) + total.shape[1:]), axis=0)
    total = total / factor[:, None, None, :]
    total = total.reshape(videos, frames, row_count, col_count, OUT)
    stamps = span * frames + jnp.arange(frames, dtype=jnp.int32)
    present = stamps[None, :] < lengths[:, None]
    return jnp.where(present[:, :, None, None, None], total, 0.0).astype(jnp.bfloat16)


def solution(mesh):
    spans, tiles = mesh.devices.shape
    fine = Mesh(mesh.devices.reshape(spans // 2, 2, 8, tiles // 8), TM + TILE)
    placed = (
        P(None, TM, TILE, None, None),
        P(),
        P(),
        P(),
        P(TILE, None, None),
        P(TILE, None),
    )
    return jax.shard_map(
        per_device,
        mesh=fine,
        in_specs=placed,
        out_specs=P(None, TM, TILE, None, None),
        check_vma=False,
    )
```

```python
import functools

import jax
import jax.numpy as jnp
from jax import lax
from jax.experimental import pallas as pl
from jax.experimental.pallas import tpu as pltpu
from jax.sharding import Mesh
from jax.sharding import PartitionSpec as P

GROUPS = 32
EPS = 1e-06
TM = ("x", "core")
TILE = ("y", "z")
SPANS = 8
VIDEOS = 2
FRAMES = 4
COLS = 16
SHARE = 64
CHIPS = 4
PART = 2 * SHARE
ROWS = 4
LINE = 15
OUT = 256


def to_all(block, axis):
    count = lax.axis_size(axis)
    copies = jnp.broadcast_to(block[None], (count,) + block.shape)
    return lax.all_to_all(copies, axis, 0, 0, tiled=True)


def exact_dot(value, chosen):
    high = value.astype(jnp.bfloat16)
    rest = value - high.astype(jnp.float32)
    middle = rest.astype(jnp.bfloat16)
    low = (rest - middle.astype(jnp.float32)).astype(jnp.bfloat16)
    total = jnp.dot(low, chosen, preferred_element_type=jnp.float32)
    total = total + jnp.dot(middle, chosen, preferred_element_type=jnp.float32)
    return total + jnp.dot(high, chosen, preferred_element_type=jnp.float32)


def payload_kernel(features, conv, skip, lengths, copies, planes, taps, skips, valid, rows, packed, few, done, left):
    moves = [
        pltpu.make_async_copy(source, target, done.at[index])
        for index, (source, target) in enumerate(
            ((features, planes), (conv, taps), (skip, skips), (lengths, valid))
        )
    ]
    for move in moves:
        move.start()
    for move in moves[1:]:
        move.wait()
    count, channels = taps.shape[0], planes.shape[-1]
    span = lax.axis_index(TM)
    pick = lax.broadcasted_iota(jnp.int32, (count, SPANS, OUT), 1) == span
    rows[...] = jnp.zeros_like(rows)
    rows[0:count, :] = jnp.sum(jnp.where(pick, taps[...].astype(jnp.float32), 0.0), axis=1)
    pick = lax.broadcasted_iota(jnp.int32, (SPANS, OUT), 0) == span
    rows[count : count + 1, :] = jnp.sum(
        jnp.where(pick, skips[...].astype(jnp.float32), 0.0), axis=0, keepdims=True
    )
    moves[0].wait()
    lines = []
    for video in range(VIDEOS):
        linear = jnp.zeros((1, channels), jnp.float32)
        square = jnp.zeros((1, channels), jnp.float32)
        for frame in range(FRAMES):
            block = planes[video * FRAMES + frame].astype(jnp.float32)
            shown = (span * FRAMES + frame < valid[video]).astype(jnp.float32)
            linear += jnp.sum(block, axis=0, keepdims=True) * shown
            square += jnp.sum(block * block, axis=0, keepdims=True) * shown
        lines += [(video, linear), (VIDEOS + video, square)]
    lines = jnp.concatenate([line for _, line in sorted(lines, key=lambda pair: pair[0])], axis=0)
    group = lax.broadcasted_iota(jnp.int32, (channels, 128), 0) // (channels // GROUPS)
    lane = lax.broadcasted_iota(jnp.int32, (channels, 128), 1)
    spots = exact_dot(lines, (lane % GROUPS == group).astype(jnp.bfloat16))
    line = lax.broadcasted_iota(jnp.int32, spots.shape, 0)
    lane = lax.broadcasted_iota(jnp.int32, spots.shape, 1)
    sums = jnp.sum(jnp.where(lane // GROUPS == line, spots, 0.0), axis=0, keepdims=True)
    high = sums.astype(jnp.bfloat16).astype(jnp.float32)
    middle = (sums - high).astype(jnp.bfloat16).astype(jnp.float32)
    rows[count + 1 : count + 2, 0:128] = high
    rows[count + 1 : count + 2, 128:256] = middle
    rows[count + 2 : count + 3, 0:128] = sums - high - middle
    for row in range(2 * LINE):
        at = row % LINE * OUT
        packed[row // LINE : row // LINE + 1, at : at + OUT] = rows[row : row + 1, :]
    value = packed[0:2, :].astype(jnp.bfloat16)
    some = few.shape[0]
    for index in range(some):
        few[index] = value
    moves = [
        pltpu.make_async_copy(few, copies.at[pl.ds(index * some, some)], left.at[index])
        for index in range(copies.shape[0] // some)
    ]
    for move in moves:
        move.start()
    for move in moves:
        move.wait()


def sums_kernel(arrived, copies, *, first):
    at = (first - LINE) * OUT
    line = jnp.sum(arrived[:, :, at : at + 2 * OUT].astype(jnp.float32), axis=0)[1:2]
    total = line[:, 256:384] + line[:, 128:256] + line[:, 0:128]
    copies[...] = jnp.broadcast_to(total[None], copies.shape)


def member_kernel(features, gain, bias, kept, sent, lanes):
    voxels, channels = features.shape[0] * COLS, features.shape[-1]
    column = lax.broadcasted_iota(jnp.int32, (channels, channels), 1)
    place = column % PART
    source = place % SHARE * SPANS + column // PART * 2 + place // SHARE
    match = lax.broadcasted_iota(jnp.int32, (channels, channels), 0) == source
    chosen = jnp.where(match, 1.0, 0.0).astype(jnp.bfloat16)
    even = lax.axis_index("core") == 0
    for row in range(2):
        block = features[:, row * COLS : (row + 1) * COLS].reshape(voxels, channels)
        flat = jnp.dot(block, chosen, preferred_element_type=jnp.float32).astype(jnp.bfloat16)
        flat = flat.reshape(VIDEOS, FRAMES, COLS, channels)
        mine, other = jnp.where(even, flat[0], flat[1]), jnp.where(even, flat[1], flat[0])
        at = slice(row * PART, (row + 1) * PART)
        for chip in range(CHIPS):
            kept[chip, :, :, at] = mine[..., chip * PART : (chip + 1) * PART]
            sent[chip, :, :, at] = other[..., chip * PART : (chip + 1) * PART]
    place = lax.broadcasted_iota(jnp.int32, (channels, PART), 1)
    source = place % SHARE * SPANS + lax.axis_index("x") * 2 + place // SHARE
    match = lax.broadcasted_iota(jnp.int32, (channels, PART), 0) == source
    pair = jnp.concatenate([gain[...], bias[...]], axis=0)
    lanes[...] = exact_dot(pair, jnp.where(match, 1.0, 0.0).astype(jnp.bfloat16))


def edges_kernel(*refs):
    signal, upper, lower = refs[-3:]
    for step, block in enumerate(refs[:-3]):
        value = block[...]
        signal[step] = value
        upper[step] = value[..., PART:]
        lower[step] = value[..., :PART]


def norm_kernel(
    lengths, totals, lanes, signal, above, below, shifted, raw, factor, moments,
    *, cells, tiles, tap_bound, skip_bound
):
    chip, core = lax.axis_index("x"), lax.axis_index("core")
    tile = lax.axis_index(TILE)
    summed = [totals[0:1, :]]
    for span in range(1, SPANS):
        summed.append(summed[-1] + totals[span : span + 1, :])
    summed = jnp.concatenate(summed, axis=0)
    entry = lax.broadcasted_iota(jnp.int32, (128, 4 * PART), 0)
    lane = lax.broadcasted_iota(jnp.int32, (128, 4 * PART), 1)
    wanted = lane // PART * GROUPS + lane % SHARE // 2
    spread = exact_dot(summed, jnp.where(entry == wanted, 1.0, 0.0).astype(jnp.bfloat16))
    ends = (lax.broadcasted_iota(jnp.int32, (SPANS, PART), 0) + 1) * FRAMES
    for video in range(VIDEOS):
        seen = jnp.minimum(ends, lengths[video]).astype(jnp.float32) * cells
        square = spread[:, (VIDEOS + video) * PART : (VIDEOS + video + 1) * PART]
        centre = spread[:, video * PART : (video + 1) * PART] / seen
        inverse = lax.rsqrt(square / seen - centre * centre + EPS)
        moments[2 * video] = centre
        moments[2 * video + 1] = 0.5 * inverse * lanes[0:1, :]
        size = jnp.sqrt(square)
        ratio = size * inverse
        ratio = jnp.where(ratio < 1e30, ratio, 0.0)
        bound = tap_bound * (3.0 * jnp.max(ratio, keepdims=True) + 3.0)
        bound = bound + skip_bound * jnp.max(size, keepdims=True)
        bound = jnp.exp2(14.0 - jnp.floor(jnp.log2(bound)))
        factor[video : video + 1, :] = jnp.broadcast_to(bound, (1, OUT))
    half_bias = 0.5 * lanes[1:2, :]

    def normed(value, span):
        frame = lax.broadcasted_iota(jnp.int32, (FRAMES, 1, PART), 0) + span * FRAMES
        shown = frame < lengths[core]
        centre = moments[2 * core, pl.ds(span, 1)].reshape(1, 1, PART)
        scale = jnp.where(shown, moments[2 * core + 1, pl.ds(span, 1)].reshape(1, 1, PART), 0.0)
        offset = jnp.where(shown, half_bias.reshape(1, 1, PART), 0.0)
        value = (value.astype(jnp.float32) - centre) * scale + offset
        return value + value * jnp.tanh(value)

    for step in range(CHIPS):
        for other in range(2):
            span = lax.rem(chip - step + CHIPS, CHIPS) * 2 + lax.rem(core + other, 2)
            raw[pl.ds(span * FRAMES, FRAMES)] = signal[step, other]
            for row in range(ROWS):
                if row == 0:
                    value = jnp.where(tile == 0, signal[step, other, :, :, :PART], above[step, other])
                elif row == ROWS - 1:
                    value = jnp.where(
                        tile == tiles - 1, signal[step, other, :, :, PART:], below[step, other]
                    )
                else:
                    value = signal[step, other, :, :, (row - 1) * PART : row * PART]
                value = normed(value, span)
                left = jnp.concatenate([value[:, :1], value[:, :-1]], axis=1)
                right = jnp.concatenate([value[:, 1:], value[:, -1:]], axis=1)
                for side, part in enumerate((left, value, right)):
                    shifted[
                        side, pl.ds(2 + span * FRAMES, FRAMES), :, row * PART : (row + 1) * PART
                    ] = part.astype(jnp.bfloat16)
    for side in range(3):
        shifted[side, 0] = shifted[side, 2]
        shifted[side, 1] = shifted[side, 2]


def taps_kernel(shifted, raw, mine, theirs, factor, out, weights):
    core = lax.axis_index("core")
    count = weights.shape[0]
    for tap in range(count):
        line, at = tap // LINE, tap % LINE * OUT
        for place, half in ((core, mine), (1 - core, theirs)):
            rows = pl.ds(pl.multiple_of(place * SHARE, SHARE), SHARE)
            weights[tap, rows] = half[line, :, at : at + OUT]
    length = SPANS * FRAMES
    scale = jnp.where(core == 0, factor[0:1, :], factor[1:2, :])
    for row in range(2):
        total = None
        for pair in range(count // 2):
            blocks = []
            for tap in (2 * pair, 2 * pair + 1):
                if tap < count - 1:
                    at = (row + tap // 3 % 3) * PART
                    block = shifted[tap % 3, tap // 9 : tap // 9 + length, :, at : at + PART]
                else:
                    block = raw[..., row * PART : (row + 1) * PART]
                blocks.append(block.reshape(-1, PART))
            term = jnp.dot(
                jnp.concatenate(blocks, axis=1),
                weights[2 * pair : 2 * pair + 2].reshape(2 * PART, OUT),
                preferred_element_type=jnp.float32,
            )
            total = term if total is None else total + term
        total = (total * scale).reshape(SPANS, FRAMES, COLS, OUT)
        out[:, :, row * COLS : (row + 1) * COLS, :] = total


def per_device(features, lengths, gain_in, bias_in, conv_in, skip_weight):
    videos, frames, row_count, col_count, wide_in = features.shape
    span, chip = lax.axis_index(TM), lax.axis_index("x")
    tiles, chips = lax.axis_size(TILE), lax.axis_size("x")
    taps = conv_in.shape[1]
    on_chip = pl.BlockSpec(memory_space=pltpu.VMEM)
    outside = pl.BlockSpec(memory_space=pl.ANY)
    scalar = pl.BlockSpec(memory_space=pltpu.SMEM)
    params = pltpu.CompilerParams(vmem_limit_bytes=20 * 1024 * 1024)

    planes = features.reshape(videos * frames, row_count * col_count, wide_in)
    copies = pl.pallas_call(
        payload_kernel,
        out_shape=jax.ShapeDtypeStruct((tiles, 2, LINE * OUT), jnp.bfloat16),
        in_specs=[outside] * 4,
        out_specs=outside,
        scratch_shapes=[
            pltpu.VMEM(planes.shape, jnp.bfloat16),
            pltpu.VMEM((taps, SPANS, OUT), jnp.bfloat16),
            pltpu.VMEM((SPANS, OUT), jnp.bfloat16),
            pltpu.SMEM((videos,), jnp.int32),
            pltpu.VMEM((32, OUT), jnp.float32),
            pltpu.VMEM((8, LINE * OUT), jnp.float32),
            pltpu.VMEM((8, 2, LINE * OUT), jnp.bfloat16),
            pltpu.SemaphoreType.DMA((4,)),
            pltpu.SemaphoreType.DMA((tiles // 8,)),
        ],
        compiler_params=params,
        name="payload",
    )(
        *[
            pltpu.with_memory_space_constraint(value, pltpu.HBM)
            for value in (planes, conv_in.transpose(1, 0, 2), skip_weight, lengths)
        ]
    )
    arrived = lax.all_to_all(copies, TILE, 0, 0, tiled=True)

    shape = (chips, frames, col_count, 2 * PART)
    kept, sent, lanes = pl.pallas_call(
        member_kernel,
        out_shape=(
            jax.ShapeDtypeStruct(shape, jnp.bfloat16),
            jax.ShapeDtypeStruct(shape, jnp.bfloat16),
            jax.ShapeDtypeStruct((2, PART), jnp.float32),
        ),
        in_specs=[on_chip] * 3,
        out_specs=(on_chip, on_chip, on_chip),
        compiler_params=params,
        name="member_shares",
    )(planes, gain_in.reshape(1, -1), bias_in.reshape(1, -1))
    swap = [(0, 1), (1, 0)]
    shares = jnp.stack([kept, lax.ppermute(sent, "core", swap)], axis=1)
    signal = []
    for step in range(chips):
        block = lax.dynamic_index_in_dim(shares, lax.rem(chip + step, chips), 0, False)
        if step:
            block = lax.ppermute(block, "x", [(i, (i + step) % chips) for i in range(chips)])
        signal.append(block)
    whole = (chips,) + signal[0].shape
    edge = whole[:-1] + (PART,)
    signal, upper, lower = pl.pallas_call(
        edges_kernel,
        out_shape=tuple(pltpu.VMEM(shape, jnp.bfloat16) for shape in (whole, edge, edge)),
        in_specs=[on_chip] * chips,
        out_specs=(on_chip, on_chip, on_chip),
        compiler_params=params,
        name="edges",
    )(*signal)
    above = lax.ppermute(upper, TILE, [(i, i + 1) for i in range(tiles - 1)])
    below = lax.ppermute(lower, TILE, [(i + 1, i) for i in range(tiles - 1)])

    held, upper, lower = lax.optimization_barrier((arrived, upper, lower))
    copies = pl.pallas_call(
        functools.partial(sums_kernel, first=taps + 1),
        out_shape=jax.ShapeDtypeStruct((SPANS, 1, 128), jnp.float32),
        in_specs=[on_chip],
        out_specs=on_chip,
        compiler_params=params,
        name="sums",
    )(pltpu.with_memory_space_constraint(held, pltpu.VMEM))
    totals = lax.all_to_all(copies, TM, 0, 0, tiled=True).reshape(SPANS, -1)
    mine = arrived.transpose(1, 0, 2)
    theirs = lax.ppermute(mine, "core", swap)

    shifted, raw, factor = pl.pallas_call(
        functools.partial(
            norm_kernel,
            cells=float(row_count * tiles * col_count * (wide_in // GROUPS)),
            tiles=tiles,
            tap_bound=float(taps * PART) * 0.0546875,
            skip_bound=float(PART) * 0.25,
        ),
        out_shape=(
            jax.ShapeDtypeStruct((3, SPANS * frames + 2, col_count, ROWS * PART), jnp.bfloat16),
            jax.ShapeDtypeStruct((SPANS * frames, col_count, 2 * PART), jnp.bfloat16),
            jax.ShapeDtypeStruct((videos, OUT), jnp.float32),
        ),
        in_specs=[scalar] + [on_chip] * 5,
        out_specs=(on_chip, on_chip, on_chip),
        scratch_shapes=[pltpu.VMEM((2 * videos + 1, SPANS, PART), jnp.float32)],
        compiler_params=params,
        cost_estimate=pl.CostEstimate(flops=1 << 34, bytes_accessed=1 << 26, transcendentals=1 << 24),
        name="norm",
    )(lengths, totals, lanes, signal, above, below)
    total = pl.pallas_call(
        taps_kernel,
        out_shape=jax.ShapeDtypeStruct((SPANS, frames, row_count * col_count, OUT), jnp.float32),
        in_specs=[on_chip] * 5,
        out_specs=on_chip,
        scratch_shapes=[pltpu.VMEM((taps + 1, PART, OUT), jnp.bfloat16)],
        compiler_params=params,
        cost_estimate=pl.CostEstimate(
            flops=2 * 28 * 1024 * 128 * 256, bytes_accessed=6 << 20, transcendentals=0
        ),
        name="taps",
    )(shifted, raw, mine, theirs, factor)

    total = total.astype(jnp.float16)
    total = lax.all_to_all(total, TM, 0, 0, tiled=True).astype(jnp.float32)
    total = jnp.sum(total.reshape((chips, videos) + total.shape[1:]), axis=0)
    total = total / factor[:, None, None, :]
    total = total.reshape(videos, frames, row_count, col_count, OUT)
    stamps = span * frames + jnp.arange(frames, dtype=jnp.int32)
    present = stamps[None, :] < lengths[:, None]
    return jnp.where(present[:, :, None, None, None], total, 0.0).astype(jnp.bfloat16)


def solution(mesh):
    spans, tiles = mesh.devices.shape
    fine = Mesh(mesh.devices.reshape(spans // 2, 2, 8, tiles // 8), TM + TILE)
    placed = (
        P(None, TM, TILE, None, None),
        P(),
        P(),
        P(),
        P(TILE, None, None),
        P(TILE, None),
    )
    return jax.shard_map(
        per_device,
        mesh=fine,
        in_specs=placed,
        out_specs=P(None, TM, TILE, None, None),
        check_vma=False,
    )
```

```python
import functools

import jax
import jax.numpy as jnp
from jax import lax
from jax.experimental import pallas as pl
from jax.experimental.pallas import tpu as pltpu
from jax.sharding import Mesh
from jax.sharding import PartitionSpec as P

GROUPS = 32
EPS = 1e-06
TM = ("x", "core")
TILE = ("y", "z")
SPANS = 8
VIDEOS = 2
FRAMES = 4
COLS = 16
SHARE = 64
CHIPS = 4
PART = 2 * SHARE
ROWS = 4
LINE = 14
OUT = 256
WIDTH = LINE * OUT + 128


def to_all(block, axis):
    count = lax.axis_size(axis)
    copies = jnp.broadcast_to(block[None], (count,) + block.shape)
    return lax.all_to_all(copies, axis, 0, 0, tiled=True)


def exact_dot(value, chosen):
    high = value.astype(jnp.bfloat16)
    rest = value - high.astype(jnp.float32)
    middle = rest.astype(jnp.bfloat16)
    low = (rest - middle.astype(jnp.float32)).astype(jnp.bfloat16)
    total = jnp.dot(low, chosen, preferred_element_type=jnp.float32)
    total = total + jnp.dot(middle, chosen, preferred_element_type=jnp.float32)
    return total + jnp.dot(high, chosen, preferred_element_type=jnp.float32)


def own_counts(lengths, span):
    lane = lax.broadcasted_iota(jnp.int32, (1, 128), 1)
    count = jnp.where(lane % (2 * GROUPS) < GROUPS, lengths[0], lengths[1]) - span * FRAMES
    count = jnp.clip(count, 1, FRAMES).astype(jnp.float32)
    return 1.0 / (count * float(2 * COLS * SPANS * SHARE // GROUPS))


def own_square(value, inverse):
    axis = value.ndim - 1
    turned = pltpu.roll(value, 2 * GROUPS, axis)
    upper = lax.broadcasted_iota(jnp.int32, (1,) * axis + (128,), axis) >= 2 * GROUPS
    return jnp.where(upper, turned * turned * inverse, 0.0)


def payload_kernel(features, conv, skip, lengths, copies, counts, planes, taps, skips, valid, rows, packed, few, done, left):
    moves = [
        pltpu.make_async_copy(source, target, done.at[index])
        for index, (source, target) in enumerate(
            ((features, planes), (conv, taps), (skip, skips), (lengths, valid))
        )
    ]
    for move in moves:
        move.start()
    for move in moves[1:]:
        move.wait()
    count, channels = taps.shape[0], planes.shape[-1]
    span = lax.axis_index(TM)
    pick = lax.broadcasted_iota(jnp.int32, (count, SPANS, OUT), 1) == span
    rows[...] = jnp.zeros_like(rows)
    rows[0:count, :] = jnp.sum(jnp.where(pick, taps[...].astype(jnp.float32), 0.0), axis=1)
    pick = lax.broadcasted_iota(jnp.int32, (SPANS, OUT), 0) == span
    rows[count : count + 1, :] = jnp.sum(
        jnp.where(pick, skips[...].astype(jnp.float32), 0.0), axis=0, keepdims=True
    )
    moves[0].wait()
    lines = []
    for video in range(VIDEOS):
        linear = jnp.zeros((1, channels), jnp.float32)
        square = jnp.zeros((1, channels), jnp.float32)
        for frame in range(FRAMES):
            block = planes[video * FRAMES + frame].astype(jnp.float32)
            shown = (span * FRAMES + frame < valid[video]).astype(jnp.float32)
            linear += jnp.sum(block, axis=0, keepdims=True) * shown
            square += jnp.sum(block * block, axis=0, keepdims=True) * shown
        lines += [(video, linear), (VIDEOS + video, square)]
    lines = jnp.concatenate([line for _, line in sorted(lines, key=lambda pair: pair[0])], axis=0)
    group = lax.broadcasted_iota(jnp.int32, (channels, 128), 0) // (channels // GROUPS)
    lane = lax.broadcasted_iota(jnp.int32, (channels, 128), 1)
    spots = exact_dot(lines, (lane % GROUPS == group).astype(jnp.bfloat16))
    line = lax.broadcasted_iota(jnp.int32, spots.shape, 0)
    lane = lax.broadcasted_iota(jnp.int32, spots.shape, 1)
    sums = jnp.sum(jnp.where(lane // GROUPS == line, spots, 0.0), axis=0, keepdims=True)
    sums = jnp.broadcast_to(sums, (8, 128))
    inverse = own_counts(valid, span)
    sums = sums - own_square(sums, inverse)
    counts[...] = jnp.concatenate(
        [jnp.full((1, 128), valid[video]).astype(jnp.float32) for video in range(VIDEOS)]
        + [inverse, jnp.zeros((5, 128), jnp.float32)],
        axis=0,
    )
    high = sums.astype(jnp.bfloat16).astype(jnp.float32)
    for line, value in enumerate((high, sums - high)):
        packed[line : line + 1, LINE * OUT : WIDTH] = value[0:1]
    for row in range(2 * LINE):
        at = row % LINE * OUT
        packed[row // LINE : row // LINE + 1, at : at + OUT] = rows[row : row + 1, :]
    value = packed[0:2, :].astype(jnp.bfloat16)
    some = few.shape[0]
    for index in range(some):
        few[index] = value
    moves = [
        pltpu.make_async_copy(few, copies.at[pl.ds(index * some, some)], left.at[index])
        for index in range(copies.shape[0] // some)
    ]
    for move in moves:
        move.start()
    for move in moves:
        move.wait()


def sums_kernel(counts, arrived, copies):
    value = arrived[:, 0:1, LINE * OUT : WIDTH].astype(jnp.float32)
    value = value + arrived[:, 1:2, LINE * OUT : WIDTH].astype(jnp.float32)
    value = value + own_square(value, counts[2:3, :].reshape(1, 1, 128))
    total = jnp.sum(value, axis=0, keepdims=True)
    copies[...] = jnp.broadcast_to(total, copies.shape)


def member_kernel(features, gain, bias, kept, sent, lanes):
    voxels, channels = features.shape[0] * COLS, features.shape[-1]
    column = lax.broadcasted_iota(jnp.int32, (channels, channels), 1)
    place = column % PART
    source = place % SHARE * SPANS + column // PART * 2 + place // SHARE
    match = lax.broadcasted_iota(jnp.int32, (channels, channels), 0) == source
    chosen = jnp.where(match, 1.0, 0.0).astype(jnp.bfloat16)
    even = lax.axis_index("core") == 0
    for row in range(2):
        block = features[:, row * COLS : (row + 1) * COLS].reshape(voxels, channels)
        flat = jnp.dot(block, chosen, preferred_element_type=jnp.float32).astype(jnp.bfloat16)
        flat = flat.reshape(VIDEOS, FRAMES, COLS, channels)
        mine, other = jnp.where(even, flat[0], flat[1]), jnp.where(even, flat[1], flat[0])
        at = slice(row * PART, (row + 1) * PART)
        for chip in range(CHIPS):
            kept[chip, :, :, at] = mine[..., chip * PART : (chip + 1) * PART]
            sent[chip, :, :, at] = other[..., chip * PART : (chip + 1) * PART]
    place = lax.broadcasted_iota(jnp.int32, (channels, PART), 1)
    source = place % SHARE * SPANS + lax.axis_index("x") * 2 + place // SHARE
    match = lax.broadcasted_iota(jnp.int32, (channels, PART), 0) == source
    pair = jnp.concatenate([gain[...], bias[...]], axis=0)
    lanes[...] = exact_dot(pair, jnp.where(match, 1.0, 0.0).astype(jnp.bfloat16))


def edges_kernel(*refs):
    signal, upper, lower = refs[-3:]
    for step, block in enumerate(refs[:-3]):
        value = block[...]
        signal[step] = value
        upper[step] = value[..., PART:]
        lower[step] = value[..., :PART]


def norm_kernel(
    totals, counts, lanes, signal, above, below, shifted, raw, factor, moments,
    *, cells, tiles, tap_bound, skip_bound
):
    chip, core = lax.axis_index("x"), lax.axis_index("core")
    tile = lax.axis_index(TILE)
    summed = [totals[0:1, :]]
    for span in range(1, SPANS):
        summed.append(summed[-1] + totals[span : span + 1, :])
    summed = jnp.concatenate(summed, axis=0)
    entry = lax.broadcasted_iota(jnp.int32, (128, 4 * PART), 0)
    lane = lax.broadcasted_iota(jnp.int32, (128, 4 * PART), 1)
    wanted = lane // PART * GROUPS + lane % SHARE // 2
    spread = exact_dot(summed, jnp.where(entry == wanted, 1.0, 0.0).astype(jnp.bfloat16))
    ends = ((lax.broadcasted_iota(jnp.int32, (SPANS, PART), 0) + 1) * FRAMES).astype(jnp.float32)
    for video in range(VIDEOS):
        seen = jnp.minimum(ends, counts[video : video + 1, :]) * cells
        square = spread[:, (VIDEOS + video) * PART : (VIDEOS + video + 1) * PART]
        centre = spread[:, video * PART : (video + 1) * PART] / seen
        inverse = lax.rsqrt(square / seen - centre * centre + EPS)
        moments[2 * video] = centre
        moments[2 * video + 1] = 0.5 * inverse * lanes[0:1, :]
        size = jnp.sqrt(square)
        ratio = size * inverse
        ratio = jnp.where(ratio < 1e30, ratio, 0.0)
        bound = tap_bound * (3.0 * jnp.max(ratio, keepdims=True) + 3.0)
        bound = bound + skip_bound * jnp.max(size, keepdims=True)
        bound = jnp.exp2(14.0 - jnp.floor(jnp.log2(bound)))
        factor[video : video + 1, :] = jnp.broadcast_to(bound, (1, OUT))
    half_bias = 0.5 * lanes[1:2, :]
    length = jnp.where(core == 0, counts[0:1, :], counts[1:2, :]).reshape(1, 1, PART)

    def normed(value, span):
        frame = lax.broadcasted_iota(jnp.int32, (FRAMES, 1, PART), 0) + span * FRAMES
        shown = frame.astype(jnp.float32) < length
        centre = moments[2 * core, pl.ds(span, 1)].reshape(1, 1, PART)
        scale = jnp.where(shown, moments[2 * core + 1, pl.ds(span, 1)].reshape(1, 1, PART), 0.0)
        offset = jnp.where(shown, half_bias.reshape(1, 1, PART), 0.0)
        value = (value.astype(jnp.float32) - centre) * scale + offset
        return value + value * jnp.tanh(value)

    for step in range(CHIPS):
        for other in range(2):
            span = lax.rem(chip - step + CHIPS, CHIPS) * 2 + lax.rem(core + other, 2)
            raw[pl.ds(span * FRAMES, FRAMES)] = signal[step, other]
            for row in range(ROWS):
                if row == 0:
                    value = jnp.where(tile == 0, signal[step, other, :, :, :PART], above[step, other])
                elif row == ROWS - 1:
                    value = jnp.where(
                        tile == tiles - 1, signal[step, other, :, :, PART:], below[step, other]
                    )
                else:
                    value = signal[step, other, :, :, (row - 1) * PART : row * PART]
                value = normed(value, span)
                left = jnp.concatenate([value[:, :1], value[:, :-1]], axis=1)
                right = jnp.concatenate([value[:, 1:], value[:, -1:]], axis=1)
                for side, part in enumerate((left, value, right)):
                    shifted[
                        side, pl.ds(2 + span * FRAMES, FRAMES), :, row * PART : (row + 1) * PART
                    ] = part.astype(jnp.bfloat16)
    for side in range(3):
        shifted[side, 0] = shifted[side, 2]
        shifted[side, 1] = shifted[side, 2]


def taps_kernel(shifted, raw, mine, theirs, factor, out, weights):
    core = lax.axis_index("core")
    count = weights.shape[0]
    for tap in range(count):
        line, at = tap // LINE, tap % LINE * OUT
        for place, half in ((core, mine), (1 - core, theirs)):
            rows = pl.ds(pl.multiple_of(place * SHARE, SHARE), SHARE)
            weights[tap, rows] = half[line, :, at : at + OUT]
    length = SPANS * FRAMES
    scale = jnp.where(core == 0, factor[0:1, :], factor[1:2, :])
    for row in range(2):
        total = None
        for pair in range(count // 2):
            blocks = []
            for tap in (2 * pair, 2 * pair + 1):
                if tap < count - 1:
                    at = (row + tap // 3 % 3) * PART
                    block = shifted[tap % 3, tap // 9 : tap // 9 + length, :, at : at + PART]
                else:
                    block = raw[..., row * PART : (row + 1) * PART]
                blocks.append(block.reshape(-1, PART))
            term = jnp.dot(
                jnp.concatenate(blocks, axis=1),
                weights[2 * pair : 2 * pair + 2].reshape(2 * PART, OUT),
                preferred_element_type=jnp.float32,
            )
            total = term if total is None else total + term
        total = (total * scale).reshape(SPANS, FRAMES, COLS, OUT)
        out[:, :, row * COLS : (row + 1) * COLS, :] = total


def per_device(features, lengths, gain_in, bias_in, conv_in, skip_weight):
    videos, frames, row_count, col_count, wide_in = features.shape
    span, chip = lax.axis_index(TM), lax.axis_index("x")
    tiles, chips = lax.axis_size(TILE), lax.axis_size("x")
    taps = conv_in.shape[1]
    on_chip = pl.BlockSpec(memory_space=pltpu.VMEM)
    outside = pl.BlockSpec(memory_space=pl.ANY)
    params = pltpu.CompilerParams(vmem_limit_bytes=20 * 1024 * 1024)

    planes = features.reshape(videos * frames, row_count * col_count, wide_in)
    copies, counts = pl.pallas_call(
        payload_kernel,
        out_shape=(
            jax.ShapeDtypeStruct((tiles, 2, WIDTH), jnp.bfloat16),
            jax.ShapeDtypeStruct((8, 128), jnp.float32),
        ),
        in_specs=[outside] * 4,
        out_specs=(outside, on_chip),
        scratch_shapes=[
            pltpu.VMEM(planes.shape, jnp.bfloat16),
            pltpu.VMEM((taps, SPANS, OUT), jnp.bfloat16),
            pltpu.VMEM((SPANS, OUT), jnp.bfloat16),
            pltpu.SMEM((videos,), jnp.int32),
            pltpu.VMEM((32, OUT), jnp.float32),
            pltpu.VMEM((8, WIDTH), jnp.float32),
            pltpu.VMEM((8, 2, WIDTH), jnp.bfloat16),
            pltpu.SemaphoreType.DMA((4,)),
            pltpu.SemaphoreType.DMA((tiles // 8,)),
        ],
        compiler_params=params,
        name="payload",
    )(
        *[
            pltpu.with_memory_space_constraint(value, pltpu.HBM)
            for value in (planes, conv_in.transpose(1, 0, 2), skip_weight, lengths)
        ]
    )
    arrived = lax.all_to_all(copies, TILE, 0, 0, tiled=True)

    shape = (chips, frames, col_count, 2 * PART)
    kept, sent, lanes = pl.pallas_call(
        member_kernel,
        out_shape=(
            jax.ShapeDtypeStruct(shape, jnp.bfloat16),
            jax.ShapeDtypeStruct(shape, jnp.bfloat16),
            jax.ShapeDtypeStruct((2, PART), jnp.float32),
        ),
        in_specs=[on_chip] * 3,
        out_specs=(on_chip, on_chip, on_chip),
        compiler_params=params,
        name="member_shares",
    )(planes, gain_in.reshape(1, -1), bias_in.reshape(1, -1))
    swap = [(0, 1), (1, 0)]
    shares = jnp.stack([kept, lax.ppermute(sent, "core", swap)], axis=1)
    signal = []
    for step in range(chips):
        block = lax.dynamic_index_in_dim(shares, lax.rem(chip + step, chips), 0, False)
        if step:
            block = lax.ppermute(block, "x", [(i, (i + step) % chips) for i in range(chips)])
        signal.append(block)
    whole = (chips,) + signal[0].shape
    edge = whole[:-1] + (PART,)
    signal, upper, lower = pl.pallas_call(
        edges_kernel,
        out_shape=tuple(pltpu.VMEM(shape, jnp.bfloat16) for shape in (whole, edge, edge)),
        in_specs=[on_chip] * chips,
        out_specs=(on_chip, on_chip, on_chip),
        compiler_params=params,
        name="edges",
    )(*signal)
    above = lax.ppermute(upper, TILE, [(i, i + 1) for i in range(tiles - 1)])
    below = lax.ppermute(lower, TILE, [(i + 1, i) for i in range(tiles - 1)])

    held, upper, lower = lax.optimization_barrier((arrived, upper, lower))
    copies = pl.pallas_call(
        sums_kernel,
        out_shape=jax.ShapeDtypeStruct((SPANS, 1, 128), jnp.float32),
        in_specs=[on_chip, on_chip],
        out_specs=on_chip,
        compiler_params=params,
        name="sums",
    )(counts, pltpu.with_memory_space_constraint(held, pltpu.VMEM))
    totals = lax.all_to_all(copies, TM, 0, 0, tiled=True).reshape(SPANS, -1)
    mine = arrived.transpose(1, 0, 2)
    theirs = lax.ppermute(mine, "core", swap)

    shifted, raw, factor = pl.pallas_call(
        functools.partial(
            norm_kernel,
            cells=float(row_count * tiles * col_count * (wide_in // GROUPS)),
            tiles=tiles,
            tap_bound=float(taps * PART) * 0.0546875,
            skip_bound=float(PART) * 0.25,
        ),
        out_shape=(
            jax.ShapeDtypeStruct((3, SPANS * frames + 2, col_count, ROWS * PART), jnp.bfloat16),
            jax.ShapeDtypeStruct((SPANS * frames, col_count, 2 * PART), jnp.bfloat16),
            jax.ShapeDtypeStruct((videos, OUT), jnp.float32),
        ),
        in_specs=[on_chip] * 6,
        out_specs=(on_chip, on_chip, on_chip),
        scratch_shapes=[pltpu.VMEM((2 * videos + 1, SPANS, PART), jnp.float32)],
        compiler_params=params,
        cost_estimate=pl.CostEstimate(flops=1 << 34, bytes_accessed=1 << 26, transcendentals=1 << 24),
        name="norm",
    )(totals, counts, lanes, signal, above, below)
    total = pl.pallas_call(
        taps_kernel,
        out_shape=jax.ShapeDtypeStruct((SPANS, frames, row_count * col_count, OUT), jnp.float32),
        in_specs=[on_chip] * 5,
        out_specs=on_chip,
        scratch_shapes=[pltpu.VMEM((taps + 1, PART, OUT), jnp.bfloat16)],
        compiler_params=params,
        cost_estimate=pl.CostEstimate(
            flops=2 * 28 * 1024 * 128 * 256, bytes_accessed=6 << 20, transcendentals=0
        ),
        name="taps",
    )(shifted, raw, mine, theirs, factor)

    total = total.astype(jnp.float16)
    total = lax.all_to_all(total, TM, 0, 0, tiled=True).astype(jnp.float32)
    total = jnp.sum(total.reshape((chips, videos) + total.shape[1:]), axis=0)
    total = total / factor[:, None, None, :]
    total = total.reshape(videos, frames, row_count, col_count, OUT)
    stamps = span * frames + jnp.arange(frames, dtype=jnp.int32)
    present = stamps[None, :] < lengths[:, None]
    return jnp.where(present[:, :, None, None, None], total, 0.0).astype(jnp.bfloat16)


def solution(mesh):
    spans, tiles = mesh.devices.shape
    fine = Mesh(mesh.devices.reshape(spans // 2, 2, 8, tiles // 8), TM + TILE)
    placed = (
        P(None, TM, TILE, None, None),
        P(),
        P(),
        P(),
        P(TILE, None, None),
        P(TILE, None),
    )
    return jax.shard_map(
        per_device,
        mesh=fine,
        in_specs=placed,
        out_specs=P(None, TM, TILE, None, None),
        check_vma=False,
    )
```

```python
import functools

import jax
import jax.numpy as jnp
from jax import lax
from jax.experimental import pallas as pl
from jax.experimental.pallas import tpu as pltpu
from jax.sharding import Mesh
from jax.sharding import PartitionSpec as P

GROUPS = 32
EPS = 1e-06
TM = ("x", "core")
TILE = ("y", "z")
SPANS = 8
VIDEOS = 2
FRAMES = 4
COLS = 16
SHARE = 64
CHIPS = 4
PART = 2 * SHARE
ROWS = 4
LINE = 14
OUT = 256
WIDTH = LINE * OUT + 128


def to_all(block, axis):
    count = lax.axis_size(axis)
    copies = jnp.broadcast_to(block[None], (count,) + block.shape)
    return lax.all_to_all(copies, axis, 0, 0, tiled=True)


def exact_dot(value, chosen):
    high = value.astype(jnp.bfloat16)
    rest = value - high.astype(jnp.float32)
    middle = rest.astype(jnp.bfloat16)
    low = (rest - middle.astype(jnp.float32)).astype(jnp.bfloat16)
    total = jnp.dot(low, chosen, preferred_element_type=jnp.float32)
    total = total + jnp.dot(middle, chosen, preferred_element_type=jnp.float32)
    return total + jnp.dot(high, chosen, preferred_element_type=jnp.float32)


def own_counts(lengths, span):
    lane = lax.broadcasted_iota(jnp.int32, (1, 128), 1)
    count = jnp.where(lane % (2 * GROUPS) < GROUPS, lengths[0], lengths[1]) - span * FRAMES
    count = jnp.clip(count, 1, FRAMES).astype(jnp.float32)
    return 1.0 / (count * float(2 * COLS * SPANS * SHARE // GROUPS))


def own_square(value, inverse):
    axis = value.ndim - 1
    turned = pltpu.roll(value, 2 * GROUPS, axis)
    upper = lax.broadcasted_iota(jnp.int32, (1,) * axis + (128,), axis) >= 2 * GROUPS
    return jnp.where(upper, turned * turned * inverse, 0.0)


def payload_kernel(features, conv, skip, lengths, copies, counts, planes, taps, skips, valid, rows, packed, few, done, left):
    moves = [
        pltpu.make_async_copy(source, target, done.at[index])
        for index, (source, target) in enumerate(
            ((features, planes), (conv, taps), (skip, skips), (lengths, valid))
        )
    ]
    for move in moves:
        move.start()
    for move in moves[1:]:
        move.wait()
    count, channels = taps.shape[0], planes.shape[-1]
    span = lax.axis_index(TM)
    pick = lax.broadcasted_iota(jnp.int32, (count, SPANS, OUT), 1) == span
    rows[...] = jnp.zeros_like(rows)
    rows[0:count, :] = jnp.sum(jnp.where(pick, taps[...].astype(jnp.float32), 0.0), axis=1)
    pick = lax.broadcasted_iota(jnp.int32, (SPANS, OUT), 0) == span
    rows[count : count + 1, :] = jnp.sum(
        jnp.where(pick, skips[...].astype(jnp.float32), 0.0), axis=0, keepdims=True
    )
    moves[0].wait()
    lines = []
    for video in range(VIDEOS):
        linear = jnp.zeros((1, channels), jnp.float32)
        square = jnp.zeros((1, channels), jnp.float32)
        for frame in range(FRAMES):
            block = planes[video * FRAMES + frame].astype(jnp.float32)
            shown = (span * FRAMES + frame < valid[video]).astype(jnp.float32)
            linear += jnp.sum(block, axis=0, keepdims=True) * shown
            square += jnp.sum(block * block, axis=0, keepdims=True) * shown
        lines += [(video, linear), (VIDEOS + video, square)]
    lines = jnp.concatenate([line for _, line in sorted(lines, key=lambda pair: pair[0])], axis=0)
    group = lax.broadcasted_iota(jnp.int32, (channels, 128), 0) // (channels // GROUPS)
    lane = lax.broadcasted_iota(jnp.int32, (channels, 128), 1)
    spots = exact_dot(lines, (lane % GROUPS == group).astype(jnp.bfloat16))
    line = lax.broadcasted_iota(jnp.int32, spots.shape, 0)
    lane = lax.broadcasted_iota(jnp.int32, spots.shape, 1)
    sums = jnp.sum(jnp.where(lane // GROUPS == line, spots, 0.0), axis=0, keepdims=True)
    sums = jnp.broadcast_to(sums, (8, 128))
    inverse = own_counts(valid, span)
    sums = sums - own_square(sums, inverse)
    counts[...] = jnp.concatenate(
        [jnp.full((1, 128), valid[video]).astype(jnp.float32) for video in range(VIDEOS)]
        + [inverse, jnp.zeros((5, 128), jnp.float32)],
        axis=0,
    )
    high = sums.astype(jnp.bfloat16).astype(jnp.float32)
    for line, value in enumerate((high, sums - high)):
        packed[line : line + 1, LINE * OUT : WIDTH] = value[0:1]
    for row in range(2 * LINE):
        at = row % LINE * OUT
        packed[row // LINE : row // LINE + 1, at : at + OUT] = rows[row : row + 1, :]
    value = packed[0:2, :].astype(jnp.bfloat16)
    some = few.shape[0]
    for index in range(some):
        few[index] = value
    moves = [
        pltpu.make_async_copy(few, copies.at[pl.ds(index * some, some)], left.at[index])
        for index in range(copies.shape[0] // some)
    ]
    for move in moves:
        move.start()
    for move in moves:
        move.wait()


def sums_kernel(counts, arrived, copies):
    value = arrived[:, 0:1, LINE * OUT : WIDTH].astype(jnp.float32)
    value = value + arrived[:, 1:2, LINE * OUT : WIDTH].astype(jnp.float32)
    value = value + own_square(value, counts[2:3, :].reshape(1, 1, 128))
    total = jnp.sum(value, axis=0, keepdims=True)
    copies[...] = jnp.broadcast_to(total, copies.shape)


def member_kernel(features, gain, bias, kept, sent, lanes):
    voxels, channels = features.shape[0] * COLS, features.shape[-1]
    column = lax.broadcasted_iota(jnp.int32, (channels, channels), 1)
    place = column % PART
    source = place % SHARE * SPANS + column // PART * 2 + place // SHARE
    match = lax.broadcasted_iota(jnp.int32, (channels, channels), 0) == source
    chosen = jnp.where(match, 1.0, 0.0).astype(jnp.bfloat16)
    even = lax.axis_index("core") == 0
    for row in range(2):
        block = features[:, row * COLS : (row + 1) * COLS].reshape(voxels, channels)
        flat = jnp.dot(block, chosen, preferred_element_type=jnp.float32).astype(jnp.bfloat16)
        flat = flat.reshape(VIDEOS, FRAMES, COLS, channels)
        mine, other = jnp.where(even, flat[0], flat[1]), jnp.where(even, flat[1], flat[0])
        at = slice(row * PART, (row + 1) * PART)
        for chip in range(CHIPS):
            kept[chip, :, :, at] = mine[..., chip * PART : (chip + 1) * PART]
            sent[chip, :, :, at] = other[..., chip * PART : (chip + 1) * PART]
    place = lax.broadcasted_iota(jnp.int32, (channels, PART), 1)
    source = place % SHARE * SPANS + lax.axis_index("x") * 2 + place // SHARE
    match = lax.broadcasted_iota(jnp.int32, (channels, PART), 0) == source
    pair = jnp.concatenate([gain[...], bias[...]], axis=0)
    lanes[...] = exact_dot(pair, jnp.where(match, 1.0, 0.0).astype(jnp.bfloat16))


def norm_kernel(
    totals, counts, lanes, signal, above, below, shifted, raw, factor, moments,
    *, cells, tiles, tap_bound, skip_bound
):
    chip, core = lax.axis_index("x"), lax.axis_index("core")
    tile = lax.axis_index(TILE)
    summed = [totals[0:1, :]]
    for span in range(1, SPANS):
        summed.append(summed[-1] + totals[span : span + 1, :])
    summed = jnp.concatenate(summed, axis=0)
    entry = lax.broadcasted_iota(jnp.int32, (128, 4 * PART), 0)
    lane = lax.broadcasted_iota(jnp.int32, (128, 4 * PART), 1)
    wanted = lane // PART * GROUPS + lane % SHARE // 2
    spread = exact_dot(summed, jnp.where(entry == wanted, 1.0, 0.0).astype(jnp.bfloat16))
    ends = ((lax.broadcasted_iota(jnp.int32, (SPANS, PART), 0) + 1) * FRAMES).astype(jnp.float32)
    for video in range(VIDEOS):
        seen = jnp.minimum(ends, counts[video : video + 1, :]) * cells
        square = spread[:, (VIDEOS + video) * PART : (VIDEOS + video + 1) * PART]
        centre = spread[:, video * PART : (video + 1) * PART] / seen
        inverse = lax.rsqrt(square / seen - centre * centre + EPS)
        moments[2 * video] = centre
        moments[2 * video + 1] = 0.5 * inverse * lanes[0:1, :]
        size = jnp.sqrt(square)
        ratio = size * inverse
        ratio = jnp.where(ratio < 1e30, ratio, 0.0)
        bound = tap_bound * (3.0 * jnp.max(ratio, keepdims=True) + 3.0)
        bound = bound + skip_bound * jnp.max(size, keepdims=True)
        bound = jnp.exp2(14.0 - jnp.floor(jnp.log2(bound)))
        factor[video : video + 1, :] = jnp.broadcast_to(bound, (1, OUT))
    half_bias = 0.5 * lanes[1:2, :]
    length = jnp.where(core == 0, counts[0:1, :], counts[1:2, :]).reshape(1, 1, PART)

    def normed(value, span):
        frame = lax.broadcasted_iota(jnp.int32, (FRAMES, 1, PART), 0) + span * FRAMES
        shown = frame.astype(jnp.float32) < length
        centre = moments[2 * core, pl.ds(span, 1)].reshape(1, 1, PART)
        scale = jnp.where(shown, moments[2 * core + 1, pl.ds(span, 1)].reshape(1, 1, PART), 0.0)
        offset = jnp.where(shown, half_bias.reshape(1, 1, PART), 0.0)
        value = (value.astype(jnp.float32) - centre) * scale + offset
        return value + value * jnp.tanh(value)

    for step in range(CHIPS):
        for other in range(2):
            span = lax.rem(chip - step + CHIPS, CHIPS) * 2 + lax.rem(core + other, 2)
            raw[pl.ds(span * FRAMES, FRAMES)] = signal[step, other]
            for row in range(ROWS):
                if row == 0:
                    value = jnp.where(tile == 0, signal[step, other, :, :, :PART], above[step, other])
                elif row == ROWS - 1:
                    value = jnp.where(
                        tile == tiles - 1, signal[step, other, :, :, PART:], below[step, other]
                    )
                else:
                    value = signal[step, other, :, :, (row - 1) * PART : row * PART]
                value = normed(value, span)
                left = jnp.concatenate([value[:, :1], value[:, :-1]], axis=1)
                right = jnp.concatenate([value[:, 1:], value[:, -1:]], axis=1)
                for side, part in enumerate((left, value, right)):
                    shifted[
                        side, pl.ds(2 + span * FRAMES, FRAMES), :, row * PART : (row + 1) * PART
                    ] = part.astype(jnp.bfloat16)
    for side in range(3):
        shifted[side, 0] = shifted[side, 2]
        shifted[side, 1] = shifted[side, 2]


def taps_kernel(shifted, raw, mine, theirs, factor, out, weights):
    core = lax.axis_index("core")
    count = weights.shape[0]
    for tap in range(count):
        line, at = tap // LINE, tap % LINE * OUT
        for place, half in ((core, mine), (1 - core, theirs)):
            rows = pl.ds(pl.multiple_of(place * SHARE, SHARE), SHARE)
            weights[tap, rows] = half[line, :, at : at + OUT]
    length = SPANS * FRAMES
    scale = jnp.where(core == 0, factor[0:1, :], factor[1:2, :])
    for row in range(2):
        total = None
        for pair in range(count // 2):
            blocks = []
            for tap in (2 * pair, 2 * pair + 1):
                if tap < count - 1:
                    at = (row + tap // 3 % 3) * PART
                    block = shifted[tap % 3, tap // 9 : tap // 9 + length, :, at : at + PART]
                else:
                    block = raw[..., row * PART : (row + 1) * PART]
                blocks.append(block.reshape(-1, PART))
            term = jnp.dot(
                jnp.concatenate(blocks, axis=1),
                weights[2 * pair : 2 * pair + 2].reshape(2 * PART, OUT),
                preferred_element_type=jnp.float32,
            )
            total = term if total is None else total + term
        total = (total * scale).reshape(SPANS, FRAMES, COLS, OUT)
        out[:, :, row * COLS : (row + 1) * COLS, :] = total


def per_device(features, lengths, gain_in, bias_in, conv_in, skip_weight):
    videos, frames, row_count, col_count, wide_in = features.shape
    span, chip = lax.axis_index(TM), lax.axis_index("x")
    tiles, chips = lax.axis_size(TILE), lax.axis_size("x")
    taps = conv_in.shape[1]
    on_chip = pl.BlockSpec(memory_space=pltpu.VMEM)
    outside = pl.BlockSpec(memory_space=pl.ANY)
    params = pltpu.CompilerParams(vmem_limit_bytes=20 * 1024 * 1024)

    planes = features.reshape(videos * frames, row_count * col_count, wide_in)
    copies, counts = pl.pallas_call(
        payload_kernel,
        out_shape=(
            jax.ShapeDtypeStruct((tiles, 2, WIDTH), jnp.bfloat16),
            jax.ShapeDtypeStruct((8, 128), jnp.float32),
        ),
        in_specs=[outside] * 4,
        out_specs=(outside, on_chip),
        scratch_shapes=[
            pltpu.VMEM(planes.shape, jnp.bfloat16),
            pltpu.VMEM((taps, SPANS, OUT), jnp.bfloat16),
            pltpu.VMEM((SPANS, OUT), jnp.bfloat16),
            pltpu.SMEM((videos,), jnp.int32),
            pltpu.VMEM((32, OUT), jnp.float32),
            pltpu.VMEM((8, WIDTH), jnp.float32),
            pltpu.VMEM((8, 2, WIDTH), jnp.bfloat16),
            pltpu.SemaphoreType.DMA((4,)),
            pltpu.SemaphoreType.DMA((tiles // 8,)),
        ],
        compiler_params=params,
        name="payload",
    )(
        *[
            pltpu.with_memory_space_constraint(value, pltpu.HBM)
            for value in (planes, conv_in.transpose(1, 0, 2), skip_weight, lengths)
        ]
    )
    arrived = lax.all_to_all(copies, TILE, 0, 0, tiled=True)

    shape = (chips, frames, col_count, 2 * PART)
    kept, sent, lanes = pl.pallas_call(
        member_kernel,
        out_shape=(
            jax.ShapeDtypeStruct(shape, jnp.bfloat16),
            jax.ShapeDtypeStruct(shape, jnp.bfloat16),
            jax.ShapeDtypeStruct((2, PART), jnp.float32),
        ),
        in_specs=[on_chip] * 3,
        out_specs=(on_chip, on_chip, on_chip),
        compiler_params=params,
        name="member_shares",
    )(planes, gain_in.reshape(1, -1), bias_in.reshape(1, -1))
    swap = [(0, 1), (1, 0)]
    shares = jnp.stack([kept, lax.ppermute(sent, "core", swap)], axis=1)
    signal = []
    for step in range(chips):
        block = lax.dynamic_index_in_dim(shares, lax.rem(chip + step, chips), 0, False)
        if step:
            block = lax.ppermute(block, "x", [(i, (i + step) % chips) for i in range(chips)])
        signal.append(block)
    signal = jnp.stack(signal)
    upper, lower = signal[..., PART:], signal[..., :PART]
    above = lax.ppermute(upper, TILE, [(i, i + 1) for i in range(tiles - 1)])
    below = lax.ppermute(lower, TILE, [(i + 1, i) for i in range(tiles - 1)])

    held, upper, lower = lax.optimization_barrier((arrived, upper, lower))
    copies = pl.pallas_call(
        sums_kernel,
        out_shape=jax.ShapeDtypeStruct((SPANS, 1, 128), jnp.float32),
        in_specs=[on_chip, on_chip],
        out_specs=on_chip,
        compiler_params=params,
        name="sums",
    )(counts, pltpu.with_memory_space_constraint(held, pltpu.VMEM))
    totals = lax.all_to_all(copies, TM, 0, 0, tiled=True).reshape(SPANS, -1)
    mine = arrived.transpose(1, 0, 2)
    theirs = lax.ppermute(mine, "core", swap)

    shifted, raw, factor = pl.pallas_call(
        functools.partial(
            norm_kernel,
            cells=float(row_count * tiles * col_count * (wide_in // GROUPS)),
            tiles=tiles,
            tap_bound=float(taps * PART) * 0.0546875,
            skip_bound=float(PART) * 0.25,
        ),
        out_shape=(
            jax.ShapeDtypeStruct((3, SPANS * frames + 2, col_count, ROWS * PART), jnp.bfloat16),
            jax.ShapeDtypeStruct((SPANS * frames, col_count, 2 * PART), jnp.bfloat16),
            jax.ShapeDtypeStruct((videos, OUT), jnp.float32),
        ),
        in_specs=[on_chip] * 6,
        out_specs=(on_chip, on_chip, on_chip),
        scratch_shapes=[pltpu.VMEM((2 * videos + 1, SPANS, PART), jnp.float32)],
        compiler_params=params,
        cost_estimate=pl.CostEstimate(flops=1 << 34, bytes_accessed=1 << 26, transcendentals=1 << 24),
        name="norm",
    )(totals, counts, lanes, signal, above, below)
    total = pl.pallas_call(
        taps_kernel,
        out_shape=jax.ShapeDtypeStruct((SPANS, frames, row_count * col_count, OUT), jnp.float32),
        in_specs=[on_chip] * 5,
        out_specs=on_chip,
        scratch_shapes=[pltpu.VMEM((taps + 1, PART, OUT), jnp.bfloat16)],
        compiler_params=params,
        cost_estimate=pl.CostEstimate(
            flops=2 * 28 * 1024 * 128 * 256, bytes_accessed=6 << 20, transcendentals=0
        ),
        name="taps",
    )(shifted, raw, mine, theirs, factor)

    total = total.astype(jnp.float16)
    total = lax.all_to_all(total, TM, 0, 0, tiled=True).astype(jnp.float32)
    total = jnp.sum(total.reshape((chips, videos) + total.shape[1:]), axis=0)
    total = total / factor[:, None, None, :]
    total = total.reshape(videos, frames, row_count, col_count, OUT)
    stamps = span * frames + jnp.arange(frames, dtype=jnp.int32)
    present = stamps[None, :] < lengths[:, None]
    return jnp.where(present[:, :, None, None, None], total, 0.0).astype(jnp.bfloat16)


def solution(mesh):
    spans, tiles = mesh.devices.shape
    fine = Mesh(mesh.devices.reshape(spans // 2, 2, 8, tiles // 8), TM + TILE)
    placed = (
        P(None, TM, TILE, None, None),
        P(),
        P(),
        P(),
        P(TILE, None, None),
        P(TILE, None),
    )
    return jax.shard_map(
        per_device,
        mesh=fine,
        in_specs=placed,
        out_specs=P(None, TM, TILE, None, None),
        check_vma=False,
    )
```

```python
import functools

import jax
import jax.numpy as jnp
from jax import lax
from jax.experimental import pallas as pl
from jax.experimental.pallas import tpu as pltpu
from jax.sharding import Mesh
from jax.sharding import PartitionSpec as P

GROUPS = 32
EPS = 1e-06
TM = ("x", "core")
TILE = ("y", "z")
SPANS = 8
VIDEOS = 2
FRAMES = 4
COLS = 16
SHARE = 64
CHIPS = 4
PART = 2 * SHARE
ROWS = 4
LINE = 14
OUT = 256
WIDTH = LINE * OUT + 128


def exact_dot(value, chosen):
    high = value.astype(jnp.bfloat16)
    rest = value - high.astype(jnp.float32)
    middle = rest.astype(jnp.bfloat16)
    low = (rest - middle.astype(jnp.float32)).astype(jnp.bfloat16)
    total = jnp.dot(low, chosen, preferred_element_type=jnp.float32)
    total = total + jnp.dot(middle, chosen, preferred_element_type=jnp.float32)
    return total + jnp.dot(high, chosen, preferred_element_type=jnp.float32)


def own_counts(lengths, span):
    lane = lax.broadcasted_iota(jnp.int32, (1, 128), 1)
    count = jnp.where(lane % (2 * GROUPS) < GROUPS, lengths[0], lengths[1]) - span * FRAMES
    count = jnp.clip(count, 1, FRAMES).astype(jnp.float32)
    return 1.0 / (count * float(2 * COLS * SPANS * SHARE // GROUPS))


def own_square(value, inverse):
    axis = value.ndim - 1
    turned = pltpu.roll(value, 2 * GROUPS, axis)
    upper = lax.broadcasted_iota(jnp.int32, (1,) * axis + (128,), axis) >= 2 * GROUPS
    return jnp.where(upper, turned * (turned * inverse), 0.0)


def payload_kernel(features, conv, skip, lengths, copies, counts, planes, taps, skips, valid, rows, packed, few, done, left):
    moves = [
        pltpu.make_async_copy(source, target, done.at[index])
        for index, (source, target) in enumerate(
            ((features, planes), (conv, taps), (skip, skips), (lengths, valid))
        )
    ]
    for move in moves:
        move.start()
    for move in moves[1:]:
        move.wait()
    count, channels = taps.shape[0], planes.shape[-1]
    span = lax.axis_index(TM)
    pick = lax.broadcasted_iota(jnp.int32, (count, SPANS, OUT), 1) == span
    rows[...] = jnp.zeros_like(rows)
    rows[0:count, :] = jnp.sum(jnp.where(pick, taps[...].astype(jnp.float32), 0.0), axis=1)
    pick = lax.broadcasted_iota(jnp.int32, (SPANS, OUT), 0) == span
    rows[count : count + 1, :] = jnp.sum(
        jnp.where(pick, skips[...].astype(jnp.float32), 0.0), axis=0, keepdims=True
    )
    moves[0].wait()
    lines = []
    for video in range(VIDEOS):
        linear = jnp.zeros((1, channels), jnp.float32)
        square = jnp.zeros((1, channels), jnp.float32)
        for frame in range(FRAMES):
            block = planes[video * FRAMES + frame].astype(jnp.float32)
            shown = (span * FRAMES + frame < valid[video]).astype(jnp.float32)
            linear += jnp.sum(block, axis=0, keepdims=True) * shown
            square += jnp.sum(block * block, axis=0, keepdims=True) * shown
        lines += [(video, linear), (VIDEOS + video, square)]
    lines = jnp.concatenate([line for _, line in sorted(lines, key=lambda pair: pair[0])], axis=0)
    group = lax.broadcasted_iota(jnp.int32, (channels, 128), 0) // (channels // GROUPS)
    lane = lax.broadcasted_iota(jnp.int32, (channels, 128), 1)
    spots = exact_dot(lines, (lane % GROUPS == group).astype(jnp.bfloat16))
    line = lax.broadcasted_iota(jnp.int32, spots.shape, 0)
    lane = lax.broadcasted_iota(jnp.int32, spots.shape, 1)
    sums = jnp.sum(jnp.where(lane // GROUPS == line, spots, 0.0), axis=0, keepdims=True)
    sums = jnp.broadcast_to(sums, (8, 128))
    inverse = own_counts(valid, span)
    sums = sums - own_square(sums, inverse)
    counts[...] = jnp.concatenate(
        [jnp.full((1, 128), valid[video]).astype(jnp.float32) for video in range(VIDEOS)]
        + [inverse, jnp.zeros((5, 128), jnp.float32)],
        axis=0,
    )
    high = sums.astype(jnp.bfloat16).astype(jnp.float32)
    for line, value in enumerate((high, sums - high)):
        packed[line : line + 1, LINE * OUT : WIDTH] = value[0:1]
    for row in range(2 * LINE):
        at = row % LINE * OUT
        packed[row // LINE : row // LINE + 1, at : at + OUT] = rows[row : row + 1, :]
    value = packed[0:2, :].astype(jnp.bfloat16)
    some = few.shape[0]
    for index in range(some):
        few[index] = value
    moves = [
        pltpu.make_async_copy(few, copies.at[pl.ds(index * some, some)], left.at[index])
        for index in range(copies.shape[0] // some)
    ]
    for move in moves:
        move.start()
    for move in moves:
        move.wait()


def sums_kernel(counts, arrived, copies):
    value = arrived[:, 0:1, LINE * OUT : WIDTH].astype(jnp.float32)
    value = value + arrived[:, 1:2, LINE * OUT : WIDTH].astype(jnp.float32)
    value = value + own_square(value, counts[2:3, :].reshape(1, 1, 128))
    total = jnp.sum(value, axis=0, keepdims=True)
    copies[...] = jnp.broadcast_to(total, copies.shape)


def member_kernel(features, gain, bias, kept, sent, lanes):
    voxels, channels = features.shape[0] * COLS, features.shape[-1]
    column = lax.broadcasted_iota(jnp.int32, (channels, channels), 1)
    place = column % PART
    source = place % SHARE * SPANS + column // PART * 2 + place // SHARE
    match = lax.broadcasted_iota(jnp.int32, (channels, channels), 0) == source
    chosen = jnp.where(match, 1.0, 0.0).astype(jnp.bfloat16)
    even = lax.axis_index("core") == 0
    for row in range(2):
        block = features[:, row * COLS : (row + 1) * COLS].reshape(voxels, channels)
        flat = jnp.dot(block, chosen, preferred_element_type=jnp.float32).astype(jnp.bfloat16)
        flat = flat.reshape(VIDEOS, FRAMES, COLS, channels)
        mine, other = jnp.where(even, flat[0], flat[1]), jnp.where(even, flat[1], flat[0])
        at = slice(row * PART, (row + 1) * PART)
        for chip in range(CHIPS):
            kept[chip, :, :, at] = mine[..., chip * PART : (chip + 1) * PART]
            sent[chip, :, :, at] = other[..., chip * PART : (chip + 1) * PART]
    place = lax.broadcasted_iota(jnp.int32, (channels, PART), 1)
    source = place % SHARE * SPANS + lax.axis_index("x") * 2 + place // SHARE
    match = lax.broadcasted_iota(jnp.int32, (channels, PART), 0) == source
    pair = jnp.concatenate([gain[...], bias[...]], axis=0)
    lanes[...] = exact_dot(pair, jnp.where(match, 1.0, 0.0).astype(jnp.bfloat16))


def norm_kernel(
    totals, counts, lanes, signal, above, below, shifted, raw, factor, moments,
    *, cells, tiles, tap_bound, skip_bound
):
    chip, core = lax.axis_index("x"), lax.axis_index("core")
    tile = lax.axis_index(TILE)
    summed = [totals[0:1, :]]
    for span in range(1, SPANS):
        summed.append(summed[-1] + totals[span : span + 1, :])
    summed = jnp.concatenate(summed, axis=0)
    entry = lax.broadcasted_iota(jnp.int32, (128, 4 * PART), 0)
    lane = lax.broadcasted_iota(jnp.int32, (128, 4 * PART), 1)
    wanted = lane // PART * GROUPS + lane % SHARE // 2
    spread = exact_dot(summed, jnp.where(entry == wanted, 1.0, 0.0).astype(jnp.bfloat16))
    ends = ((lax.broadcasted_iota(jnp.int32, (SPANS, PART), 0) + 1) * FRAMES).astype(jnp.float32)
    for video in range(VIDEOS):
        seen = jnp.minimum(ends, counts[video : video + 1, :]) * cells
        square = spread[:, (VIDEOS + video) * PART : (VIDEOS + video + 1) * PART]
        centre = spread[:, video * PART : (video + 1) * PART] / seen
        inverse = lax.rsqrt(square / seen - centre * centre + EPS)
        moments[2 * video] = centre
        moments[2 * video + 1] = 0.5 * inverse * lanes[0:1, :]
        size = jnp.sqrt(square)
        ratio = size * inverse
        ratio = jnp.where(ratio < 1e30, ratio, 0.0)
        bound = tap_bound * (3.0 * jnp.max(ratio, keepdims=True) + 3.0)
        bound = bound + skip_bound * jnp.max(size, keepdims=True)
        bound = jnp.exp2(14.0 - jnp.floor(jnp.log2(bound)))
        factor[video : video + 1, :] = jnp.broadcast_to(bound, (1, OUT))
    half_bias = 0.5 * lanes[1:2, :]
    length = jnp.where(core == 0, counts[0:1, :], counts[1:2, :]).reshape(1, 1, PART)

    def normed(value, span):
        frame = lax.broadcasted_iota(jnp.int32, (FRAMES, 1, PART), 0) + span * FRAMES
        shown = frame.astype(jnp.float32) < length
        centre = moments[2 * core, pl.ds(span, 1)].reshape(1, 1, PART)
        scale = jnp.where(shown, moments[2 * core + 1, pl.ds(span, 1)].reshape(1, 1, PART), 0.0)
        offset = jnp.where(shown, half_bias.reshape(1, 1, PART), 0.0)
        value = (value.astype(jnp.float32) - centre) * scale + offset
        return value + value * jnp.tanh(value)

    for step in range(CHIPS):
        for other in range(2):
            span = lax.rem(chip - step + CHIPS, CHIPS) * 2 + lax.rem(core + other, 2)
            raw[pl.ds(span * FRAMES, FRAMES)] = signal[step, other]
            for row in range(ROWS):
                if row == 0:
                    value = jnp.where(tile == 0, signal[step, other, :, :, :PART], above[step, other])
                elif row == ROWS - 1:
                    value = jnp.where(
                        tile == tiles - 1, signal[step, other, :, :, PART:], below[step, other]
                    )
                else:
                    value = signal[step, other, :, :, (row - 1) * PART : row * PART]
                value = normed(value, span)
                left = jnp.concatenate([value[:, :1], value[:, :-1]], axis=1)
                right = jnp.concatenate([value[:, 1:], value[:, -1:]], axis=1)
                for side, part in enumerate((left, value, right)):
                    shifted[
                        side, pl.ds(2 + span * FRAMES, FRAMES), :, row * PART : (row + 1) * PART
                    ] = part.astype(jnp.bfloat16)
    for side in range(3):
        shifted[side, 0] = shifted[side, 2]
        shifted[side, 1] = shifted[side, 2]


def taps_kernel(shifted, raw, mine, theirs, factor, out, weights):
    core = lax.axis_index("core")
    count = weights.shape[0]
    for tap in range(count):
        line, at = tap // LINE, tap % LINE * OUT
        for place, half in ((core, mine), (1 - core, theirs)):
            rows = pl.ds(pl.multiple_of(place * SHARE, SHARE), SHARE)
            weights[tap, rows] = half[line, :, at : at + OUT]
    length = SPANS * FRAMES
    scale = jnp.where(core == 0, factor[0:1, :], factor[1:2, :])
    for row in range(2):
        total = None
        for pair in range(count // 2):
            blocks = []
            for tap in (2 * pair, 2 * pair + 1):
                if tap < count - 1:
                    at = (row + tap // 3 % 3) * PART
                    block = shifted[tap % 3, tap // 9 : tap // 9 + length, :, at : at + PART]
                else:
                    block = raw[..., row * PART : (row + 1) * PART]
                blocks.append(block.reshape(-1, PART))
            term = jnp.dot(
                jnp.concatenate(blocks, axis=1),
                weights[2 * pair : 2 * pair + 2].reshape(2 * PART, OUT),
                preferred_element_type=jnp.float32,
            )
            total = term if total is None else total + term
        total = (total * scale).reshape(SPANS, FRAMES, COLS, OUT)
        out[:, :, row * COLS : (row + 1) * COLS, :] = total


def per_device(features, lengths, gain_in, bias_in, conv_in, skip_weight):
    videos, frames, row_count, col_count, wide_in = features.shape
    span, chip = lax.axis_index(TM), lax.axis_index("x")
    tiles, chips = lax.axis_size(TILE), lax.axis_size("x")
    taps = conv_in.shape[1]
    on_chip = pl.BlockSpec(memory_space=pltpu.VMEM)
    outside = pl.BlockSpec(memory_space=pl.ANY)
    params = pltpu.CompilerParams(vmem_limit_bytes=20 * 1024 * 1024)

    planes = features.reshape(videos * frames, row_count * col_count, wide_in)
    copies, counts = pl.pallas_call(
        payload_kernel,
        out_shape=(
            jax.ShapeDtypeStruct((tiles, 2, WIDTH), jnp.bfloat16),
            jax.ShapeDtypeStruct((8, 128), jnp.float32),
        ),
        in_specs=[outside] * 4,
        out_specs=(outside, on_chip),
        scratch_shapes=[
            pltpu.VMEM(planes.shape, jnp.bfloat16),
            pltpu.VMEM((taps, SPANS, OUT), jnp.bfloat16),
            pltpu.VMEM((SPANS, OUT), jnp.bfloat16),
            pltpu.SMEM((videos,), jnp.int32),
            pltpu.VMEM((32, OUT), jnp.float32),
            pltpu.VMEM((8, WIDTH), jnp.float32),
            pltpu.VMEM((8, 2, WIDTH), jnp.bfloat16),
            pltpu.SemaphoreType.DMA((4,)),
            pltpu.SemaphoreType.DMA((tiles // 8,)),
        ],
        compiler_params=params,
        name="payload",
    )(
        *[
            pltpu.with_memory_space_constraint(value, pltpu.HBM)
            for value in (planes, conv_in.transpose(1, 0, 2), skip_weight, lengths)
        ]
    )
    arrived = lax.all_to_all(copies, TILE, 0, 0, tiled=True)

    shape = (chips, frames, col_count, 2 * PART)
    kept, sent, lanes = pl.pallas_call(
        member_kernel,
        out_shape=(
            jax.ShapeDtypeStruct(shape, jnp.bfloat16),
            jax.ShapeDtypeStruct(shape, jnp.bfloat16),
            jax.ShapeDtypeStruct((2, PART), jnp.float32),
        ),
        in_specs=[on_chip] * 3,
        out_specs=(on_chip, on_chip, on_chip),
        compiler_params=params,
        name="member_shares",
    )(planes, gain_in.reshape(1, -1), bias_in.reshape(1, -1))
    swap = [(0, 1), (1, 0)]
    shares = jnp.stack([kept, lax.ppermute(sent, "core", swap)], axis=1)
    signal = []
    for step in range(chips):
        block = lax.dynamic_index_in_dim(shares, lax.rem(chip + step, chips), 0, False)
        if step:
            block = lax.ppermute(block, "x", [(i, (i + step) % chips) for i in range(chips)])
        signal.append(block)
    signal = jnp.stack(signal)
    upper, lower = signal[..., PART:], signal[..., :PART]
    above = lax.ppermute(upper, TILE, [(i, i + 1) for i in range(tiles - 1)])
    below = lax.ppermute(lower, TILE, [(i + 1, i) for i in range(tiles - 1)])

    held, upper, lower = lax.optimization_barrier((arrived, upper, lower))
    copies = pl.pallas_call(
        sums_kernel,
        out_shape=jax.ShapeDtypeStruct((SPANS, 1, 128), jnp.float32),
        in_specs=[on_chip, on_chip],
        out_specs=on_chip,
        compiler_params=params,
        name="sums",
    )(counts, pltpu.with_memory_space_constraint(held, pltpu.VMEM))
    totals = lax.all_to_all(copies, TM, 0, 0, tiled=True).reshape(SPANS, -1)
    mine = arrived.transpose(1, 0, 2)
    theirs = lax.ppermute(mine, "core", swap)

    shifted, raw, factor = pl.pallas_call(
        functools.partial(
            norm_kernel,
            cells=float(row_count * tiles * col_count * (wide_in // GROUPS)),
            tiles=tiles,
            tap_bound=float(taps * PART) * 0.0546875,
            skip_bound=float(PART) * 0.25,
        ),
        out_shape=(
            jax.ShapeDtypeStruct((3, SPANS * frames + 2, col_count, ROWS * PART), jnp.bfloat16),
            jax.ShapeDtypeStruct((SPANS * frames, col_count, 2 * PART), jnp.bfloat16),
            jax.ShapeDtypeStruct((videos, OUT), jnp.float32),
        ),
        in_specs=[on_chip] * 6,
        out_specs=(on_chip, on_chip, on_chip),
        scratch_shapes=[pltpu.VMEM((2 * videos + 1, SPANS, PART), jnp.float32)],
        compiler_params=params,
        cost_estimate=pl.CostEstimate(flops=1 << 34, bytes_accessed=1 << 26, transcendentals=1 << 24),
        name="norm",
    )(totals, counts, lanes, signal, above, below)
    total = pl.pallas_call(
        taps_kernel,
        out_shape=jax.ShapeDtypeStruct((SPANS, frames, row_count * col_count, OUT), jnp.float32),
        in_specs=[on_chip] * 5,
        out_specs=on_chip,
        scratch_shapes=[pltpu.VMEM((taps + 1, PART, OUT), jnp.bfloat16)],
        compiler_params=params,
        cost_estimate=pl.CostEstimate(
            flops=2 * 28 * 1024 * 128 * 256, bytes_accessed=6 << 20, transcendentals=0
        ),
        name="taps",
    )(shifted, raw, mine, theirs, factor)

    total = total.astype(jnp.float16)
    total = lax.all_to_all(total, TM, 0, 0, tiled=True).astype(jnp.float32)
    total = jnp.sum(total.reshape((chips, videos) + total.shape[1:]), axis=0)
    total = total / factor[:, None, None, :]
    total = total.reshape(videos, frames, row_count, col_count, OUT)
    stamps = span * frames + jnp.arange(frames, dtype=jnp.int32)
    present = stamps[None, :] < lengths[:, None]
    return jnp.where(present[:, :, None, None, None], total, 0.0).astype(jnp.bfloat16)


def solution(mesh):
    spans, tiles = mesh.devices.shape
    fine = Mesh(mesh.devices.reshape(spans // 2, 2, 8, tiles // 8), TM + TILE)
    placed = (
        P(None, TM, TILE, None, None),
        P(),
        P(),
        P(),
        P(TILE, None, None),
        P(TILE, None),
    )
    return jax.shard_map(
        per_device,
        mesh=fine,
        in_specs=placed,
        out_specs=P(None, TM, TILE, None, None),
        check_vma=False,
    )
```

```python
import functools

import jax
import jax.numpy as jnp
from jax import lax
from jax.experimental import pallas as pl
from jax.experimental.pallas import tpu as pltpu
from jax.sharding import Mesh
from jax.sharding import PartitionSpec as P

GROUPS = 32
EPS = 1e-06
TM = ("x", "core")
TILE = ("y", "z")
SPANS = 8
VIDEOS = 2
FRAMES = 4
COLS = 16
SHARE = 64
CHIPS = 4
PART = 2 * SHARE
ROWS = 4
LINE = 14
OUT = 256
WIDTH = LINE * OUT + 128


def exact_dot(value, chosen):
    high = value.astype(jnp.bfloat16)
    rest = value - high.astype(jnp.float32)
    middle = rest.astype(jnp.bfloat16)
    low = (rest - middle.astype(jnp.float32)).astype(jnp.bfloat16)
    total = jnp.dot(low, chosen, preferred_element_type=jnp.float32)
    total = total + jnp.dot(middle, chosen, preferred_element_type=jnp.float32)
    return total + jnp.dot(high, chosen, preferred_element_type=jnp.float32)


def own_counts(lengths, span):
    lane = lax.broadcasted_iota(jnp.int32, (1, 128), 1)
    count = jnp.where(lane % (2 * GROUPS) < GROUPS, lengths[0], lengths[1]) - span * FRAMES
    count = jnp.clip(count, 1, FRAMES).astype(jnp.float32)
    return 1.0 / (count * float(2 * COLS * SPANS * SHARE // GROUPS))


def own_square(value, inverse):
    axis = value.ndim - 1
    turned = pltpu.roll(value, 2 * GROUPS, axis)
    upper = lax.broadcasted_iota(jnp.int32, (1,) * axis + (128,), axis) >= 2 * GROUPS
    return jnp.where(upper, turned * (turned * inverse), 0.0)


def payload_kernel(features, conv, skip, lengths, copies, counts, planes, taps, skips, valid, rows, packed, few, done, left):
    moves = [
        pltpu.make_async_copy(source, target, done.at[index])
        for index, (source, target) in enumerate(
            ((features, planes), (conv, taps), (skip, skips), (lengths, valid))
        )
    ]
    for move in moves:
        move.start()
    for move in moves[1:]:
        move.wait()
    count, channels = taps.shape[0], planes.shape[-1]
    span = lax.axis_index(TM)
    pick = lax.broadcasted_iota(jnp.int32, (count, SPANS, OUT), 1) == span
    rows[...] = jnp.zeros_like(rows)
    rows[0:count, :] = jnp.sum(jnp.where(pick, taps[...].astype(jnp.float32), 0.0), axis=1)
    pick = lax.broadcasted_iota(jnp.int32, (SPANS, OUT), 0) == span
    rows[count : count + 1, :] = jnp.sum(
        jnp.where(pick, skips[...].astype(jnp.float32), 0.0), axis=0, keepdims=True
    )
    moves[0].wait()
    lines = []
    for video in range(VIDEOS):
        linear = jnp.zeros((1, channels), jnp.float32)
        square = jnp.zeros((1, channels), jnp.float32)
        for frame in range(FRAMES):
            block = planes[video * FRAMES + frame].astype(jnp.float32)
            shown = (span * FRAMES + frame < valid[video]).astype(jnp.float32)
            linear += jnp.sum(block, axis=0, keepdims=True) * shown
            square += jnp.sum(block * block, axis=0, keepdims=True) * shown
        lines += [(video, linear), (VIDEOS + video, square)]
    lines = jnp.concatenate([line for _, line in sorted(lines, key=lambda pair: pair[0])], axis=0)
    group = lax.broadcasted_iota(jnp.int32, (channels, 128), 0) // (channels // GROUPS)
    lane = lax.broadcasted_iota(jnp.int32, (channels, 128), 1)
    spots = exact_dot(lines, (lane % GROUPS == group).astype(jnp.bfloat16))
    line = lax.broadcasted_iota(jnp.int32, spots.shape, 0)
    lane = lax.broadcasted_iota(jnp.int32, spots.shape, 1)
    sums = jnp.sum(jnp.where(lane // GROUPS == line, spots, 0.0), axis=0, keepdims=True)
    sums = jnp.broadcast_to(sums, (8, 128))
    inverse = own_counts(valid, span)
    sums = sums - own_square(sums, inverse)
    counts[...] = jnp.concatenate(
        [jnp.full((1, 128), valid[video]).astype(jnp.float32) for video in range(VIDEOS)]
        + [inverse, jnp.zeros((5, 128), jnp.float32)],
        axis=0,
    )
    high = sums.astype(jnp.bfloat16).astype(jnp.float32)
    for line, value in enumerate((high, sums - high)):
        packed[line : line + 1, LINE * OUT : WIDTH] = value[0:1]
    for row in range(2 * LINE):
        at = row % LINE * OUT
        packed[row // LINE : row // LINE + 1, at : at + OUT] = rows[row : row + 1, :]
    value = packed[0:2, :].astype(jnp.bfloat16)
    some = few.shape[0]
    for index in range(some):
        few[index] = value
    moves = [
        pltpu.make_async_copy(few, copies.at[pl.ds(index * some, some)], left.at[index])
        for index in range(copies.shape[0] // some)
    ]
    for move in moves:
        move.start()
    for move in moves:
        move.wait()


def sums_kernel(counts, arrived, copies):
    value = arrived[:, 0:1, LINE * OUT : WIDTH].astype(jnp.float32)
    value = value + arrived[:, 1:2, LINE * OUT : WIDTH].astype(jnp.float32)
    value = value + own_square(value, counts[2:3, :].reshape(1, 1, 128))
    total = jnp.sum(value, axis=0, keepdims=True)
    copies[...] = jnp.broadcast_to(total, copies.shape)


def member_kernel(features, gain, bias, kept, sent, lanes):
    voxels, channels = features.shape[0] * COLS, features.shape[-1]
    column = lax.broadcasted_iota(jnp.int32, (channels, channels), 1)
    place = column % PART
    source = place % SHARE * SPANS + column // PART * 2 + place // SHARE
    match = lax.broadcasted_iota(jnp.int32, (channels, channels), 0) == source
    chosen = jnp.where(match, 1.0, 0.0).astype(jnp.bfloat16)
    even = lax.axis_index("core") == 0
    for row in range(2):
        block = features[:, row * COLS : (row + 1) * COLS].reshape(voxels, channels)
        flat = jnp.dot(block, chosen, preferred_element_type=jnp.float32).astype(jnp.bfloat16)
        flat = flat.reshape(VIDEOS, FRAMES, COLS, channels)
        mine, other = jnp.where(even, flat[0], flat[1]), jnp.where(even, flat[1], flat[0])
        at = slice(row * PART, (row + 1) * PART)
        for chip in range(CHIPS):
            kept[chip, :, :, at] = mine[..., chip * PART : (chip + 1) * PART]
            sent[chip, :, :, at] = other[..., chip * PART : (chip + 1) * PART]
    place = lax.broadcasted_iota(jnp.int32, (channels, PART), 1)
    source = place % SHARE * SPANS + lax.axis_index("x") * 2 + place // SHARE
    match = lax.broadcasted_iota(jnp.int32, (channels, PART), 0) == source
    pair = jnp.concatenate([gain[...], bias[...]], axis=0)
    lanes[...] = exact_dot(pair, jnp.where(match, 1.0, 0.0).astype(jnp.bfloat16))


def norm_kernel(
    totals, counts, lanes, signal, above, below, shifted, raw, factor, moments,
    *, cells, tiles, tap_bound, skip_bound
):
    chip, core = lax.axis_index("x"), lax.axis_index("core")
    tile = lax.axis_index(TILE)
    summed = [totals[0:1, :]]
    for span in range(1, SPANS):
        summed.append(summed[-1] + totals[span : span + 1, :])
    summed = jnp.concatenate(summed, axis=0)
    entry = lax.broadcasted_iota(jnp.int32, (128, 4 * PART), 0)
    lane = lax.broadcasted_iota(jnp.int32, (128, 4 * PART), 1)
    wanted = lane // PART * GROUPS + lane % SHARE // 2
    spread = exact_dot(summed, jnp.where(entry == wanted, 1.0, 0.0).astype(jnp.bfloat16))
    ends = ((lax.broadcasted_iota(jnp.int32, (SPANS, PART), 0) + 1) * FRAMES).astype(jnp.float32)
    for video in range(VIDEOS):
        seen = jnp.minimum(ends, counts[video : video + 1, :]) * cells
        square = spread[:, (VIDEOS + video) * PART : (VIDEOS + video + 1) * PART]
        centre = spread[:, video * PART : (video + 1) * PART] / seen
        inverse = lax.rsqrt(square / seen - centre * centre + EPS)
        moments[2 * video] = centre
        moments[2 * video + 1] = 0.5 * inverse * lanes[0:1, :]
        size = jnp.sqrt(square)
        ratio = size * inverse
        ratio = jnp.where(ratio < 1e30, ratio, 0.0)
        bound = tap_bound * (3.0 * jnp.max(ratio, keepdims=True) + 3.0)
        bound = bound + skip_bound * jnp.max(size, keepdims=True)
        bound = jnp.exp2(14.0 - jnp.floor(jnp.log2(bound)))
        factor[video : video + 1, :] = jnp.broadcast_to(bound, (1, OUT))
    half_bias = 0.5 * lanes[1:2, :]
    length = jnp.where(core == 0, counts[0:1, :], counts[1:2, :]).reshape(1, 1, PART)

    def normed(value, span):
        frame = lax.broadcasted_iota(jnp.int32, (FRAMES, 1, PART), 0) + span * FRAMES
        shown = frame.astype(jnp.float32) < length
        centre = moments[2 * core, pl.ds(span, 1)].reshape(1, 1, PART)
        scale = jnp.where(shown, moments[2 * core + 1, pl.ds(span, 1)].reshape(1, 1, PART), 0.0)
        offset = jnp.where(shown, half_bias.reshape(1, 1, PART), 0.0)
        value = (value.astype(jnp.float32) - centre) * scale + offset
        return value + value * jnp.tanh(value)

    for step in range(CHIPS):
        for other in range(2):
            span = lax.rem(chip - step + CHIPS, CHIPS) * 2 + lax.rem(core + other, 2)
            raw[pl.ds(span * FRAMES, FRAMES)] = signal[step, other]
            for row in range(ROWS):
                if row == 0:
                    value = jnp.where(tile == 0, signal[step, other, :, :, :PART], above[step, other])
                elif row == ROWS - 1:
                    value = jnp.where(
                        tile == tiles - 1, signal[step, other, :, :, PART:], below[step, other]
                    )
                else:
                    value = signal[step, other, :, :, (row - 1) * PART : row * PART]
                value = normed(value, span)
                left = jnp.concatenate([value[:, :1], value[:, :-1]], axis=1)
                right = jnp.concatenate([value[:, 1:], value[:, -1:]], axis=1)
                for side, part in enumerate((left, value, right)):
                    shifted[
                        side, pl.ds(2 + span * FRAMES, FRAMES), :, row * PART : (row + 1) * PART
                    ] = part.astype(jnp.bfloat16)
    for side in range(3):
        shifted[side, 0] = shifted[side, 2]
        shifted[side, 1] = shifted[side, 2]


def taps_kernel(shifted, raw, mine, theirs, factor, out, weights):
    core = lax.axis_index("core")
    count = weights.shape[0]
    for tap in range(count):
        line, at = tap // LINE, tap % LINE * OUT
        for place, half in ((core, mine), (1 - core, theirs)):
            rows = pl.ds(pl.multiple_of(place * SHARE, SHARE), SHARE)
            weights[tap, rows] = half[line, :, at : at + OUT]
    length = SPANS * FRAMES
    scale = jnp.where(core == 0, factor[0:1, :], factor[1:2, :])
    for row in range(2):
        total = None
        for pair in range(count // 2):
            blocks = []
            for tap in (2 * pair, 2 * pair + 1):
                if tap < count - 1:
                    at = (row + tap // 3 % 3) * PART
                    block = shifted[tap % 3, tap // 9 : tap // 9 + length, :, at : at + PART]
                else:
                    block = raw[..., row * PART : (row + 1) * PART]
                blocks.append(block.reshape(-1, PART))
            term = jnp.dot(
                jnp.concatenate(blocks, axis=1),
                weights[2 * pair : 2 * pair + 2].reshape(2 * PART, OUT),
                preferred_element_type=jnp.float32,
            )
            total = term if total is None else total + term
        total = (total * scale).reshape(SPANS, FRAMES, COLS, OUT)
        out[:, :, row * COLS : (row + 1) * COLS, :] = total


def per_device(features, lengths, gain_in, bias_in, conv_in, skip_weight):
    videos, frames, row_count, col_count, wide_in = features.shape
    span, chip = lax.axis_index(TM), lax.axis_index("x")
    tiles, chips = lax.axis_size(TILE), lax.axis_size("x")
    taps = conv_in.shape[1]
    on_chip = pl.BlockSpec(memory_space=pltpu.VMEM)
    outside = pl.BlockSpec(memory_space=pl.ANY)
    params = pltpu.CompilerParams(vmem_limit_bytes=20 * 1024 * 1024)

    planes = features.reshape(videos * frames, row_count * col_count, wide_in)
    copies, counts = pl.pallas_call(
        payload_kernel,
        out_shape=(
            jax.ShapeDtypeStruct((tiles, 2, WIDTH), jnp.bfloat16),
            jax.ShapeDtypeStruct((8, 128), jnp.float32),
        ),
        in_specs=[outside] * 4,
        out_specs=(outside, on_chip),
        scratch_shapes=[
            pltpu.VMEM(planes.shape, jnp.bfloat16),
            pltpu.VMEM((taps, SPANS, OUT), jnp.bfloat16),
            pltpu.VMEM((SPANS, OUT), jnp.bfloat16),
            pltpu.SMEM((videos,), jnp.int32),
            pltpu.VMEM((32, OUT), jnp.float32),
            pltpu.VMEM((8, WIDTH), jnp.float32),
            pltpu.VMEM((8, 2, WIDTH), jnp.bfloat16),
            pltpu.SemaphoreType.DMA((4,)),
            pltpu.SemaphoreType.DMA((tiles // 8,)),
        ],
        compiler_params=params,
        name="payload",
    )(
        *[
            pltpu.with_memory_space_constraint(value, pltpu.HBM)
            for value in (planes, conv_in.transpose(1, 0, 2), skip_weight, lengths)
        ]
    )
    arrived = lax.all_to_all(copies, TILE, 0, 0, tiled=True)

    shape = (chips, frames, col_count, 2 * PART)
    kept, sent, lanes = pl.pallas_call(
        member_kernel,
        out_shape=(
            jax.ShapeDtypeStruct(shape, jnp.bfloat16),
            jax.ShapeDtypeStruct(shape, jnp.bfloat16),
            jax.ShapeDtypeStruct((2, PART), jnp.float32),
        ),
        in_specs=[on_chip] * 3,
        out_specs=(on_chip, on_chip, on_chip),
        compiler_params=params,
        name="member_shares",
    )(planes, gain_in.reshape(1, -1), bias_in.reshape(1, -1))
    swap = [(0, 1), (1, 0)]
    shares = jnp.stack([kept, lax.ppermute(sent, "core", swap)], axis=1)
    signal = []
    for step in range(chips):
        block = lax.dynamic_index_in_dim(shares, lax.rem(chip + step, chips), 0, False)
        if step:
            block = lax.ppermute(block, "x", [(i, (i + step) % chips) for i in range(chips)])
        signal.append(block)
    upper = jnp.stack([block[..., PART:] for block in signal])
    lower = jnp.stack([block[..., :PART] for block in signal])
    signal = jnp.stack(signal)
    above = lax.ppermute(upper, TILE, [(i, i + 1) for i in range(tiles - 1)])
    below = lax.ppermute(lower, TILE, [(i + 1, i) for i in range(tiles - 1)])

    held, upper, lower = lax.optimization_barrier((arrived, upper, lower))
    copies = pl.pallas_call(
        sums_kernel,
        out_shape=jax.ShapeDtypeStruct((SPANS, 1, 128), jnp.float32),
        in_specs=[on_chip, on_chip],
        out_specs=on_chip,
        compiler_params=params,
        name="sums",
    )(counts, pltpu.with_memory_space_constraint(held, pltpu.VMEM))
    totals = lax.all_to_all(copies, TM, 0, 0, tiled=True).reshape(SPANS, -1)
    mine = arrived.transpose(1, 0, 2)
    theirs = lax.ppermute(mine, "core", swap)

    shifted, raw, factor = pl.pallas_call(
        functools.partial(
            norm_kernel,
            cells=float(row_count * tiles * col_count * (wide_in // GROUPS)),
            tiles=tiles,
            tap_bound=float(taps * PART) * 0.0546875,
            skip_bound=float(PART) * 0.25,
        ),
        out_shape=(
            jax.ShapeDtypeStruct((3, SPANS * frames + 2, col_count, ROWS * PART), jnp.bfloat16),
            jax.ShapeDtypeStruct((SPANS * frames, col_count, 2 * PART), jnp.bfloat16),
            jax.ShapeDtypeStruct((videos, OUT), jnp.float32),
        ),
        in_specs=[on_chip] * 6,
        out_specs=(on_chip, on_chip, on_chip),
        scratch_shapes=[pltpu.VMEM((2 * videos + 1, SPANS, PART), jnp.float32)],
        compiler_params=params,
        cost_estimate=pl.CostEstimate(flops=1 << 34, bytes_accessed=1 << 26, transcendentals=1 << 24),
        name="norm",
    )(totals, counts, lanes, signal, above, below)
    total = pl.pallas_call(
        taps_kernel,
        out_shape=jax.ShapeDtypeStruct((SPANS, frames, row_count * col_count, OUT), jnp.float32),
        in_specs=[on_chip] * 5,
        out_specs=on_chip,
        scratch_shapes=[pltpu.VMEM((taps + 1, PART, OUT), jnp.bfloat16)],
        compiler_params=params,
        cost_estimate=pl.CostEstimate(
            flops=2 * 28 * 1024 * 128 * 256, bytes_accessed=6 << 20, transcendentals=0
        ),
        name="taps",
    )(shifted, raw, mine, theirs, factor)

    total = total.astype(jnp.float16)
    total = lax.all_to_all(total, TM, 0, 0, tiled=True).astype(jnp.float32)
    total = jnp.sum(total.reshape((chips, videos) + total.shape[1:]), axis=0)
    total = total / factor[:, None, None, :]
    total = total.reshape(videos, frames, row_count, col_count, OUT)
    stamps = span * frames + jnp.arange(frames, dtype=jnp.int32)
    present = stamps[None, :] < lengths[:, None]
    return jnp.where(present[:, :, None, None, None], total, 0.0).astype(jnp.bfloat16)


def solution(mesh):
    spans, tiles = mesh.devices.shape
    fine = Mesh(mesh.devices.reshape(spans // 2, 2, 8, tiles // 8), TM + TILE)
    placed = (
        P(None, TM, TILE, None, None),
        P(),
        P(),
        P(),
        P(TILE, None, None),
        P(TILE, None),
    )
    return jax.shard_map(
        per_device,
        mesh=fine,
        in_specs=placed,
        out_specs=P(None, TM, TILE, None, None),
        check_vma=False,
    )
```

```python
import functools

import jax
import jax.numpy as jnp
from jax import lax
from jax.experimental import pallas as pl
from jax.experimental.pallas import tpu as pltpu
from jax.sharding import Mesh
from jax.sharding import PartitionSpec as P

GROUPS = 32
EPS = 1e-06
TM = ("x", "core")
TILE = ("y", "z")
SPANS = 8
VIDEOS = 2
FRAMES = 4
COLS = 16
SHARE = 64
CHIPS = 4
PART = 2 * SHARE
ROWS = 4
LINE = 14
OUT = 256
WIDTH = LINE * OUT + 128


def exact_dot(value, chosen):
    high = value.astype(jnp.bfloat16)
    rest = value - high.astype(jnp.float32)
    middle = rest.astype(jnp.bfloat16)
    low = (rest - middle.astype(jnp.float32)).astype(jnp.bfloat16)
    total = jnp.dot(low, chosen, preferred_element_type=jnp.float32)
    total = total + jnp.dot(middle, chosen, preferred_element_type=jnp.float32)
    return total + jnp.dot(high, chosen, preferred_element_type=jnp.float32)


def own_counts(lengths, span):
    lane = lax.broadcasted_iota(jnp.int32, (1, 128), 1)
    count = jnp.where(lane % (2 * GROUPS) < GROUPS, lengths[0], lengths[1]) - span * FRAMES
    count = jnp.clip(count, 1, FRAMES).astype(jnp.float32)
    return 1.0 / (count * float(2 * COLS * SPANS * SHARE // GROUPS))


def own_square(value, inverse):
    axis = value.ndim - 1
    turned = pltpu.roll(value, 2 * GROUPS, axis)
    upper = lax.broadcasted_iota(jnp.int32, (1,) * axis + (128,), axis) >= 2 * GROUPS
    return jnp.where(upper, turned * (turned * inverse), 0.0)


def payload_kernel(features, conv, skip, lengths, copies, counts, planes, taps, skips, valid, rows, packed, few, done, left):
    moves = [
        pltpu.make_async_copy(source, target, done.at[index])
        for index, (source, target) in enumerate(
            ((features, planes), (conv, taps), (skip, skips), (lengths, valid))
        )
    ]
    for move in moves:
        move.start()
    for move in moves[1:]:
        move.wait()
    count, channels = taps.shape[0], planes.shape[-1]
    span = lax.axis_index(TM)
    pick = lax.broadcasted_iota(jnp.int32, (count, SPANS, OUT), 1) == span
    rows[...] = jnp.zeros_like(rows)
    rows[0:count, :] = jnp.sum(jnp.where(pick, taps[...].astype(jnp.float32), 0.0), axis=1)
    pick = lax.broadcasted_iota(jnp.int32, (SPANS, OUT), 0) == span
    rows[count : count + 1, :] = jnp.sum(
        jnp.where(pick, skips[...].astype(jnp.float32), 0.0), axis=0, keepdims=True
    )
    moves[0].wait()
    lines = []
    for video in range(VIDEOS):
        linear = jnp.zeros((1, channels), jnp.float32)
        square = jnp.zeros((1, channels), jnp.float32)
        for frame in range(FRAMES):
            block = planes[video * FRAMES + frame].astype(jnp.float32)
            shown = (span * FRAMES + frame < valid[video]).astype(jnp.float32)
            linear += jnp.sum(block, axis=0, keepdims=True) * shown
            square += jnp.sum(block * block, axis=0, keepdims=True) * shown
        lines += [(video, linear), (VIDEOS + video, square)]
    lines = jnp.concatenate([line for _, line in sorted(lines, key=lambda pair: pair[0])], axis=0)
    group = lax.broadcasted_iota(jnp.int32, (channels, 128), 0) // (channels // GROUPS)
    lane = lax.broadcasted_iota(jnp.int32, (channels, 128), 1)
    spots = exact_dot(lines, (lane % GROUPS == group).astype(jnp.bfloat16))
    line = lax.broadcasted_iota(jnp.int32, spots.shape, 0)
    lane = lax.broadcasted_iota(jnp.int32, spots.shape, 1)
    sums = jnp.sum(jnp.where(lane // GROUPS == line, spots, 0.0), axis=0, keepdims=True)
    sums = jnp.broadcast_to(sums, (8, 128))
    inverse = own_counts(valid, span)
    sums = sums - own_square(sums, inverse)
    counts[...] = jnp.concatenate(
        [jnp.full((1, 128), valid[video]).astype(jnp.float32) for video in range(VIDEOS)]
        + [inverse, jnp.zeros((5, 128), jnp.float32)],
        axis=0,
    )
    high = sums.astype(jnp.bfloat16).astype(jnp.float32)
    for line, value in enumerate((high, sums - high)):
        packed[line : line + 1, LINE * OUT : WIDTH] = value[0:1]
    for row in range(2 * LINE):
        at = row % LINE * OUT
        packed[row // LINE : row // LINE + 1, at : at + OUT] = rows[row : row + 1, :]
    value = packed[0:2, :].astype(jnp.bfloat16)
    some = few.shape[0]
    for index in range(some):
        few[index] = value
    moves = [
        pltpu.make_async_copy(few, copies.at[pl.ds(index * some, some)], left.at[index])
        for index in range(copies.shape[0] // some)
    ]
    for move in moves:
        move.start()
    for move in moves:
        move.wait()


def sums_kernel(counts, arrived, copies):
    value = arrived[:, 0:1, LINE * OUT : WIDTH].astype(jnp.float32)
    value = value + arrived[:, 1:2, LINE * OUT : WIDTH].astype(jnp.float32)
    value = value + own_square(value, counts[2:3, :].reshape(1, 1, 128))
    total = jnp.sum(value, axis=0, keepdims=True)
    copies[...] = jnp.broadcast_to(total, copies.shape)


def member_kernel(features, gain, bias, kept, sent, lanes):
    voxels, channels = features.shape[0] * COLS, features.shape[-1]
    column = lax.broadcasted_iota(jnp.int32, (channels, channels), 1)
    place = column % PART
    source = place % SHARE * SPANS + column // PART * 2 + place // SHARE
    match = lax.broadcasted_iota(jnp.int32, (channels, channels), 0) == source
    chosen = jnp.where(match, 1.0, 0.0).astype(jnp.bfloat16)
    even = lax.axis_index("core") == 0
    for row in range(2):
        block = features[:, row * COLS : (row + 1) * COLS].reshape(voxels, channels)
        flat = jnp.dot(block, chosen, preferred_element_type=jnp.float32).astype(jnp.bfloat16)
        flat = flat.reshape(VIDEOS, FRAMES, COLS, channels)
        mine, other = jnp.where(even, flat[0], flat[1]), jnp.where(even, flat[1], flat[0])
        at = slice(row * PART, (row + 1) * PART)
        for chip in range(CHIPS):
            kept[chip, :, :, at] = mine[..., chip * PART : (chip + 1) * PART]
            sent[chip, :, :, at] = other[..., chip * PART : (chip + 1) * PART]
    place = lax.broadcasted_iota(jnp.int32, (channels, PART), 1)
    source = place % SHARE * SPANS + lax.axis_index("x") * 2 + place // SHARE
    match = lax.broadcasted_iota(jnp.int32, (channels, PART), 0) == source
    pair = jnp.concatenate([gain[...], bias[...]], axis=0)
    lanes[...] = exact_dot(pair, jnp.where(match, 1.0, 0.0).astype(jnp.bfloat16))


def norm_kernel(
    totals, counts, lanes, signal, above, below, shifted, raw, factor, moments,
    *, cells, tiles, tap_bound, skip_bound
):
    chip, core = lax.axis_index("x"), lax.axis_index("core")
    tile = lax.axis_index(TILE)
    summed = [totals[0:1, :]]
    for span in range(1, SPANS):
        summed.append(summed[-1] + totals[span : span + 1, :])
    summed = jnp.concatenate(summed, axis=0)
    entry = lax.broadcasted_iota(jnp.int32, (128, 4 * PART), 0)
    lane = lax.broadcasted_iota(jnp.int32, (128, 4 * PART), 1)
    wanted = lane // PART * GROUPS + lane % SHARE // 2
    spread = exact_dot(summed, jnp.where(entry == wanted, 1.0, 0.0).astype(jnp.bfloat16))
    ends = ((lax.broadcasted_iota(jnp.int32, (SPANS, PART), 0) + 1) * FRAMES).astype(jnp.float32)
    for video in range(VIDEOS):
        seen = jnp.minimum(ends, counts[video : video + 1, :]) * cells
        square = spread[:, (VIDEOS + video) * PART : (VIDEOS + video + 1) * PART]
        centre = spread[:, video * PART : (video + 1) * PART] / seen
        inverse = lax.rsqrt(square / seen - centre * centre + EPS)
        moments[2 * video] = centre
        moments[2 * video + 1] = 0.5 * inverse * lanes[0:1, :]
        size = jnp.sqrt(square)
        ratio = size * inverse
        ratio = jnp.where(ratio < 1e30, ratio, 0.0)
        bound = tap_bound * (3.0 * jnp.max(ratio, keepdims=True) + 3.0)
        bound = bound + skip_bound * jnp.max(size, keepdims=True)
        bound = jnp.exp2(14.0 - jnp.floor(jnp.log2(bound)))
        factor[video : video + 1, :] = jnp.broadcast_to(bound, (1, OUT))
    half_bias = 0.5 * lanes[1:2, :]
    length = jnp.where(core == 0, counts[0:1, :], counts[1:2, :]).reshape(1, 1, PART)

    def normed(value, span):
        frame = lax.broadcasted_iota(jnp.int32, (FRAMES, 1, PART), 0) + span * FRAMES
        shown = frame.astype(jnp.float32) < length
        centre = moments[2 * core, pl.ds(span, 1)].reshape(1, 1, PART)
        scale = jnp.where(shown, moments[2 * core + 1, pl.ds(span, 1)].reshape(1, 1, PART), 0.0)
        offset = jnp.where(shown, half_bias.reshape(1, 1, PART), 0.0)
        value = (value.astype(jnp.float32) - centre) * scale + offset
        return value + value * jnp.tanh(value)

    for step in range(CHIPS):
        for other in range(2):
            span = lax.rem(chip - step + CHIPS, CHIPS) * 2 + lax.rem(core + other, 2)
            raw[pl.ds(span * FRAMES, FRAMES)] = signal[step, other]
            for row in range(ROWS):
                if row == 0:
                    value = jnp.where(tile == 0, signal[step, other, :, :, :PART], above[step, other])
                elif row == ROWS - 1:
                    value = jnp.where(
                        tile == tiles - 1, signal[step, other, :, :, PART:], below[step, other]
                    )
                else:
                    value = signal[step, other, :, :, (row - 1) * PART : row * PART]
                value = normed(value, span)
                left = jnp.concatenate([value[:, :1], value[:, :-1]], axis=1)
                right = jnp.concatenate([value[:, 1:], value[:, -1:]], axis=1)
                for side, part in enumerate((left, value, right)):
                    shifted[
                        side, pl.ds(2 + span * FRAMES, FRAMES), :, row * PART : (row + 1) * PART
                    ] = part.astype(jnp.bfloat16)
    for side in range(3):
        shifted[side, 0] = shifted[side, 2]
        shifted[side, 1] = shifted[side, 2]


def taps_kernel(shifted, raw, mine, theirs, out, weights):
    core = lax.axis_index("core")
    count = weights.shape[0]
    for tap in range(count):
        line, at = tap // LINE, tap % LINE * OUT
        for place, half in ((core, mine), (1 - core, theirs)):
            rows = pl.ds(pl.multiple_of(place * SHARE, SHARE), SHARE)
            weights[tap, rows] = half[line, :, at : at + OUT]
    length = SPANS * FRAMES
    for row in range(2):
        total = None
        for pair in range(count // 2):
            blocks = []
            for tap in (2 * pair, 2 * pair + 1):
                if tap < count - 1:
                    at = (row + tap // 3 % 3) * PART
                    block = shifted[tap % 3, tap // 9 : tap // 9 + length, :, at : at + PART]
                else:
                    block = raw[..., row * PART : (row + 1) * PART]
                blocks.append(block.reshape(-1, PART))
            term = jnp.dot(
                jnp.concatenate(blocks, axis=1),
                weights[2 * pair : 2 * pair + 2].reshape(2 * PART, OUT),
                preferred_element_type=jnp.float32,
            )
            total = term if total is None else total + term
        total = total.reshape(SPANS, FRAMES, COLS, OUT)
        out[:, :, row * COLS : (row + 1) * COLS, :] = total


def per_device(features, lengths, gain_in, bias_in, conv_in, skip_weight):
    videos, frames, row_count, col_count, wide_in = features.shape
    span, chip = lax.axis_index(TM), lax.axis_index("x")
    tiles, chips = lax.axis_size(TILE), lax.axis_size("x")
    taps = conv_in.shape[1]
    on_chip = pl.BlockSpec(memory_space=pltpu.VMEM)
    outside = pl.BlockSpec(memory_space=pl.ANY)
    params = pltpu.CompilerParams(vmem_limit_bytes=20 * 1024 * 1024)

    planes = features.reshape(videos * frames, row_count * col_count, wide_in)
    copies, counts = pl.pallas_call(
        payload_kernel,
        out_shape=(
            jax.ShapeDtypeStruct((tiles, 2, WIDTH), jnp.bfloat16),
            jax.ShapeDtypeStruct((8, 128), jnp.float32),
        ),
        in_specs=[outside] * 4,
        out_specs=(outside, on_chip),
        scratch_shapes=[
            pltpu.VMEM(planes.shape, jnp.bfloat16),
            pltpu.VMEM((taps, SPANS, OUT), jnp.bfloat16),
            pltpu.VMEM((SPANS, OUT), jnp.bfloat16),
            pltpu.SMEM((videos,), jnp.int32),
            pltpu.VMEM((32, OUT), jnp.float32),
            pltpu.VMEM((8, WIDTH), jnp.float32),
            pltpu.VMEM((8, 2, WIDTH), jnp.bfloat16),
            pltpu.SemaphoreType.DMA((4,)),
            pltpu.SemaphoreType.DMA((tiles // 8,)),
        ],
        compiler_params=params,
        name="payload",
    )(
        *[
            pltpu.with_memory_space_constraint(value, pltpu.HBM)
            for value in (planes, conv_in.transpose(1, 0, 2), skip_weight, lengths)
        ]
    )
    arrived = lax.all_to_all(copies, TILE, 0, 0, tiled=True)

    shape = (chips, frames, col_count, 2 * PART)
    kept, sent, lanes = pl.pallas_call(
        member_kernel,
        out_shape=(
            jax.ShapeDtypeStruct(shape, jnp.bfloat16),
            jax.ShapeDtypeStruct(shape, jnp.bfloat16),
            jax.ShapeDtypeStruct((2, PART), jnp.float32),
        ),
        in_specs=[on_chip] * 3,
        out_specs=(on_chip, on_chip, on_chip),
        compiler_params=params,
        name="member_shares",
    )(planes, gain_in.reshape(1, -1), bias_in.reshape(1, -1))
    swap = [(0, 1), (1, 0)]
    shares = jnp.stack([kept, lax.ppermute(sent, "core", swap)], axis=1)
    signal = []
    for step in range(chips):
        block = lax.dynamic_index_in_dim(shares, lax.rem(chip + step, chips), 0, False)
        if step:
            block = lax.ppermute(block, "x", [(i, (i + step) % chips) for i in range(chips)])
        signal.append(block)
    signal = jnp.stack(signal)
    upper, lower = signal[..., PART:], signal[..., :PART]
    above = lax.ppermute(upper, TILE, [(i, i + 1) for i in range(tiles - 1)])
    below = lax.ppermute(lower, TILE, [(i + 1, i) for i in range(tiles - 1)])

    held, upper, lower = lax.optimization_barrier((arrived, upper, lower))
    copies = pl.pallas_call(
        sums_kernel,
        out_shape=jax.ShapeDtypeStruct((SPANS, 1, 128), jnp.float32),
        in_specs=[on_chip, on_chip],
        out_specs=on_chip,
        compiler_params=params,
        name="sums",
    )(counts, pltpu.with_memory_space_constraint(held, pltpu.VMEM))
    totals = lax.all_to_all(copies, TM, 0, 0, tiled=True).reshape(SPANS, -1)
    mine = arrived.transpose(1, 0, 2)
    theirs = lax.ppermute(mine, "core", swap)

    shifted, raw, factor = pl.pallas_call(
        functools.partial(
            norm_kernel,
            cells=float(row_count * tiles * col_count * (wide_in // GROUPS)),
            tiles=tiles,
            tap_bound=float(taps * PART) * 0.0546875,
            skip_bound=float(PART) * 0.25,
        ),
        out_shape=(
            jax.ShapeDtypeStruct((3, SPANS * frames + 2, col_count, ROWS * PART), jnp.bfloat16),
            jax.ShapeDtypeStruct((SPANS * frames, col_count, 2 * PART), jnp.bfloat16),
            jax.ShapeDtypeStruct((videos, OUT), jnp.float32),
        ),
        in_specs=[on_chip] * 6,
        out_specs=(on_chip, on_chip, on_chip),
        scratch_shapes=[pltpu.VMEM((2 * videos + 1, SPANS, PART), jnp.float32)],
        compiler_params=params,
        cost_estimate=pl.CostEstimate(flops=1 << 34, bytes_accessed=1 << 26, transcendentals=1 << 24),
        name="norm",
    )(totals, counts, lanes, signal, above, below)
    total = pl.pallas_call(
        taps_kernel,
        out_shape=jax.ShapeDtypeStruct((SPANS, frames, row_count * col_count, OUT), jnp.float32),
        in_specs=[on_chip] * 4,
        out_specs=on_chip,
        scratch_shapes=[pltpu.VMEM((taps + 1, PART, OUT), jnp.bfloat16)],
        compiler_params=params,
        cost_estimate=pl.CostEstimate(
            flops=2 * 28 * 1024 * 128 * 256, bytes_accessed=6 << 20, transcendentals=0
        ),
        name="taps",
    )(shifted, raw, mine, theirs)

    scale = jnp.where(lax.axis_index("core") == 0, factor[0], factor[1])
    total = (total * scale).astype(jnp.float16)
    total = lax.all_to_all(total, TM, 0, 0, tiled=True).astype(jnp.float32)
    total = jnp.sum(total.reshape((chips, videos) + total.shape[1:]), axis=0)
    total = total / factor[:, None, None, :]
    total = total.reshape(videos, frames, row_count, col_count, OUT)
    stamps = span * frames + jnp.arange(frames, dtype=jnp.int32)
    present = stamps[None, :] < lengths[:, None]
    return jnp.where(present[:, :, None, None, None], total, 0.0).astype(jnp.bfloat16)


def solution(mesh):
    spans, tiles = mesh.devices.shape
    fine = Mesh(mesh.devices.reshape(spans // 2, 2, 8, tiles // 8), TM + TILE)
    placed = (
        P(None, TM, TILE, None, None),
        P(),
        P(),
        P(),
        P(TILE, None, None),
        P(TILE, None),
    )
    return jax.shard_map(
        per_device,
        mesh=fine,
        in_specs=placed,
        out_specs=P(None, TM, TILE, None, None),
        check_vma=False,
    )
```
